256 devices in a mesh: row: 8 (over y, core), col: 32 (over z, x).
Axes of the slice: x: 4, y: 4, z: 8, core: 2. Of those that a mesh axis runs over, the one named last changes fastest.
Arguments:
- uv_coords: float32 [65536, 2, 128], P(('row', 'col')), may hold values from -12 to 12
- visibilities: float32 [65536, 2, 128], P(('row', 'col')), may hold values from -6 to 6
- aterm_left: bfloat16 [65536, 2, 1024], P(('row', 'col')), may hold values from -4 to 4
- aterm_right: bfloat16 [65536, 2, 1024], P(('row', 'col')), may hold values from -4 to 4
- block_subgrid: int32 [256, 256], P(('row', 'col')), may hold values from 0 to 127, never falling along the last dimension, each value on 1 to 4 neighbouring positions
- subgrid_tile: int32 [32768, 1], P(('row', 'col')), may hold values from 0 to 255; in each aligned block of 128 rows (0 to 127, 128 to 255, ...) at most 2 rows name the same one
- block_row: int32 [32768], P(('row', 'col')), may hold values from 0 to 31
- block_col: int32 [32768], P(('row', 'col')), may hold values from 0 to 7
Outputs:
- sky: float32 [8192, 8192], P(('row', 'col'))
The draws below stay inside these ranges and needn't reach their ends.
Inputs may be any that keep to these rules, and one draw needn't show every extreme that they name: `subgrid_tile`: among one device's 128 subgrids no tile is named more than 2 times, a bound that some block reaches. `block_subgrid`: each row, for one device's blocks in order, never falls; every local subgrid gets 1 to 4 blocks, and some exactly 4.
All inputs are finite; a program needn't handle non-finite values.
Results may differ from the reference program's by a relative error of at most 0.0003.
Values sent between devices are 32-bit elements; how exact they have to be, the bound alone decides.
A program may use at most 128 MiB of HBM per device.

```python
import math
import jax
import jax.numpy as jnp
import numpy as np
from jax import lax

G = 8192
SUB = 32
VIS = 128
SUB_DEV = 128
BLK_DEV = 256
CAP = 2
BLOCKS = 65536
SUBGRIDS = 32768
N_ROW = 8
N_COL = 32


def plant(entries, own_key, smallest, high):
    shape = entries.shape
    spot = [jax.random.randint(jax.random.fold_in(own_key, axis), (), 0, shape[axis]) for axis in range(len(shape))]
    entries = entries.at[tuple(spot)].set(smallest)
    longest = shape.index(max(shape))
    spot[longest] = (spot[longest] + 1) % shape[longest]
    return entries.at[tuple(spot)].set(high)


def block_levels(own_key, extent, shards, least, largest):
    def one(dim, parts):
        heights = jax.random.uniform(jax.random.fold_in(jax.random.fold_in(own_key, 6), dim), (parts,), jnp.float32, least / len(shards), largest / len(shards))
        return jnp.repeat(jnp.exp(heights), extent[dim] // parts).reshape((-1,) + (1,) * (len(extent) - dim - 1))

    level = one(*shards[0])
    for cut in shards[1:]:
        level = level * one(*cut)
    return level


def length_profile(count, total, limit, slope):
    loads = [(1 << 20) // math.isqrt(rank ** slope) + 1 for rank in range(2, count + 1)]
    spare, counts = total - limit - (count - 1), [1] * (count - 1)
    while spare > 0:
        candidates = [i for i in range(count - 1) if counts[i] < limit]
        pool, budget = sum([loads[i] for i in candidates]), spare
        for i in candidates:
            extra = min(limit - counts[i], max(1, budget * loads[i] // pool), spare)
            counts[i] = counts[i] + extra
            spare = spare - extra
    return np.array([limit] + counts)


def uneven(rng, count, total, limit, slope):
    if count == 2:
        one = jax.random.randint(rng, (), max(1, total - limit), min(limit, total - 1) + 1)
        return jnp.stack([one, total - one])
    sizes = jnp.asarray(length_profile(count, total, limit, slope), jnp.int32)
    twos = (count - 1) // 2
    giver, taker = sizes[1:1 + 2 * twos:2], sizes[2:2 + 2 * twos:2]
    room = jnp.minimum(giver - 1, limit - taker)
    passed = jax.random.randint(jax.random.fold_in(rng, 1), (twos,), 0, 1 << 20) % (room + 1)
    sizes = sizes.at[1:1 + 2 * twos:2].set(giver - passed).at[2:2 + 2 * twos:2].set(taker + passed)
    return sizes[jax.random.permutation(jax.random.fold_in(rng, 2), count)]


def assign_block(stream_key, own, number, rows, count, top, bound, skew):
    order = jax.random.permutation(stream_key, count)
    heavy_load, common = load_shares(count, rows * top, bound, skew, True), load_shares(count, rows * top, bound, skew, False)
    places = jnp.arange(count)

    def named(tallies, rotation):
        used = int((tallies > 0).sum())
        fixed = max(1, used // 4)
        shifted = fixed + (places - fixed + rotation * (used - fixed)) % max(1, count - fixed)
        return jnp.zeros((count,), jnp.int32).at[order[jnp.where(places < fixed, places, shifted)]].set(jnp.asarray(tallies, jnp.int32))

    tallies = jnp.where(number % 4 == 0, named(heavy_load, number // 4), named(common, number - number // 4 - 1))
    mixed = jax.random.permutation(jax.random.fold_in(own, 3), count)
    source_of, receiver = mixed[0:count // 2 * 2:2], mixed[1:count // 2 * 2:2]
    margin = jnp.minimum(tallies[source_of] - 1, bound - tallies[receiver]) // 2
    margin = jnp.where((source_of == order[0]) | (receiver == order[0]) | (tallies[receiver] == 0), 0, jnp.maximum(margin, 0))
    shifted = jax.random.randint(jax.random.fold_in(own, 4), (count // 2,), 0, 1 << 20) % (margin + 1)
    tallies = tallies.at[source_of].add(-shifted).at[receiver].add(shifted)
    members = jnp.searchsorted(jnp.cumsum(tallies), jnp.arange(rows * top), side="right").astype(jnp.int32)
    table = members.reshape(top, rows).T
    table = table[jax.random.permutation(jax.random.fold_in(own, 1), rows)]
    rotation = jax.random.randint(jax.random.fold_in(own, 2), (rows, 1), 0, top)
    return jnp.take_along_axis(table, (jnp.arange(top)[None, :] + rotation) % top, axis=1)


def load_shares(amount, total, most, slope, full):
    weights = [(1 << 20) // math.isqrt(standing ** slope) + 1 for standing in range(1, amount + 1)]
    largest = most if full else min(most, max(-(-total // amount), total * weights[0] // sum(weights)))
    least = 1 if total - largest >= amount - 1 else 0
    counts, spare = [largest] + [least] * (amount - 1), total - largest - least * (amount - 1)
    while spare > 0:
        movable = [i for i in range(1, amount) if counts[i] < largest] or [i for i in range(1, amount) if counts[i] < most]
        whole, remaining = sum([weights[i] for i in movable]), spare
        for i in movable:
            more = min(most - counts[i], max(1, remaining * weights[i] // whole), spare)
            counts[i] = counts[i] + more
            spare = spare - more
    return np.array(counts)


def noise(own_key, dims, scale, most, cuts=(), kind=jnp.bfloat16):
    level = block_levels(own_key, dims, cuts, -0.22, 0.18) if cuts else 1.0
    drawn = jax.random.normal(own_key, dims, jnp.float32) * scale * level
    return jnp.minimum(jnp.maximum(drawn, -most), most).astype(kind)


def setup_inputs(seed: int = 0) -> dict:
    arg_keys = jax.random.split(jax.random.key(seed), 9)
    uv_coords = jnp.clip(jax.random.uniform(arg_keys[0], (BLOCKS, 2, VIS), jnp.float32, -12.0, 12.0) * block_levels(arg_keys[0], (BLOCKS, 2, VIS), ((0, 256),), -0.4, 0.0), -12.0, 12.0)
    visibilities = noise(arg_keys[1], (BLOCKS, 2, VIS), 1.0, 6.0, ((0, 256),), jnp.float32)
    aterm_left = noise(arg_keys[2], (BLOCKS, 2, SUB * SUB), 0.7, 4.0, ((0, 256),))
    aterm_right = noise(arg_keys[3], (BLOCKS, 2, SUB * SUB), 0.7, 4.0, ((0, 256),))
    block_subgrid = jax.vmap(lambda own: jnp.searchsorted(jnp.cumsum(uneven(own, SUB_DEV, BLK_DEV, 4, 0)), jnp.arange(BLK_DEV), side="right"))(jax.random.split(arg_keys[4], (N_ROW * N_COL))).reshape((N_ROW * N_COL, BLK_DEV)).astype(jnp.int32)
    subgrid_tile_keys = jax.random.split(jax.random.fold_in(arg_keys[5], 1), SUBGRIDS // SUB_DEV)
    subgrid_tile_turns = jax.random.permutation(jax.random.fold_in(arg_keys[5], 3), SUBGRIDS // SUB_DEV)
    subgrid_tile = jax.vmap(lambda own, number: assign_block(jax.random.fold_in(arg_keys[5], 2), own, number, SUB_DEV, N_ROW * N_COL, 1, CAP, 2))(subgrid_tile_keys, subgrid_tile_turns).reshape((SUBGRIDS, 1))
    block_row = plant(jax.random.randint(arg_keys[6], (SUBGRIDS,), 0, G // N_ROW // SUB), jax.random.fold_in(arg_keys[6], 1), 0, (G // N_ROW // SUB) - 1).astype(jnp.int32)
    block_col = plant(jax.random.randint(arg_keys[7], (SUBGRIDS,), 0, G // N_COL // SUB), jax.random.fold_in(arg_keys[7], 1), 0, (G // N_COL // SUB) - 1).astype(jnp.int32)
    return {"uv_coords": uv_coords, "visibilities": visibilities, "aterm_left": aterm_left, "aterm_right": aterm_right, "block_subgrid": block_subgrid, "subgrid_tile": subgrid_tile, "block_row": block_row, "block_col": block_col}


exact_prec = lax.Precision.HIGHEST


def phasor_image(coords, visib, left_term, right_term):
    centred = jnp.arange(SUB).astype(jnp.float32) - SUB / 2
    step_angle = 2 * math.pi / SUB
    theta_l = step_angle * coords[:, 0, :, None] * centred
    theta_m = step_angle * coords[:, 1, :, None] * centred
    vis_re = visib[:, 0, :, None]
    vis_im = visib[:, 1, :, None]
    cos_l = jnp.cos(theta_l)
    sin_l = jnp.sin(theta_l)
    cos_m = jnp.cos(theta_m)
    sin_m = jnp.sin(theta_m)
    wave_re = vis_re * cos_l - vis_im * sin_l
    wave_im = vis_re * sin_l + vis_im * cos_l
    pattern = 'bkl,bkm->blm'
    image_re = jnp.einsum(pattern, wave_re, cos_m, precision=exact_prec) - jnp.einsum(pattern, wave_im, sin_m, precision=exact_prec)
    image_im = jnp.einsum(pattern, wave_re, sin_m, precision=exact_prec) + jnp.einsum(pattern, wave_im, cos_m, precision=exact_prec)
    number = image_re.shape[0]
    image_re = image_re.reshape(number, SUB * SUB)
    image_im = image_im.reshape(number, SUB * SUB)
    left_beam = left_term.astype(jnp.float32)
    right_beam = right_term.astype(jnp.float32)
    beam_re = left_beam[:, 0] * right_beam[:, 0] + left_beam[:, 1] * right_beam[:, 1]
    beam_im = left_beam[:, 1] * right_beam[:, 0] - left_beam[:, 0] * right_beam[:, 1]
    norm_scale = coords.shape[2] ** -0.5
    contrib_re = (beam_re * image_re - beam_im * image_im) * norm_scale
    contrib_im = (beam_re * image_im + beam_im * image_re) * norm_scale
    return jnp.concatenate([contrib_re, contrib_im], axis=1)


def taper_table():
    position = jnp.arange(SUB).astype(jnp.float32)
    window = jnp.sin(math.pi * (position + 0.5) / SUB)
    square = (window[:, None] * window[None, :]).reshape(SUB * SUB)
    return jnp.concatenate([square, square])


def subgrid_dft(images):
    number = images.shape[0]
    stacked = images.reshape(number, 2, SUB, SUB)
    position = jnp.arange(SUB, dtype=jnp.int32)
    product = (position[:, None] * position[None, :]) % SUB
    angles = (-2 * math.pi / SUB) * product.astype(jnp.float32)
    fwd_re = jnp.cos(angles)
    fwd_im = jnp.sin(angles)
    first = 'nlm,bm->nlb'
    mid_re = jnp.einsum(first, stacked[:, 0], fwd_re, precision=exact_prec) - jnp.einsum(first, stacked[:, 1], fwd_im, precision=exact_prec)
    mid_im = jnp.einsum(first, stacked[:, 0], fwd_im, precision=exact_prec) + jnp.einsum(first, stacked[:, 1], fwd_re, precision=exact_prec)
    second = 'al,nlb->nab'
    out_re = jnp.einsum(second, fwd_re, mid_re, precision=exact_prec) - jnp.einsum(second, fwd_im, mid_im, precision=exact_prec)
    out_im = jnp.einsum(second, fwd_im, mid_re, precision=exact_prec) + jnp.einsum(second, fwd_re, mid_im, precision=exact_prec)
    result = jnp.stack([out_re, out_im], axis=1) / SUB
    return result.reshape(number, 2 * SUB * SUB)


def reference(uv_coords, visibilities, aterm_left, aterm_right, block_subgrid, subgrid_tile, block_row, block_col):
    devices = N_ROW * N_COL

    def per_device(pieces):
        coords, visib, left_term, right_term, index_row = pieces
        contrib = phasor_image(coords, visib, left_term, right_term)
        return jax.ops.segment_sum(contrib, index_row, num_segments=SUB_DEV)

    images = lax.map(per_device, (
        uv_coords.reshape(devices, BLK_DEV, 2, VIS),
        visibilities.reshape(devices, BLK_DEV, 2, VIS),
        aterm_left.reshape(devices, BLK_DEV, 2, SUB * SUB),
        aterm_right.reshape(devices, BLK_DEV, 2, SUB * SUB),
        block_subgrid))
    images = images.reshape(devices * SUB_DEV, 2 * SUB * SUB) * taper_table()
    spectra = subgrid_dft(images).reshape(devices * SUB_DEV, 2, SUB, SUB)
    tile_index = subgrid_tile[:, 0]
    u_start = (tile_index // N_COL) * (G // N_ROW) + block_row * SUB
    v_start = (tile_index % N_COL) * (G // N_COL) + block_col * SUB
    offsets = jnp.arange(SUB, dtype=jnp.int32)
    row_index = jnp.broadcast_to(u_start[:, None, None] + offsets[None, :, None], (devices * SUB_DEV, SUB, SUB))
    col_index = jnp.broadcast_to(v_start[:, None, None] + offsets[None, None, :], (devices * SUB_DEV, SUB, SUB))
    grid_re = jnp.zeros((G, G), jnp.float32).at[row_index, col_index].add(spectra[:, 0])
    grid_im = jnp.zeros((G, G), jnp.float32).at[row_index, col_index].add(spectra[:, 1])
    image_field = jnp.fft.ifft2(lax.complex(grid_re, grid_im))
    return (jnp.real(image_field) * G).astype(jnp.float32)
```

```python
import math
from functools import partial

import jax
import jax.numpy as jnp
import ml_dtypes
import numpy as np
from jax import lax
from jax.experimental import pallas as pl
from jax.experimental.pallas import tpu as pltpu
from jax.sharding import PartitionSpec as P

G = 8192
SUB = 32
PAIRS = 16
CLASSES = 16
STEP = 32
F32 = jnp.float32
BF16 = jnp.bfloat16
MB = 1 << 20


def halves(table):
    high = np.asarray(table, np.float32).astype(ml_dtypes.bfloat16)
    low = (np.asarray(table, np.float64) - high.astype(np.float64)).astype(ml_dtypes.bfloat16)
    return high, low


def split(x):
    high = x.astype(BF16)
    return high, (x - high.astype(F32)).astype(BF16)


def dot(a, b):
    return lax.dot_general(a, b, (((1,), (0,)), ((), ())), preferred_element_type=F32)


def dot_nt(a, b):
    return lax.dot_general(a, b, (((1,), (1,)), ((), ())), preferred_element_type=F32)


def dot3(ah, al, bh, bl):
    return dot(ah, bh) + (dot(al, bh) + dot(ah, bl))


def taper(p):
    return np.sin(math.pi * (p + 0.5) / SUB)


def class_column(j, c2):
    return j if c2 == 0 else (16 if j == 0 else 32 - j)


def subgrid_tables(visible):
    m = np.arange(32)
    first = np.zeros((2, 4, 32, 2, 4, 2, 8, 2))
    second = np.zeros((8, 4, 2, 8, 2, 8, 2, 2, 32))
    for cg in range(2):
        for j8 in range(8):
            for c2 in range(2):
                phi = 2 * math.pi * ((class_column(cg * 8 + j8, c2) * m) % 32) / 32
                for l4 in range(4):
                    first[0, l4, :, cg, l4, 0, j8, c2] = np.cos(phi) * taper(m)
                    first[1, l4, :, cg, l4, 0, j8, c2] = np.sin(phi) * taper(m)
                    first[0, l4, :, cg, l4, 1, j8, c2] = -np.sin(phi) * taper(m)
                    first[1, l4, :, cg, l4, 1, j8, c2] = np.cos(phi) * taper(m)
    a = np.arange(32)
    scale = visible ** (-0.5) / SUB / G
    for l8 in range(8):
        for l4 in range(4):
            l = 4 * l8 + l4
            phi = 2 * math.pi * ((a * l) % 32) / 32
            weight = taper(l) * scale
            for j8 in range(8):
                for c2 in range(2):
                    second[l8, l4, 0, j8, c2, j8, c2, 0] = np.cos(phi) * weight
                    second[l8, l4, 1, j8, c2, j8, c2, 0] = np.sin(phi) * weight
                    second[l8, l4, 0, j8, c2, j8, c2, 1] = -np.sin(phi) * weight
                    second[l8, l4, 1, j8, c2, j8, c2, 1] = np.cos(phi) * weight
    return first.reshape(256, 256), second.reshape(1024, 1024)


def down_tables():
    r = np.arange(256)[:, None, None, None]
    nt, q4, lo = np.meshgrid(np.arange(2), np.arange(4), np.arange(32), indexing="ij")
    l1 = ((nt * 4 + q4) * 32 + lo)[None]
    phi = 2 * math.pi * ((r * l1) % 256) / 256
    c, s = np.cos(phi), np.sin(phi)
    w = np.zeros((2, 256, 2, 2, 4, 2, 32))
    w[0, :, :, 0, :, 0], w[1, :, :, 0, :, 0] = c, -s
    w[0, :, :, 0, :, 1], w[1, :, :, 0, :, 1] = s, c
    w[0, :, :, 1, :, 0], w[1, :, :, 1, :, 0] = -s, -c
    w[0, :, :, 1, :, 1], w[1, :, :, 1, :, 1] = c, -s
    a = np.arange(32)[None, :, None, None]
    l1 = ((nt * 4 + q4) * 32 + lo)[:, None]
    psi = 2 * math.pi * a * l1 / G
    c, s = np.cos(psi), np.sin(psi)
    t = np.zeros((2, 4, 2, 2, 32, 4, 2, 32))
    for which in range(2):
        t[which, 0, :, 0, :, :, 0], t[which, 1, :, 0, :, :, 0] = c, s
        t[which, 2, :, 0, :, :, 0], t[which, 3, :, 0, :, :, 0] = -s, c
    t[0, 0, :, 0, :, :, 1], t[0, 1, :, 0, :, :, 1] = c, s
    t[0, 2, :, 0, :, :, 1], t[0, 3, :, 0, :, :, 1] = -s, c
    t[0, 0, :, 1, :, :, 0], t[0, 1, :, 1, :, :, 0] = c, s
    t[0, 2, :, 1, :, :, 0], t[0, 3, :, 1, :, :, 0] = s, -c
    t[0, 0, :, 1, :, :, 1], t[0, 1, :, 1, :, :, 1] = -c, -s
    t[0, 2, :, 1, :, :, 1], t[0, 3, :, 1, :, :, 1] = -s, c
    t[1, 0, :, 1, :, :, 1], t[1, 1, :, 1, :, :, 1] = -s, c
    t[1, 2, :, 1, :, :, 1], t[1, 3, :, 1, :, :, 1] = c, s
    phi = 2 * math.pi * ((np.arange(32)[:, None] * np.arange(32)[None, :]) % 32) / 32
    e = np.zeros((32, 2, 2, 32))
    e[:, 0, 0], e[:, 0, 1] = np.cos(phi), np.cos(phi)
    e[:, 1, 0], e[:, 1, 1] = np.sin(phi), -np.sin(phi)
    return w.reshape(512, 1024), t.reshape(16, 64, 256).astype(np.float32), e.reshape(32, 128)


def across_tables():
    p, bc = np.meshgrid(np.arange(16), np.arange(8), indexing="ij")
    m1 = np.arange(256)[None, None, :]
    w = np.zeros((2, 2, 128, 2, 256))
    for s in range(2):
        v1 = (8 * p + bc if s == 0 else 8 * (31 - p) + bc).reshape(128, 1)
        phi = 2 * math.pi * ((v1 * np.arange(256)[None, :]) % 256) / 256
        w[s, 0, :, 0], w[s, 1, :, 0] = np.cos(phi), -np.sin(phi)
        w[s, 0, :, 1], w[s, 1, :, 1] = np.sin(phi), np.cos(phi)
    zero = w[0].copy()
    zero[1, 0, 0] = 1 - 2 * (np.arange(256) % 2)
    zero[1, 0, 1] = 0
    psi = 2 * math.pi * np.arange(17)[:, None] * np.arange(256)[None, :] / G
    twist = np.concatenate([np.cos(psi), np.sin(psi)], axis=1).astype(np.float32)
    return w.reshape(512, 512), zero.reshape(256, 512), twist


def turn(t):
    quarter = jnp.round(t * 4.0)
    x = (t - quarter * 0.25) * (2 * math.pi)
    y = x * x
    sine = x * (1 + y * (-1 / 6 + y * (1 / 120 + y * (-1 / 5040 + y * (1 / 362880)))))
    cosine = 1 + y * (-0.5 + y * (1 / 24 + y * (-1 / 720 + y * (1 / 40320))))
    q = quarter.astype(jnp.int32)
    odd = (q & 1) != 0
    c = jnp.where(odd, sine, cosine)
    s = jnp.where(odd, cosine, sine)
    c = jnp.where(((q + 1) & 2) != 0, -c, c)
    s = jnp.where((q & 2) != 0, -s, s)
    return c, s


def times(x, y):
    return x[0] * y[0] - x[1] * y[1], x[0] * y[1] + x[1] * y[0]


def conj(x):
    return x[0], -x[1]


def grid_kernel(
    uv_ref, vis_ref, beam_ref, seg_ref, slot_ref, d1h, d1l, d2h, d2l,
    out_ref,
    base_l, base_m, fact_l, fact_m, image, ch, cl, ah, al,
):
    step = pl.program_id(0)
    n = STEP
    zu = turn(uv_ref[:, 0, :] * (1 / 32))
    zv = turn(uv_ref[:, 1, :] * (1 / 32))
    vis = (vis_ref[:, 0, :], vis_ref[:, 1, :])
    u2 = times(zu, zu)
    u3 = times(u2, zu)
    u4 = times(u2, u2)
    u8 = times(u4, u4)
    u12 = times(u8, u4)
    u16 = times(u8, u8)
    for i, f in enumerate((conj(u16), conj(u12), conj(u8), conj(u4), None, u4, u8, u12)):
        b = vis if f is None else times(vis, f)
        base_l[0, pl.ds(i, n, stride=8), :] = b[0]
        base_l[1, pl.ds(i, n, stride=8), :] = b[1]
    for i, f in enumerate((zu, u2, u3)):
        fact_l[2 * i] = f[0]
        fact_l[2 * i + 1] = f[1]
    v2 = times(zv, zv)
    v3 = times(v2, zv)
    v4 = times(v2, v2)
    v5 = times(v4, zv)
    v6 = times(v4, v2)
    v7 = times(v4, v3)
    v8 = times(v4, v4)
    v16 = times(v8, v8)
    one = (jnp.ones_like(zv[0]), jnp.zeros_like(zv[0]))
    for i, f in enumerate((one, zv, v2, v3, v4, v5, v6, v7)):
        base_m[0, pl.ds(i, n, stride=8), :] = f[0]
        base_m[1, pl.ds(i, n, stride=8), :] = f[1]
    for i, f in enumerate((conj(v16), conj(v8), v8)):
        fact_m[2 * i] = f[0]
        fact_m[2 * i + 1] = f[1]

    def one_block(b, _):
        rows = pl.ds(pl.multiple_of(b * 8, 8), 8)
        line = pl.ds(b, 1)
        bl = (base_l[0, rows, :], base_l[1, rows, :])
        bm = (base_m[0, rows, :], base_m[1, rows, :])
        left, right = [], []
        for t in range(4):
            w = bl if t == 0 else times(bl, (fact_l[2 * t - 2, line, :], fact_l[2 * t - 1, line, :]))
            left += [w[0], w[1]]
            right += [-w[1], w[0]]
        lh, ll = split(jnp.concatenate(
            [jnp.concatenate(left, axis=0), jnp.concatenate(right, axis=0)], axis=1))
        cosine, sine = [], []
        for t in range(4):
            i = {0: 0, 1: 1, 3: 2}.get(t)
            w = bm if i is None else times(bm, (fact_m[2 * i, line, :], fact_m[2 * i + 1, line, :]))
            cosine.append(w[0])
            sine.append(w[1])
        mh, ml = split(jnp.concatenate(
            [jnp.concatenate(cosine, axis=0), jnp.concatenate(sine, axis=0)], axis=1))
        o = dot_nt(lh, mh) + (dot_nt(ll, mh) + dot_nt(lh, ml))
        image[0, rows, :] = jnp.concatenate([o[16 * t:16 * t + 8] for t in range(4)], axis=1)
        image[1, rows, :] = jnp.concatenate([o[16 * t + 8:16 * t + 16] for t in range(4)], axis=1)
        return 0

    lax.fori_loop(0, n, one_block, 0, unroll=4)

    here = pl.ds(pl.multiple_of(step * n, n), n)
    for l8 in range(8):
        im = (image[0, pl.ds(l8, n, stride=8), :], image[1, pl.ds(l8, n, stride=8), :])
        bm = (beam_ref[0, :, l8 * 128:(l8 + 1) * 128], beam_ref[1, :, l8 * 128:(l8 + 1) * 128])
        c = times(bm, im)
        for ri in range(2):
            h, l = split(c[ri])
            ch[here, (2 * l8 + ri) * 128:(2 * l8 + ri + 1) * 128] = h
            cl[here, (2 * l8 + ri) * 128:(2 * l8 + ri + 1) * 128] = l

    @pl.when(step == pl.num_programs(0) - 1)
    def _():
        subs = slot_ref.shape[1]
        blocks = seg_ref.shape[1]
        pick = (seg_ref[...] == lax.broadcasted_iota(jnp.int32, (subs, blocks), 0)).astype(F32).astype(BF16)
        for l8 in range(8):
            lanes = slice(l8 * 256, (l8 + 1) * 256)
            ih, il = split(dot(pick, ch[:, lanes]) + dot(pick, cl[:, lanes]))
            a = dot3(ih, il, d1h[...], d1l[...])
            for cg in range(2):
                h, l = split(a[:, cg * 128:(cg + 1) * 128])
                ah[cg * subs:(cg + 1) * subs, l8 * 128:(l8 + 1) * 128] = h
                al[cg * subs:(cg + 1) * subs, l8 * 128:(l8 + 1) * 128] = l
        slots = 2 * 256
        place = (slot_ref[...] == lax.broadcasted_iota(jnp.int32, (slots, subs), 0)).astype(F32).astype(BF16)
        place = jnp.concatenate([place, place], axis=1)
        for tile in range(4):
            lanes = slice(tile * 256, (tile + 1) * 256)
            spec = dot3(ah[...], al[...], d2h[:, lanes], d2l[:, lanes])
            for cg in range(2):
                h, l = split(spec[cg * subs:(cg + 1) * subs])
                o = dot(place, jnp.concatenate([h, l], axis=0))
                j = cg * 8 + tile * 2
                out_ref[j * slots:(j + 1) * slots, :] = o[:, :128]
                out_ref[(j + 1) * slots:(j + 2) * slots, :] = o[:, 128:]


def make_outbox(uv, vis, beam, seg, slot, tables):
    blocks, _, visible = uv.shape
    subs = slot.shape[1]
    (d1h, d1l), (d2h, d2l) = [halves(t) for t in tables]
    whole = lambda shape: pl.BlockSpec(shape, lambda i: (0,) * len(shape))
    return pl.pallas_call(
        grid_kernel,
        grid=(blocks // STEP,),
        in_specs=[
            pl.BlockSpec((STEP, 2, visible), lambda i: (i, 0, 0)),
            pl.BlockSpec((STEP, 2, visible), lambda i: (i, 0, 0)),
            pl.BlockSpec((2, STEP, SUB * SUB), lambda i: (0, i, 0)),
            whole((1, blocks)), whole((1, subs)),
            whole((256, 256)), whole((256, 256)), whole((1024, 1024)), whole((1024, 1024)),
        ],
        out_specs=whole((8192, 128)),
        out_shape=jax.ShapeDtypeStruct((8192, 128), F32),
        scratch_shapes=[
            pltpu.VMEM((2, STEP * 8, 128), F32),
            pltpu.VMEM((2, STEP * 8, 128), F32),
            pltpu.VMEM((6, STEP, 128), F32),
            pltpu.VMEM((6, STEP, 128), F32),
            pltpu.VMEM((2, STEP * 8, 128), F32),
            pltpu.VMEM((blocks, 2048), BF16),
            pltpu.VMEM((blocks, 2048), BF16),
            pltpu.VMEM((2 * subs, 1024), BF16),
            pltpu.VMEM((2 * subs, 1024), BF16),
        ],
        compiler_params=pltpu.CompilerParams(vmem_limit_bytes=48 * MB),
        name="gridding",
    )(uv, vis, beam, seg, slot, d1h, d1l, d2h, d2l)


def place_kernel(data_ref, label_ref, out_ref, grid_ref):
    pos = lax.broadcasted_iota(jnp.int32, (256, 256), 0).astype(F32)

    def one(i, _):
        s, r = i // 8, i % 8
        hot, data = [], []
        for k in range(2):
            slot = i * 2 + k
            label = label_ref[pl.ds(slot, 1), :]
            hot.append((label == pos).astype(F32).astype(BF16))
            data.append(data_ref[pl.ds(slot, 256, stride=32), :])
        h, l = split(jnp.concatenate(data, axis=0))
        g = dot(jnp.concatenate(hot, axis=1), jnp.concatenate([h, l], axis=1))
        g = g[:, :128] + g[:, 128:]
        for bc in range(8):
            grid_ref[s * 8 + bc, pl.ds(pl.multiple_of(r * 32, 32), 32), :] = g[bc * 32:(bc + 1) * 32]
        return 0

    lax.fori_loop(0, 16, one, 0)

    def flip(i, _):
        out_ref[i] = grid_ref[i].T
        return 0

    lax.fori_loop(0, 16, flip, 0)


def place(data, labels):
    return pl.pallas_call(
        place_kernel,
        out_shape=jax.ShapeDtypeStruct((16, 128, 256), F32),
        scratch_shapes=[pltpu.VMEM((16, 256, 128), F32)],
        compiler_params=pltpu.CompilerParams(vmem_limit_bytes=32 * MB),
        name="placing",
    )(data, labels)


def down_kernel(flag_ref, x_ref, extra_ref, wh, wl, t_ref, eh, el, out_ref, lh, ll):
    zero_class = flag_ref[0]
    special = flag_ref[1]
    for bc in range(8):
        for s in range(2):
            plain = (s * 8 + bc) * 128
            other = ((1 - s) * 8 + 7 - bc) * 128 + 64
            if s == 0:
                own = x_ref[plain:plain + 64, :]
                if bc == 0:
                    mirror = jnp.where(zero_class == 1, extra_ref[...], x_ref[other:other + 64, :])
                else:
                    off = jnp.where(zero_class == 1, (16 - bc) * 128, other)
                    mirror = x_ref[pl.ds(pl.multiple_of(off, 64), 64), :]
            else:
                off = jnp.where(zero_class == 1, bc * 128 + 64, plain)
                own = x_ref[pl.ds(pl.multiple_of(off, 64), 64), :]
                off = jnp.where(zero_class == 1, (15 - bc) * 128 + 64, other)
                mirror = x_ref[pl.ds(pl.multiple_of(off, 64), 64), :]
            for c2, v in enumerate((own, mirror)):
                h, l = split(v)
                row = (bc * 2 + s) * 64 + c2 * 32
                for ri in range(2):
                    lh[row:row + 32, ri * 256:(ri + 1) * 256] = h[ri * 32:(ri + 1) * 32]
                    ll[row:row + 32, ri * 256:(ri + 1) * 256] = l[ri * 32:(ri + 1) * 32]
    e2 = jnp.concatenate([eh[...], eh[...]], axis=1)
    low = lax.broadcasted_iota(jnp.int32, (32, 128), 1) < 64

    def one(i, _):
        rows = pl.ds(pl.multiple_of(i * 256, 256), 256)
        for nt in range(2):
            cols = slice(nt * 512, (nt + 1) * 512)
            y = dot3(lh[rows, :], ll[rows, :], wh[:, cols], wl[:, cols])
            for k in range(2):
                bc = i * 2 + k
                parts = []
                for s in range(2):
                    r = (k * 2 + s) * 64
                    ya, yb = y[r:r + 64, :256], y[r:r + 64, 256:]
                    which = 0
                    if s == 0 and k == 0:
                        which = jnp.where(i == 0, special, 0)
                    tab = lambda n: t_ref[which * 8 + n * 2 + nt]
                    parts.append(jnp.concatenate(
                        [ya * tab(0) + yb * tab(1), ya * tab(2) + yb * tab(3)], axis=0))
                th, tl = split(jnp.concatenate(parts, axis=1))
                o = dot(e2, jnp.concatenate([th, tl], axis=0)) + dot(el[...], th)
                for g in range(2):
                    o0 = o[:, g * 128:(g + 1) * 128]
                    o1 = o[:, 256 + g * 128:256 + (g + 1) * 128]
                    q = nt * 4 + g * 2
                    out_ref[pl.ds(q * 8 + bc, 32, stride=64), :] = jnp.where(low, o0, pltpu.roll(o1, 64, 1))
                    out_ref[pl.ds((q + 1) * 8 + bc, 32, stride=64), :] = jnp.where(low, pltpu.roll(o0, 64, 1), o1)
        return 0

    lax.fori_loop(0, 4, one, 0)


def down(flags, x, extra):
    w, t, e = down_tables()
    wh, wl = halves(w)
    eh, el = halves(e)
    vmem = pl.BlockSpec(memory_space=pltpu.VMEM)
    return pl.pallas_call(
        down_kernel,
        in_specs=[pl.BlockSpec(memory_space=pltpu.SMEM)] + [vmem] * 7,
        out_shape=jax.ShapeDtypeStruct((2048, 128), F32),
        scratch_shapes=[pltpu.VMEM((1024, 512), BF16), pltpu.VMEM((1024, 512), BF16)],
        compiler_params=pltpu.CompilerParams(vmem_limit_bytes=40 * MB),
        name="down",
    )(flags, x, extra, wh, wl, t, eh, el)


def across_kernel(k_ref, wh, wl, zh, zl, twist, out_ref, lh, ll, y_ref):
    for j in range(16):
        a = k_ref[j * 128:(j + 1) * 128, :].T
        h, l = split(a)
        for i in range(4):
            lh[j * 32:(j + 1) * 32, i * 128:(i + 1) * 128] = h[i * 32:(i + 1) * 32]
            ll[j * 32:(j + 1) * 32, i * 128:(i + 1) * 128] = l[i * 32:(i + 1) * 32]
    y_ref[0:32] = dot3(lh[0:32, :256], ll[0:32, :256], zh[...], zl[...])
    y_ref[512:544] = dot3(lh[0:32, 256:], ll[0:32, 256:], wh[:256, :], wl[:256, :])
    y_ref[32:512] = dot3(lh[32:512, :], ll[32:512, :], wh[...], wl[...])

    cos = [math.cos(2 * math.pi * i / 32) for i in range(32)]
    sin = [math.sin(2 * math.pi * i / 32) for i in range(32)]

    def combine(terms):
        total = None
        for f, x in terms:
            if abs(f) < 1e-12:
                continue
            v = x if f == 1.0 else -x if f == -1.0 else x * f
            total = v if total is None else total + v
        return total

    def rows(i, _):
        at = pl.multiple_of(i * 8, 8)
        for half in range(2):
            lane = slice(half * 128, (half + 1) * 128)
            tre, tim = [], []
            for v in range(17):
                yre = y_ref[pl.ds(v * 32 + at, 8), lane]
                yim = y_ref[pl.ds(v * 32 + at, 8), 256 + half * 128:256 + (half + 1) * 128]
                c = twist[v:v + 1, lane]
                s = twist[v:v + 1, 256 + half * 128:256 + (half + 1) * 128]
                tre.append(yre * c - yim * s)
                tim.append(yre * s + yim * c)
            for m2 in range(9):
                e0 = combine([(cos[v * m2 % 32], tre[v]) for v in range(0, 17, 2)])
                e1 = combine([(cos[v * m2 % 32], tre[v]) for v in range(1, 17, 2)])
                o0 = combine([(sin[v * m2 % 32], tim[v]) for v in range(0, 17, 2)])
                o1 = combine([(sin[v * m2 % 32], tim[v]) for v in range(1, 17, 2)])
                zero = jnp.zeros((8, 128), F32)
                e0, e1, o0, o1 = [zero if x is None else x for x in (e0, e1, o0, o1)]
                puts = {m2: (e0 + e1) - (o0 + o1), (32 - m2) % 32: (e0 + e1) + (o0 + o1)}
                puts[16 - m2] = (e0 - e1) + (o0 - o1)
                puts[16 + m2] = (e0 - e1) - (o0 - o1)
                for m, v in puts.items():
                    out_ref[pl.ds(at, 8), m * 256 + half * 128:m * 256 + (half + 1) * 128] = v
        return 0

    lax.fori_loop(0, 4, rows, 0)


def across(k):
    w, zero, twist = across_tables()
    wh, wl = halves(w)
    zh, zl = halves(zero)
    return pl.pallas_call(
        across_kernel,
        out_shape=jax.ShapeDtypeStruct((32, G), F32),
        scratch_shapes=[
            pltpu.VMEM((512, 512), BF16), pltpu.VMEM((512, 512), BF16), pltpu.VMEM((544, 512), F32),
        ],
        compiler_params=pltpu.CompilerParams(vmem_limit_bytes=32 * MB),
        name="across",
    )(k, wh, wl, zh, zl, twist)


def body(uv, vis, left, right, block_subgrid, subgrid_tile, block_row, block_col):
    axes = ("row", "col")
    devices = lax.axis_size("row") * lax.axis_size("col")
    me = lax.axis_index("row") * lax.axis_size("col") + lax.axis_index("col")
    subs = subgrid_tile.shape[0]
    visible = uv.shape[2]

    tile = subgrid_tile[:, 0]
    ids = jnp.arange(subs, dtype=jnp.int32)
    earlier = (tile[None, :] == tile[:, None]) & (ids[None, :] < ids[:, None])
    rank = jnp.sum(earlier.astype(jnp.int32), axis=1)
    band = tile % 32
    side = (band >= 16).astype(jnp.int32)
    pair = jnp.where(side == 1, 31 - band, band)
    slot = pair * 32 + side * 16 + (tile // 32) * 2 + rank
    code = block_col * 32 + block_row + 1
    match = slot[None, :] == jnp.arange(512, dtype=jnp.int32)[:, None]
    labels = jnp.sum(jnp.where(match, code[None, :], 0), axis=1).astype(F32) - 1.0
    labels = jnp.broadcast_to(labels.reshape(1, PAIRS, 32), (CLASSES, PAIRS, 32)).reshape(devices, 32)
    labels = lax.all_to_all(labels, axes, split_axis=0, concat_axis=0, tiled=True).T

    l, r = left.astype(F32), right.astype(F32)
    beam = jnp.stack([
        l[:, 0] * r[:, 0] + l[:, 1] * r[:, 1],
        l[:, 1] * r[:, 0] - l[:, 0] * r[:, 1],
    ])
    outbox = make_outbox(uv, vis, beam, block_subgrid, slot[None, :], subgrid_tables(visible))
    arrived = lax.all_to_all(
        outbox.reshape(devices, 32, 128), axes, split_axis=0, concat_axis=0, tiled=True
    ).reshape(devices * 32, 128)
    x = place(arrived, labels)
    move = [(j * PAIRS + p, j * PAIRS + (p + 1) % PAIRS) for j in range(CLASSES) for p in range(PAIRS)]
    extra = lax.ppermute(x[8, :64], axes, move)
    flags = jnp.stack([me < PAIRS, me == 0]).astype(jnp.int32)
    k = down(flags, x.reshape(2048, 256), extra)
    k = lax.all_to_all(k.reshape(devices, 8, 128), axes, split_axis=0, concat_axis=0, tiled=True)
    return across(k.reshape(2048, 128))


def solution(mesh):
    placed = (
        P(("row", "col"), None, None),
        P(("row", "col"), None, None),
        P(("row", "col"), None, None),
        P(("row", "col"), None, None),
        P(("row", "col"), None),
        P(("row", "col"), None),
        P(("row", "col")),
        P(("row", "col")),
    )
    return jax.shard_map(
        body, mesh=mesh, in_specs=placed, out_specs=P(("row", "col"), None), check_vma=False
    )
```

```python
import math
from functools import partial

import jax
import jax.numpy as jnp
import ml_dtypes
import numpy as np
from jax import lax
from jax.experimental import pallas as pl
from jax.experimental.pallas import tpu as pltpu
from jax.sharding import Mesh, PartitionSpec as P

G = 8192
SUB = 32
PAIRS = 16
CLASSES = 16
STEP = 32
F32 = jnp.float32
BF16 = jnp.bfloat16
MB = 1 << 20


def halves(table):
    high = np.asarray(table, np.float32).astype(ml_dtypes.bfloat16)
    low = (np.asarray(table, np.float64) - high.astype(np.float64)).astype(ml_dtypes.bfloat16)
    return high, low


def split(x):
    high = x.astype(BF16)
    return high, (x - high.astype(F32)).astype(BF16)


def dot(a, b):
    return lax.dot_general(a, b, (((1,), (0,)), ((), ())), preferred_element_type=F32)


def dot_nt(a, b):
    return lax.dot_general(a, b, (((1,), (1,)), ((), ())), preferred_element_type=F32)


def dot3(ah, al, bh, bl):
    return dot(ah, bh) + (dot(al, bh) + dot(ah, bl))


def taper(p):
    return np.sin(math.pi * (p + 0.5) / SUB)


def class_column(j, c2):
    return j if c2 == 0 else (16 if j == 0 else 32 - j)


def subgrid_tables(visible):
    m = np.arange(32)
    first = np.zeros((2, 4, 32, 2, 4, 2, 8, 2))
    second = np.zeros((8, 4, 2, 8, 2, 8, 2, 2, 32))
    for cg in range(2):
        for j8 in range(8):
            for c2 in range(2):
                phi = 2 * math.pi * ((class_column(cg * 8 + j8, c2) * m) % 32) / 32
                for l4 in range(4):
                    first[0, l4, :, cg, l4, 0, j8, c2] = np.cos(phi) * taper(m)
                    first[1, l4, :, cg, l4, 0, j8, c2] = np.sin(phi) * taper(m)
                    first[0, l4, :, cg, l4, 1, j8, c2] = -np.sin(phi) * taper(m)
                    first[1, l4, :, cg, l4, 1, j8, c2] = np.cos(phi) * taper(m)
    a = np.arange(32)
    scale = visible ** (-0.5) / SUB / G
    for l8 in range(8):
        for l4 in range(4):
            l = 4 * l8 + l4
            phi = 2 * math.pi * ((a * l) % 32) / 32
            weight = taper(l) * scale
            for j8 in range(8):
                for c2 in range(2):
                    second[l8, l4, 0, j8, c2, j8, c2, 0] = np.cos(phi) * weight
                    second[l8, l4, 1, j8, c2, j8, c2, 0] = np.sin(phi) * weight
                    second[l8, l4, 0, j8, c2, j8, c2, 1] = -np.sin(phi) * weight
                    second[l8, l4, 1, j8, c2, j8, c2, 1] = np.cos(phi) * weight
    return first.reshape(256, 256), second.reshape(1024, 1024)


def down_tables():
    r = np.arange(256)[:, None, None, None]
    nt, q4, lo = np.meshgrid(np.arange(2), np.arange(4), np.arange(32), indexing="ij")
    l1 = ((nt * 4 + q4) * 32 + lo)[None]
    phi = 2 * math.pi * ((r * l1) % 256) / 256
    c, s = np.cos(phi), np.sin(phi)
    w = np.zeros((2, 256, 2, 2, 4, 2, 32))
    w[0, :, :, 0, :, 0], w[1, :, :, 0, :, 0] = c, -s
    w[0, :, :, 0, :, 1], w[1, :, :, 0, :, 1] = s, c
    w[0, :, :, 1, :, 0], w[1, :, :, 1, :, 0] = -s, -c
    w[0, :, :, 1, :, 1], w[1, :, :, 1, :, 1] = c, -s
    a = np.arange(32)[None, :, None, None]
    l1 = ((nt * 4 + q4) * 32 + lo)[:, None]
    psi = 2 * math.pi * a * l1 / G
    c, s = np.cos(psi), np.sin(psi)
    t = np.zeros((2, 4, 2, 2, 32, 4, 2, 32))
    for which in range(2):
        t[which, 0, :, 0, :, :, 0], t[which, 1, :, 0, :, :, 0] = c, s
        t[which, 2, :, 0, :, :, 0], t[which, 3, :, 0, :, :, 0] = -s, c
    t[0, 0, :, 0, :, :, 1], t[0, 1, :, 0, :, :, 1] = c, s
    t[0, 2, :, 0, :, :, 1], t[0, 3, :, 0, :, :, 1] = -s, c
    t[0, 0, :, 1, :, :, 0], t[0, 1, :, 1, :, :, 0] = c, s
    t[0, 2, :, 1, :, :, 0], t[0, 3, :, 1, :, :, 0] = s, -c
    t[0, 0, :, 1, :, :, 1], t[0, 1, :, 1, :, :, 1] = -c, -s
    t[0, 2, :, 1, :, :, 1], t[0, 3, :, 1, :, :, 1] = -s, c
    t[1, 0, :, 1, :, :, 1], t[1, 1, :, 1, :, :, 1] = -s, c
    t[1, 2, :, 1, :, :, 1], t[1, 3, :, 1, :, :, 1] = c, s
    phi = 2 * math.pi * ((np.arange(32)[:, None] * np.arange(32)[None, :]) % 32) / 32
    e = np.zeros((32, 2, 2, 32))
    e[:, 0, 0], e[:, 0, 1] = np.cos(phi), np.cos(phi)
    e[:, 1, 0], e[:, 1, 1] = np.sin(phi), -np.sin(phi)
    return w.reshape(512, 1024), t.reshape(16, 64, 256).astype(np.float32), e.reshape(32, 128)


def across_tables():
    p, bc = np.meshgrid(np.arange(16), np.arange(8), indexing="ij")
    m1 = np.arange(256)[None, None, :]
    w = np.zeros((2, 2, 128, 2, 256))
    for s in range(2):
        v1 = (8 * p + bc if s == 0 else 8 * (31 - p) + bc).reshape(128, 1)
        phi = 2 * math.pi * ((v1 * np.arange(256)[None, :]) % 256) / 256
        w[s, 0, :, 0], w[s, 1, :, 0] = np.cos(phi), -np.sin(phi)
        w[s, 0, :, 1], w[s, 1, :, 1] = np.sin(phi), np.cos(phi)
    zero = w[0].copy()
    zero[1, 0, 0] = 1 - 2 * (np.arange(256) % 2)
    zero[1, 0, 1] = 0
    psi = 2 * math.pi * np.arange(17)[:, None] * np.arange(256)[None, :] / G
    twist = np.concatenate([np.cos(psi), np.sin(psi)], axis=1).astype(np.float32)
    return w.reshape(512, 512), zero.reshape(256, 512), twist


def turn(t):
    quarter = jnp.round(t * 4.0)
    x = (t - quarter * 0.25) * (2 * math.pi)
    y = x * x
    sine = x * (1 + y * (-1 / 6 + y * (1 / 120 + y * (-1 / 5040 + y * (1 / 362880)))))
    cosine = 1 + y * (-0.5 + y * (1 / 24 + y * (-1 / 720 + y * (1 / 40320))))
    q = quarter.astype(jnp.int32)
    odd = (q & 1) != 0
    c = jnp.where(odd, sine, cosine)
    s = jnp.where(odd, cosine, sine)
    c = jnp.where(((q + 1) & 2) != 0, -c, c)
    s = jnp.where((q & 2) != 0, -s, s)
    return c, s


def times(x, y):
    return x[0] * y[0] - x[1] * y[1], x[0] * y[1] + x[1] * y[0]


def conj(x):
    return x[0], -x[1]


def grid_kernel(
    uv_ref, vis_ref, beam_ref, seg_ref, tile_ref, row_ref, col_ref, d1h, d1l, d2h, d2l,
    out_ref,
    base_l, base_m, fact_l, fact_m, image, ch, cl, ah, al,
):
    step = pl.program_id(0)
    n = STEP
    zu = turn(uv_ref[:, 0, :] * (1 / 32))
    zv = turn(uv_ref[:, 1, :] * (1 / 32))
    vis = (vis_ref[:, 0, :], vis_ref[:, 1, :])
    u2 = times(zu, zu)
    u3 = times(u2, zu)
    u4 = times(u2, u2)
    u8 = times(u4, u4)
    u12 = times(u8, u4)
    u16 = times(u8, u8)
    for i, f in enumerate((conj(u16), conj(u12), conj(u8), conj(u4), None, u4, u8, u12)):
        b = vis if f is None else times(vis, f)
        base_l[0, pl.ds(i, n, stride=8), :] = b[0]
        base_l[1, pl.ds(i, n, stride=8), :] = b[1]
    for i, f in enumerate((zu, u2, u3)):
        fact_l[2 * i] = f[0]
        fact_l[2 * i + 1] = f[1]
    v2 = times(zv, zv)
    v3 = times(v2, zv)
    v4 = times(v2, v2)
    v5 = times(v4, zv)
    v6 = times(v4, v2)
    v7 = times(v4, v3)
    v8 = times(v4, v4)
    v16 = times(v8, v8)
    one = (jnp.ones_like(zv[0]), jnp.zeros_like(zv[0]))
    for i, f in enumerate((one, zv, v2, v3, v4, v5, v6, v7)):
        base_m[0, pl.ds(i, n, stride=8), :] = f[0]
        base_m[1, pl.ds(i, n, stride=8), :] = f[1]
    for i, f in enumerate((conj(v16), conj(v8), v8)):
        fact_m[2 * i] = f[0]
        fact_m[2 * i + 1] = f[1]

    def one_block(b, _):
        rows = pl.ds(pl.multiple_of(b * 8, 8), 8)
        line = pl.ds(b, 1)
        bl = (base_l[0, rows, :], base_l[1, rows, :])
        bm = (base_m[0, rows, :], base_m[1, rows, :])
        left, right = [], []
        for t in range(4):
            w = bl if t == 0 else times(bl, (fact_l[2 * t - 2, line, :], fact_l[2 * t - 1, line, :]))
            left += [w[0], w[1]]
            right += [-w[1], w[0]]
        lh, ll = split(jnp.concatenate(
            [jnp.concatenate(left, axis=0), jnp.concatenate(right, axis=0)], axis=1))
        cosine, sine = [], []
        for t in range(4):
            i = {0: 0, 1: 1, 3: 2}.get(t)
            w = bm if i is None else times(bm, (fact_m[2 * i, line, :], fact_m[2 * i + 1, line, :]))
            cosine.append(w[0])
            sine.append(w[1])
        mh, ml = split(jnp.concatenate(
            [jnp.concatenate(cosine, axis=0), jnp.concatenate(sine, axis=0)], axis=1))
        o = dot_nt(lh, mh) + (dot_nt(ll, mh) + dot_nt(lh, ml))
        image[0, rows, :] = jnp.concatenate([o[16 * t:16 * t + 8] for t in range(4)], axis=1)
        image[1, rows, :] = jnp.concatenate([o[16 * t + 8:16 * t + 16] for t in range(4)], axis=1)
        return 0

    lax.fori_loop(0, n, one_block, 0, unroll=4)

    here = pl.ds(pl.multiple_of(step * n, n), n)
    for l8 in range(8):
        im = (image[0, pl.ds(l8, n, stride=8), :], image[1, pl.ds(l8, n, stride=8), :])
        bm = (beam_ref[0, :, l8 * 128:(l8 + 1) * 128], beam_ref[1, :, l8 * 128:(l8 + 1) * 128])
        c = times(bm, im)
        for ri in range(2):
            h, l = split(c[ri])
            ch[here, (2 * l8 + ri) * 128:(2 * l8 + ri + 1) * 128] = h
            cl[here, (2 * l8 + ri) * 128:(2 * l8 + ri + 1) * 128] = l

    @pl.when(step == pl.num_programs(0) - 1)
    def _():
        subs = tile_ref.shape[0]
        tall = subs + 8
        down_it = jnp.broadcast_to(tile_ref[...].astype(F32), (subs, subs))
        along = down_it.T
        ids = [lax.broadcasted_iota(jnp.int32, (subs, subs), d) for d in range(2)]
        earlier = (down_it == along) & (ids[0] < ids[1])
        rank = jnp.sum(earlier.astype(F32), axis=0, keepdims=True).astype(jnp.int32)
        tile = along[:1].astype(jnp.int32)
        band = tile % 32
        side = (band >= 16).astype(jnp.int32)
        pair = jnp.where(side == 1, 31 - band, band)
        slot = pair * 32 + side * 16 + (tile // 32) * 2 + rank
        code = (slot * 256 + col_ref[...] * 32 + row_ref[...]).astype(F32)
        for j in range(CLASSES):
            out_ref[j * tall + subs:(j + 1) * tall, :] = jnp.broadcast_to(code, (8, subs))
        blocks = seg_ref.shape[1]
        pick = (seg_ref[...] == lax.broadcasted_iota(jnp.int32, (subs, blocks), 0)).astype(F32).astype(BF16)
        for l8 in range(8):
            lanes = slice(l8 * 256, (l8 + 1) * 256)
            ih, il = split(dot(pick, ch[:, lanes]) + dot(pick, cl[:, lanes]))
            a = dot3(ih, il, d1h[...], d1l[...])
            for cg in range(2):
                h, l = split(a[:, cg * 128:(cg + 1) * 128])
                ah[cg * subs:(cg + 1) * subs, l8 * 128:(l8 + 1) * 128] = h
                al[cg * subs:(cg + 1) * subs, l8 * 128:(l8 + 1) * 128] = l
        for tile in range(4):
            lanes = slice(tile * 256, (tile + 1) * 256)
            spec = dot3(ah[...], al[...], d2h[:, lanes], d2l[:, lanes])
            for cg in range(2):
                for k in range(2):
                    j = cg * 8 + tile * 2 + k
                    out_ref[j * tall:j * tall + subs, :] = spec[cg * subs:(cg + 1) * subs, k * 128:(k + 1) * 128]


def make_payload(uv, vis, beam, seg, tile, row, col, tables):
    blocks, _, visible = uv.shape
    subs = tile.shape[0]
    tall = subs + 8
    (d1h, d1l), (d2h, d2l) = [halves(t) for t in tables]
    whole = lambda shape: pl.BlockSpec(shape, lambda i: (0,) * len(shape))
    return pl.pallas_call(
        grid_kernel,
        grid=(blocks // STEP,),
        in_specs=[
            pl.BlockSpec((STEP, 2, visible), lambda i: (i, 0, 0)),
            pl.BlockSpec((STEP, 2, visible), lambda i: (i, 0, 0)),
            pl.BlockSpec((2, STEP, SUB * SUB), lambda i: (0, i, 0)),
            whole((1, blocks)), whole((subs, 1)), whole((1, subs)), whole((1, subs)),
            whole((256, 256)), whole((256, 256)), whole((1024, 1024)), whole((1024, 1024)),
        ],
        out_specs=whole((CLASSES * tall, 128)),
        out_shape=jax.ShapeDtypeStruct((CLASSES * tall, 128), F32),
        scratch_shapes=[
            pltpu.VMEM((2, STEP * 8, 128), F32),
            pltpu.VMEM((2, STEP * 8, 128), F32),
            pltpu.VMEM((6, STEP, 128), F32),
            pltpu.VMEM((6, STEP, 128), F32),
            pltpu.VMEM((2, STEP * 8, 128), F32),
            pltpu.VMEM((blocks, 2048), BF16),
            pltpu.VMEM((blocks, 2048), BF16),
            pltpu.VMEM((2 * subs, 1024), BF16),
            pltpu.VMEM((2 * subs, 1024), BF16),
        ],
        compiler_params=pltpu.CompilerParams(vmem_limit_bytes=48 * MB),
        name="gridding",
    )(uv, vis, beam, seg, tile, row, col, d1h, d1l, d2h, d2l)


MESH = pl.DeviceIdType.MESH


def device(pair, kind):
    return (pair // 4, kind % 2, kind // 2, pair % 4)


def exchange_kernel(
    src_ref, out_ref, extra_ref,
    near, box, held, grid_ref, edge_src, edge_in,
    near_send, near_recv, far_send, far_recv, edge_send, edge_recv,
):
    group = lax.axis_index("y") * 4 + lax.axis_index("x")
    kind = lax.axis_index("z") * 2 + lax.axis_index("core")
    tall = src_ref.shape[0] // CLASSES
    subs = tall - 8
    part = 8 * 32 + 8

    barrier = pltpu.get_barrier_semaphore()

    def greet(k, _):
        pl.semaphore_signal(barrier, inc=1, device_id=device(group, (kind + k) % 16), device_id_type=MESH)
        pl.semaphore_signal(barrier, inc=1, device_id=device((group + k) % 16, kind), device_id_type=MESH)
        return 0

    lax.fori_loop(1, 16, greet, 0)
    pl.semaphore_wait(barrier, 30)

    def near_copy(k):
        to = (kind + k) % 16
        return pltpu.make_async_remote_copy(
            src_ref=src_ref.at[pl.ds(pl.multiple_of(to * tall, 8), tall), :],
            dst_ref=near.at[k],
            send_sem=near_send.at[k],
            recv_sem=near_recv.at[k],
            device_id=device(group, to),
            device_id_type=MESH,
        )

    def far_copy(g, k):
        to = (group + k) % 16
        h, rows = g // 2, pl.ds((g % 2) * 128, 128 + 8 * (g % 2))
        return pltpu.make_async_remote_copy(
            src_ref=box.at[h, to, rows, :],
            dst_ref=held.at[h, k, rows, :],
            send_sem=far_send.at[g, k],
            recv_sem=far_recv.at[g, k],
            device_id=device((group + k) % 16, kind),
            device_id_type=MESH,
        )

    def loop(lo, hi, f):
        def step(k, _):
            f(k)
            return 0

        lax.fori_loop(lo, hi, step, 0)

    loop(1, 16, lambda k: near_copy(k).start())
    near[0] = src_ref[pl.ds(pl.multiple_of(kind * tall, 8), tall), :]

    slots = lax.broadcasted_iota(jnp.int32, (512, subs), 0)
    line = lax.broadcasted_iota(jnp.int32, (8, subs), 0)

    def unfold(h, k8, codes):
        k = h * 8 + k8
        code = near[k, subs:subs + 1, :]
        fits = (code.astype(jnp.int32) // 256 == slots).astype(F32).astype(BF16)
        hi, lo = split(near[k, :subs, :])
        o = dot(jnp.concatenate([fits, fits], axis=1), jnp.concatenate([hi, lo], axis=0))
        rows = pl.ds(pl.multiple_of(k8 * 32, 32), 32)
        for p in range(PAIRS):
            box[h, p, rows, :] = o[p * 32:(p + 1) * 32]
        return jnp.where(line == k8, code, codes)

    for g in range(4):
        h = g // 2
        if g % 2 == 0:
            codes = jnp.zeros((8, subs), F32)

        def one(i, codes):
            k8 = (g % 2) * 4 + i
            near_copy(h * 8 + k8).wait_recv()
            return unfold(h, k8, codes)

        if g == 0:
            codes = unfold(0, 0, codes)
        codes = lax.fori_loop(1 if g == 0 else 0, 4, one, codes)
        if g % 2 == 1:
            for p in range(PAIRS):
                box[h, p, 256:264, :] = codes
        loop(1, 16, lambda k: far_copy(g, k).start())
        if g % 2 == 1:
            held[h, 0] = box[h, group]

    pos = lax.broadcasted_iota(jnp.int32, (256, 256), 0).astype(F32)
    for h in range(2):
        for g in (2 * h, 2 * h + 1):
            loop(1, 16, lambda k: far_copy(g, k).wait_recv())
        code = jnp.concatenate([held[h, k, 256:264, :] for k in range(16)], axis=0).T.astype(jnp.int32)
        at = code // 256 - group * 32
        value = (code % 256 + 1).astype(F32)

        def put(i, _):
            hot, data = [], []
            for rank in range(2):
                slot = i * 2 + rank
                label = jnp.sum(jnp.where(at == slot, value, 0.0), axis=0, keepdims=True) - 1.0
                hot.append(label)
                data += [held[h, k, pl.ds(slot, 8, stride=32), :] for k in range(16)]
            fits = (jnp.concatenate(hot, axis=1) == pos).astype(F32).astype(BF16)
            hi, lo = split(jnp.concatenate(data, axis=0))
            v = dot(fits, jnp.concatenate([hi, lo], axis=1))
            v = v[:, :128] + v[:, 128:]
            rows = pl.ds(pl.multiple_of(i % 8 * 32, 32), 32)
            for bc in range(8):
                where = i // 8 * 8 + bc
                add = v[bc * 32:(bc + 1) * 32]
                grid_ref[where, rows, :] = add if h == 0 else grid_ref[where, rows, :] + add
            return 0

        if h == 0:
            lax.fori_loop(0, 16, put, 0)
        else:
            lax.fori_loop(8, 16, put, 0)
            edge_src[...] = grid_ref[8].T[:64]
            edge = pltpu.make_async_remote_copy(
                src_ref=edge_src, dst_ref=edge_in, send_sem=edge_send, recv_sem=edge_recv,
                device_id=device((group + 1) % 16, kind), device_id_type=MESH,
            )
            edge.start()
            lax.fori_loop(0, 8, put, 0)

    def flip(i):
        out_ref[i] = grid_ref[i].T

    loop(0, 16, flip)
    edge.wait()
    extra_ref[...] = edge_in[...]
    loop(1, 16, lambda k: near_copy(k).wait_send())
    for g in range(4):
        loop(1, 16, lambda k: far_copy(g, k).wait_send())


def exchange(payload):
    tall = payload.shape[0] // CLASSES
    vmem = pl.BlockSpec(memory_space=pltpu.VMEM)
    dma = pltpu.SemaphoreType.DMA
    return pl.pallas_call(
        exchange_kernel,
        in_specs=[vmem],
        out_specs=[vmem, vmem],
        out_shape=[jax.ShapeDtypeStruct((16, 128, 256), F32), jax.ShapeDtypeStruct((64, 256), F32)],
        scratch_shapes=[
            pltpu.VMEM((16, tall, 128), F32),
            pltpu.VMEM((2, 16, 264, 128), F32),
            pltpu.VMEM((2, 16, 264, 128), F32),
            pltpu.VMEM((16, 256, 128), F32),
            pltpu.VMEM((64, 256), F32),
            pltpu.VMEM((64, 256), F32),
            dma((16,)), dma((16,)), dma((4, 16)), dma((4, 16)), dma(()), dma(()),
        ],
        compiler_params=pltpu.CompilerParams(
            collective_id=0, has_side_effects=True, vmem_limit_bytes=40 * MB
        ),
        name="exchange",
    )(payload)


def down_kernel(flag_ref, x_ref, extra_ref, wh, wl, t_ref, eh, el, out_ref, lh, ll):
    zero_class = flag_ref[0] == 1
    special = flag_ref[1]
    x0_ref, x1_ref = x_ref.at[0:1024, :], x_ref.at[1024:2048, :]
    near = lambda ref, bc: ref[bc * 128:bc * 128 + 64, :]
    far = lambda ref, bc: ref[bc * 128 + 64:bc * 128 + 128, :]
    for bc in range(8):
        for s in range(2):
            if s == 0:
                own = near(x0_ref, bc)
                edge = extra_ref[...] if bc == 0 else near(x1_ref, 8 - bc)
                mirror = jnp.where(zero_class, edge, far(x1_ref, 7 - bc))
            else:
                own = jnp.where(zero_class, far(x0_ref, bc), near(x1_ref, bc))
                mirror = jnp.where(zero_class, far(x1_ref, 7 - bc), far(x0_ref, 7 - bc))
            for c2, v in enumerate((own, mirror)):
                h, l = split(v)
                row = (bc * 2 + s) * 64 + c2 * 32
                for ri in range(2):
                    lh[row:row + 32, ri * 256:(ri + 1) * 256] = h[ri * 32:(ri + 1) * 32]
                    ll[row:row + 32, ri * 256:(ri + 1) * 256] = l[ri * 32:(ri + 1) * 32]
    e2 = jnp.concatenate([eh[...], eh[...]], axis=1)
    low = lax.broadcasted_iota(jnp.int32, (32, 128), 1) < 64

    def one(i, _):
        rows = pl.ds(pl.multiple_of(i * 256, 256), 256)
        for nt in range(2):
            cols = slice(nt * 512, (nt + 1) * 512)
            y = dot3(lh[rows, :], ll[rows, :], wh[:, cols], wl[:, cols])
            for k in range(2):
                bc = i * 2 + k
                parts = []
                for s in range(2):
                    r = (k * 2 + s) * 64
                    ya, yb = y[r:r + 64, :256], y[r:r + 64, 256:]
                    which = 0
                    if s == 0 and k == 0:
                        which = jnp.where(i == 0, special, 0)
                    tab = lambda n: t_ref[which * 8 + n * 2 + nt]
                    parts.append(jnp.concatenate(
                        [ya * tab(0) + yb * tab(1), ya * tab(2) + yb * tab(3)], axis=0))
                th, tl = split(jnp.concatenate(parts, axis=1))
                o = dot(e2, jnp.concatenate([th, tl], axis=0)) + dot(el[...], th)
                for g in range(2):
                    o0 = o[:, g * 128:(g + 1) * 128]
                    o1 = o[:, 256 + g * 128:256 + (g + 1) * 128]
                    q = nt * 4 + g * 2
                    out_ref[pl.ds(q * 8 + bc, 32, stride=64), :] = jnp.where(low, o0, pltpu.roll(o1, 64, 1))
                    out_ref[pl.ds((q + 1) * 8 + bc, 32, stride=64), :] = jnp.where(low, pltpu.roll(o0, 64, 1), o1)
        return 0

    lax.fori_loop(0, 4, one, 0)


def down(flags, x, extra):
    w, t, e = down_tables()
    wh, wl = halves(w)
    eh, el = halves(e)
    vmem = pl.BlockSpec(memory_space=pltpu.VMEM)
    return pl.pallas_call(
        down_kernel,
        in_specs=[pl.BlockSpec(memory_space=pltpu.SMEM)] + [vmem] * 7,
        out_shape=jax.ShapeDtypeStruct((2048, 128), F32),
        scratch_shapes=[pltpu.VMEM((1024, 512), BF16), pltpu.VMEM((1024, 512), BF16)],
        compiler_params=pltpu.CompilerParams(vmem_limit_bytes=40 * MB),
        name="down",
    )(flags, x, extra, wh, wl, t, eh, el)


def across_kernel(k_ref, wh, wl, zh, zl, twist, out_ref, lh, ll, y_ref):
    for j in range(16):
        z, core = j // 2, j % 2
        at = [((y * 2 + core) * 32 + z * 4) * 8 for y in range(4)]
        a = jnp.concatenate([k_ref[i:i + 32, :] for i in at], axis=0).T
        h, l = split(a)
        for i in range(4):
            lh[j * 32:(j + 1) * 32, i * 128:(i + 1) * 128] = h[i * 32:(i + 1) * 32]
            ll[j * 32:(j + 1) * 32, i * 128:(i + 1) * 128] = l[i * 32:(i + 1) * 32]
    y_ref[0:32] = dot3(lh[0:32, :256], ll[0:32, :256], zh[...], zl[...])
    y_ref[512:544] = dot3(lh[0:32, 256:], ll[0:32, 256:], wh[:256, :], wl[:256, :])
    y_ref[32:512] = dot3(lh[32:512, :], ll[32:512, :], wh[...], wl[...])

    cos = [math.cos(2 * math.pi * i / 32) for i in range(32)]
    sin = [math.sin(2 * math.pi * i / 32) for i in range(32)]

    def combine(terms):
        total = None
        for f, x in terms:
            if abs(f) < 1e-12:
                continue
            v = x if f == 1.0 else -x if f == -1.0 else x * f
            total = v if total is None else total + v
        return total

    def rows(i, _):
        at = pl.multiple_of(i * 8, 8)
        for half in range(2):
            lane = slice(half * 128, (half + 1) * 128)
            tre, tim = [], []
            for v in range(17):
                yre = y_ref[pl.ds(v * 32 + at, 8), lane]
                yim = y_ref[pl.ds(v * 32 + at, 8), 256 + half * 128:256 + (half + 1) * 128]
                c = twist[v:v + 1, lane]
                s = twist[v:v + 1, 256 + half * 128:256 + (half + 1) * 128]
                tre.append(yre * c - yim * s)
                tim.append(yre * s + yim * c)
            for m2 in range(9):
                e0 = combine([(cos[v * m2 % 32], tre[v]) for v in range(0, 17, 2)])
                e1 = combine([(cos[v * m2 % 32], tre[v]) for v in range(1, 17, 2)])
                o0 = combine([(sin[v * m2 % 32], tim[v]) for v in range(0, 17, 2)])
                o1 = combine([(sin[v * m2 % 32], tim[v]) for v in range(1, 17, 2)])
                zero = jnp.zeros((8, 128), F32)
                e0, e1, o0, o1 = [zero if x is None else x for x in (e0, e1, o0, o1)]
                puts = {m2: (e0 + e1) - (o0 + o1), (32 - m2) % 32: (e0 + e1) + (o0 + o1)}
                puts[16 - m2] = (e0 - e1) + (o0 - o1)
                puts[16 + m2] = (e0 - e1) - (o0 - o1)
                for m, v in puts.items():
                    out_ref[pl.ds(at, 8), m * 256 + half * 128:m * 256 + (half + 1) * 128] = v
        return 0

    lax.fori_loop(0, 4, rows, 0)


def across(k):
    w, zero, twist = across_tables()
    wh, wl = halves(w)
    zh, zl = halves(zero)
    return pl.pallas_call(
        across_kernel,
        out_shape=jax.ShapeDtypeStruct((32, G), F32),
        scratch_shapes=[
            pltpu.VMEM((512, 512), BF16), pltpu.VMEM((512, 512), BF16), pltpu.VMEM((544, 512), F32),
        ],
        compiler_params=pltpu.CompilerParams(vmem_limit_bytes=32 * MB),
        name="across",
    )(k, wh, wl, zh, zl, twist)


def body(uv, vis, left, right, block_subgrid, subgrid_tile, block_row, block_col):
    every = ("y", "core", "z", "x")
    devices = math.prod(lax.axis_size(a) for a in every)
    group = lax.axis_index("y") * lax.axis_size("x") + lax.axis_index("x")
    kind = lax.axis_index("z") * lax.axis_size("core") + lax.axis_index("core")
    visible = uv.shape[2]

    l, r = left.astype(F32), right.astype(F32)
    beam = jnp.stack([
        l[:, 0] * r[:, 0] + l[:, 1] * r[:, 1],
        l[:, 1] * r[:, 0] - l[:, 0] * r[:, 1],
    ])
    payload = make_payload(
        uv, vis, beam, block_subgrid, subgrid_tile, block_row[None], block_col[None], subgrid_tables(visible)
    )
    x, extra = exchange(payload)
    flags = jnp.stack([kind == 0, (kind == 0) & (group == 0)]).astype(jnp.int32)
    k = down(flags, x.reshape(2048, 256), extra)
    k = lax.all_to_all(k.reshape(devices, 8, 128), every, split_axis=0, concat_axis=0, tiled=True)
    return across(k.reshape(2048, 128))


def solution(mesh):
    names = ("y", "core", "z", "x")
    axes = Mesh(mesh.devices.reshape(4, 2, 8, 4), names)
    placed = (
        P(names, None, None),
        P(names, None, None),
        P(names, None, None),
        P(names, None, None),
        P(names, None),
        P(names, None),
        P(names),
        P(names),
    )
    return jax.shard_map(body, mesh=axes, in_specs=placed, out_specs=P(names, None), check_vma=False)
```

```python
import math
from functools import partial

import jax
import jax.numpy as jnp
import ml_dtypes
import numpy as np
from jax import lax
from jax.experimental import pallas as pl
from jax.experimental.pallas import tpu as pltpu
from jax.sharding import Mesh, PartitionSpec as P

G = 8192
SUB = 32
PAIRS = 16
CLASSES = 16
STEP = 32
F32 = jnp.float32
BF16 = jnp.bfloat16
MB = 1 << 20


def halves(table):
    high = np.asarray(table, np.float32).astype(ml_dtypes.bfloat16)
    low = (np.asarray(table, np.float64) - high.astype(np.float64)).astype(ml_dtypes.bfloat16)
    return high, low


def split(x):
    high = x.astype(BF16)
    return high, (x - high.astype(F32)).astype(BF16)


def dot(a, b):
    return lax.dot_general(a, b, (((1,), (0,)), ((), ())), preferred_element_type=F32)


def dot_nt(a, b):
    return lax.dot_general(a, b, (((1,), (1,)), ((), ())), preferred_element_type=F32)


def dot3(ah, al, bh, bl):
    return dot(ah, bh) + (dot(al, bh) + dot(ah, bl))


def taper(p):
    return np.sin(math.pi * (p + 0.5) / SUB)


def class_column(j, c2):
    return j if c2 == 0 else (16 if j == 0 else 32 - j)


def subgrid_tables(visible):
    m = np.arange(32)
    first = np.zeros((2, 4, 32, 2, 4, 2, 8, 2))
    second = np.zeros((8, 4, 2, 8, 2, 8, 2, 2, 32))
    for cg in range(2):
        for j8 in range(8):
            for c2 in range(2):
                phi = 2 * math.pi * ((class_column(cg * 8 + j8, c2) * m) % 32) / 32
                for l4 in range(4):
                    first[0, l4, :, cg, l4, 0, j8, c2] = np.cos(phi) * taper(m)
                    first[1, l4, :, cg, l4, 0, j8, c2] = np.sin(phi) * taper(m)
                    first[0, l4, :, cg, l4, 1, j8, c2] = -np.sin(phi) * taper(m)
                    first[1, l4, :, cg, l4, 1, j8, c2] = np.cos(phi) * taper(m)
    a = np.arange(32)
    scale = visible ** (-0.5) / SUB / G
    for l8 in range(8):
        for l4 in range(4):
            l = 4 * l8 + l4
            phi = 2 * math.pi * ((a * l) % 32) / 32
            weight = taper(l) * scale
            for j8 in range(8):
                for c2 in range(2):
                    second[l8, l4, 0, j8, c2, j8, c2, 0] = np.cos(phi) * weight
                    second[l8, l4, 1, j8, c2, j8, c2, 0] = np.sin(phi) * weight
                    second[l8, l4, 0, j8, c2, j8, c2, 1] = -np.sin(phi) * weight
                    second[l8, l4, 1, j8, c2, j8, c2, 1] = np.cos(phi) * weight
    return first.reshape(256, 256), second.reshape(1024, 1024)


def down_tables():
    r = np.arange(256)[:, None, None, None]
    nt, q4, lo = np.meshgrid(np.arange(2), np.arange(4), np.arange(32), indexing="ij")
    l1 = ((nt * 4 + q4) * 32 + lo)[None]
    phi = 2 * math.pi * ((r * l1) % 256) / 256
    c, s = np.cos(phi), np.sin(phi)
    w = np.zeros((2, 256, 2, 2, 4, 2, 32))
    w[0, :, :, 0, :, 0], w[1, :, :, 0, :, 0] = c, -s
    w[0, :, :, 0, :, 1], w[1, :, :, 0, :, 1] = s, c
    w[0, :, :, 1, :, 0], w[1, :, :, 1, :, 0] = -s, -c
    w[0, :, :, 1, :, 1], w[1, :, :, 1, :, 1] = c, -s
    a = np.arange(32)[None, :, None, None]
    l1 = ((nt * 4 + q4) * 32 + lo)[:, None]
    psi = 2 * math.pi * a * l1 / G
    c, s = np.cos(psi), np.sin(psi)
    t = np.zeros((2, 4, 2, 2, 32, 4, 2, 32))
    for which in range(2):
        t[which, 0, :, 0, :, :, 0], t[which, 1, :, 0, :, :, 0] = c, s
        t[which, 2, :, 0, :, :, 0], t[which, 3, :, 0, :, :, 0] = -s, c
    t[0, 0, :, 0, :, :, 1], t[0, 1, :, 0, :, :, 1] = c, s
    t[0, 2, :, 0, :, :, 1], t[0, 3, :, 0, :, :, 1] = -s, c
    t[0, 0, :, 1, :, :, 0], t[0, 1, :, 1, :, :, 0] = c, s
    t[0, 2, :, 1, :, :, 0], t[0, 3, :, 1, :, :, 0] = s, -c
    t[0, 0, :, 1, :, :, 1], t[0, 1, :, 1, :, :, 1] = -c, -s
    t[0, 2, :, 1, :, :, 1], t[0, 3, :, 1, :, :, 1] = -s, c
    t[1, 0, :, 1, :, :, 1], t[1, 1, :, 1, :, :, 1] = -s, c
    t[1, 2, :, 1, :, :, 1], t[1, 3, :, 1, :, :, 1] = c, s
    phi = 2 * math.pi * ((np.arange(32)[:, None] * np.arange(32)[None, :]) % 32) / 32
    e = np.zeros((32, 2, 2, 32))
    e[:, 0, 0], e[:, 0, 1] = np.cos(phi), np.cos(phi)
    e[:, 1, 0], e[:, 1, 1] = np.sin(phi), -np.sin(phi)
    return w.reshape(512, 1024), t.reshape(16, 64, 256).astype(np.float32), e.reshape(32, 128)


def across_tables():
    p, bc = np.meshgrid(np.arange(16), np.arange(8), indexing="ij")
    m1 = np.arange(256)[None, None, :]
    w = np.zeros((2, 2, 128, 2, 256))
    for s in range(2):
        v1 = (8 * p + bc if s == 0 else 8 * (31 - p) + bc).reshape(128, 1)
        phi = 2 * math.pi * ((v1 * np.arange(256)[None, :]) % 256) / 256
        w[s, 0, :, 0], w[s, 1, :, 0] = np.cos(phi), -np.sin(phi)
        w[s, 0, :, 1], w[s, 1, :, 1] = np.sin(phi), np.cos(phi)
    zero = w[0].copy()
    zero[1, 0, 0] = 1 - 2 * (np.arange(256) % 2)
    zero[1, 0, 1] = 0
    psi = 2 * math.pi * np.arange(17)[:, None] * np.arange(256)[None, :] / G
    twist = np.concatenate([np.cos(psi), np.sin(psi)], axis=1).astype(np.float32)
    return w.reshape(512, 512), zero.reshape(256, 512), twist


def turn(t):
    quarter = jnp.round(t * 4.0)
    x = (t - quarter * 0.25) * (2 * math.pi)
    y = x * x
    sine = x * (1 + y * (-1 / 6 + y * (1 / 120 + y * (-1 / 5040 + y * (1 / 362880)))))
    cosine = 1 + y * (-0.5 + y * (1 / 24 + y * (-1 / 720 + y * (1 / 40320))))
    q = quarter.astype(jnp.int32)
    odd = (q & 1) != 0
    c = jnp.where(odd, sine, cosine)
    s = jnp.where(odd, cosine, sine)
    c = jnp.where(((q + 1) & 2) != 0, -c, c)
    s = jnp.where((q & 2) != 0, -s, s)
    return c, s


def times(x, y):
    return x[0] * y[0] - x[1] * y[1], x[0] * y[1] + x[1] * y[0]


def conj(x):
    return x[0], -x[1]


def grid_kernel(
    uv_ref, vis_ref, beam_ref, seg_ref, tile_ref, row_ref, col_ref, d1h, d1l, d2h, d2l,
    out_ref,
    base_l, base_m, fact_l, fact_m, image, ch, cl, ah, al,
):
    step = pl.program_id(0)
    n = STEP
    zu = turn(uv_ref[:, 0, :] * (1 / 32))
    zv = turn(uv_ref[:, 1, :] * (1 / 32))
    vis = (vis_ref[:, 0, :], vis_ref[:, 1, :])
    u2 = times(zu, zu)
    u3 = times(u2, zu)
    u4 = times(u2, u2)
    u8 = times(u4, u4)
    u12 = times(u8, u4)
    u16 = times(u8, u8)
    for i, f in enumerate((conj(u16), conj(u12), conj(u8), conj(u4), None, u4, u8, u12)):
        b = vis if f is None else times(vis, f)
        base_l[0, pl.ds(i, n, stride=8), :] = b[0]
        base_l[1, pl.ds(i, n, stride=8), :] = b[1]
    for i, f in enumerate((zu, u2, u3)):
        fact_l[2 * i] = f[0]
        fact_l[2 * i + 1] = f[1]
    v2 = times(zv, zv)
    v3 = times(v2, zv)
    v4 = times(v2, v2)
    v5 = times(v4, zv)
    v6 = times(v4, v2)
    v7 = times(v4, v3)
    v8 = times(v4, v4)
    v16 = times(v8, v8)
    one = (jnp.ones_like(zv[0]), jnp.zeros_like(zv[0]))
    for i, f in enumerate((one, zv, v2, v3, v4, v5, v6, v7)):
        base_m[0, pl.ds(i, n, stride=8), :] = f[0]
        base_m[1, pl.ds(i, n, stride=8), :] = f[1]
    for i, f in enumerate((conj(v16), conj(v8), v8)):
        fact_m[2 * i] = f[0]
        fact_m[2 * i + 1] = f[1]

    def one_block(b, _):
        rows = pl.ds(pl.multiple_of(b * 8, 8), 8)
        line = pl.ds(b, 1)
        bl = (base_l[0, rows, :], base_l[1, rows, :])
        bm = (base_m[0, rows, :], base_m[1, rows, :])
        left, right = [], []
        for t in range(4):
            w = bl if t == 0 else times(bl, (fact_l[2 * t - 2, line, :], fact_l[2 * t - 1, line, :]))
            left += [w[0], w[1]]
            right += [-w[1], w[0]]
        lh, ll = split(jnp.concatenate(
            [jnp.concatenate(left, axis=0), jnp.concatenate(right, axis=0)], axis=1))
        cosine, sine = [], []
        for t in range(4):
            i = {0: 0, 1: 1, 3: 2}.get(t)
            w = bm if i is None else times(bm, (fact_m[2 * i, line, :], fact_m[2 * i + 1, line, :]))
            cosine.append(w[0])
            sine.append(w[1])
        mh, ml = split(jnp.concatenate(
            [jnp.concatenate(cosine, axis=0), jnp.concatenate(sine, axis=0)], axis=1))
        o = dot_nt(lh, mh) + (dot_nt(ll, mh) + dot_nt(lh, ml))
        image[0, rows, :] = jnp.concatenate([o[16 * t:16 * t + 8] for t in range(4)], axis=1)
        image[1, rows, :] = jnp.concatenate([o[16 * t + 8:16 * t + 16] for t in range(4)], axis=1)
        return 0

    lax.fori_loop(0, n, one_block, 0, unroll=4)

    here = pl.ds(pl.multiple_of(step * n, n), n)
    for l8 in range(8):
        im = (image[0, pl.ds(l8, n, stride=8), :], image[1, pl.ds(l8, n, stride=8), :])
        bm = (beam_ref[0, :, l8 * 128:(l8 + 1) * 128], beam_ref[1, :, l8 * 128:(l8 + 1) * 128])
        c = times(bm, im)
        for ri in range(2):
            h, l = split(c[ri])
            ch[here, (2 * l8 + ri) * 128:(2 * l8 + ri + 1) * 128] = h
            cl[here, (2 * l8 + ri) * 128:(2 * l8 + ri + 1) * 128] = l

    @pl.when(step == pl.num_programs(0) - 1)
    def _():
        subs = tile_ref.shape[0]
        tall = subs + 8
        down_it = jnp.broadcast_to(tile_ref[...].astype(F32), (subs, subs))
        along = down_it.T
        ids = [lax.broadcasted_iota(jnp.int32, (subs, subs), d) for d in range(2)]
        earlier = (down_it == along) & (ids[0] < ids[1])
        rank = jnp.sum(earlier.astype(F32), axis=0, keepdims=True).astype(jnp.int32)
        tile = along[:1].astype(jnp.int32)
        band = tile % 32
        side = (band >= 16).astype(jnp.int32)
        pair = jnp.where(side == 1, 31 - band, band)
        slot = pair * 32 + side * 16 + (tile // 32) * 2 + rank
        code = (slot * 256 + col_ref[...] * 32 + row_ref[...]).astype(F32)
        for j in range(CLASSES):
            out_ref[j * tall + subs:(j + 1) * tall, :] = jnp.broadcast_to(code, (8, subs))
        blocks = seg_ref.shape[1]
        pick = (seg_ref[...] == lax.broadcasted_iota(jnp.int32, (subs, blocks), 0)).astype(F32).astype(BF16)
        for l8 in range(8):
            lanes = slice(l8 * 256, (l8 + 1) * 256)
            ih, il = split(dot(pick, ch[:, lanes]) + dot(pick, cl[:, lanes]))
            a = dot3(ih, il, d1h[...], d1l[...])
            for cg in range(2):
                h, l = split(a[:, cg * 128:(cg + 1) * 128])
                ah[cg * subs:(cg + 1) * subs, l8 * 128:(l8 + 1) * 128] = h
                al[cg * subs:(cg + 1) * subs, l8 * 128:(l8 + 1) * 128] = l
        for tile in range(4):
            lanes = slice(tile * 256, (tile + 1) * 256)
            spec = dot3(ah[...], al[...], d2h[:, lanes], d2l[:, lanes])
            for cg in range(2):
                for k in range(2):
                    j = cg * 8 + tile * 2 + k
                    out_ref[j * tall:j * tall + subs, :] = spec[cg * subs:(cg + 1) * subs, k * 128:(k + 1) * 128]


def make_payload(uv, vis, beam, seg, tile, row, col, tables):
    blocks, _, visible = uv.shape
    subs = tile.shape[0]
    tall = subs + 8
    (d1h, d1l), (d2h, d2l) = [halves(t) for t in tables]
    whole = lambda shape: pl.BlockSpec(shape, lambda i: (0,) * len(shape))
    return pl.pallas_call(
        grid_kernel,
        grid=(blocks // STEP,),
        in_specs=[
            pl.BlockSpec((STEP, 2, visible), lambda i: (i, 0, 0)),
            pl.BlockSpec((STEP, 2, visible), lambda i: (i, 0, 0)),
            pl.BlockSpec((2, STEP, SUB * SUB), lambda i: (0, i, 0)),
            whole((1, blocks)), whole((subs, 1)), whole((1, subs)), whole((1, subs)),
            whole((256, 256)), whole((256, 256)), whole((1024, 1024)), whole((1024, 1024)),
        ],
        out_specs=whole((CLASSES * tall, 128)),
        out_shape=jax.ShapeDtypeStruct((CLASSES * tall, 128), F32),
        scratch_shapes=[
            pltpu.VMEM((2, STEP * 8, 128), F32),
            pltpu.VMEM((2, STEP * 8, 128), F32),
            pltpu.VMEM((6, STEP, 128), F32),
            pltpu.VMEM((6, STEP, 128), F32),
            pltpu.VMEM((2, STEP * 8, 128), F32),
            pltpu.VMEM((blocks, 2048), BF16),
            pltpu.VMEM((blocks, 2048), BF16),
            pltpu.VMEM((2 * subs, 1024), BF16),
            pltpu.VMEM((2 * subs, 1024), BF16),
        ],
        compiler_params=pltpu.CompilerParams(vmem_limit_bytes=48 * MB),
        name="gridding",
    )(uv, vis, beam, seg, tile, row, col, d1h, d1l, d2h, d2l)


MESH = pl.DeviceIdType.MESH


NEAR = [(0, 0), (0, 1), (1, 0), (-1, 0), (1, 1), (-1, 1), (2, 0), (-2, 0),
        (2, 1), (-2, 1), (3, 0), (-3, 0), (3, 1), (-3, 1), (4, 0), (4, 1)]
FAR = [(0, 1), (1, 0), (0, -1), (-1, 0), (0, 2), (2, 0), (1, 1), (-1, -1),
       (-1, 1), (1, -1), (2, 2), (1, 2), (2, 1), (-1, 2), (2, -1)]


def exchange_kernel(
    src_ref, wh_hbm, wl_hbm, t_hbm, eh, el, out_ref,
    near, box, held, grid_ref, x_ref, edge_src, edge_in, wh, wl, t_ref, lh, ll, kbuf, near2,
    near_send, near_recv, far_send, far_recv, edge_send, edge_recv, table_sem,
    near2_send, near2_recv, far2_send, far2_recv,
):
    y, core, z, x = [lax.axis_index(a) for a in ("y", "core", "z", "x")]
    group, kind = y * 4 + x, z * 2 + core
    tall = src_ref.shape[0] // CLASSES
    subs = tall - 8

    tables = [
        pltpu.make_async_copy(a, b, table_sem.at[n])
        for n, (a, b) in enumerate(((wh_hbm, wh), (wl_hbm, wl), (t_hbm, t_ref)))
    ]
    for c in tables:
        c.start()

    def loop(lo, hi, f):
        def step(k, _):
            f(k)
            return 0

        lax.fori_loop(lo, hi, step, 0)

    def to_near(k):
        dz, dc = NEAR[k]
        return (z + dz + 8) % 8, (core + dc) % 2

    def to_far(k):
        dy, dx = FAR[k]
        return (y + dy + 4) % 4, (x + dx + 4) % 4

    barrier = pltpu.get_barrier_semaphore()
    for k in range(1, 16):
        tz, tc = to_near(k)
        pl.semaphore_signal(barrier, inc=1, device_id=(y, tc, tz, x), device_id_type=MESH)
    for k in range(15):
        ty, tx = to_far(k)
        pl.semaphore_signal(barrier, inc=1, device_id=(ty, core, z, tx), device_id_type=MESH)
    pl.semaphore_wait(barrier, 30)

    def near_copy(k):
        tz, tc = to_near(k)
        return pltpu.make_async_remote_copy(
            src_ref=src_ref.at[pl.ds(pl.multiple_of((tz * 2 + tc) * tall, 8), tall), :],
            dst_ref=near.at[k],
            send_sem=near_send.at[k],
            recv_sem=near_recv.at[k],
            device_id=(y, tc, tz, x),
            device_id_type=MESH,
        )

    def far_copy(g, k):
        ty, tx = to_far(k)
        h, rows = g // 2, pl.ds((g % 2) * 128, 128 + 8 * (g % 2))
        return pltpu.make_async_remote_copy(
            src_ref=box.at[h, ty * 4 + tx, rows, :],
            dst_ref=held.at[h, k, rows, :],
            send_sem=far_send.at[g, k],
            recv_sem=far_recv.at[g, k],
            device_id=(ty, core, z, tx),
            device_id_type=MESH,
        )

    for k in range(1, 16):
        near_copy(k).start()
    near[0] = src_ref[pl.ds(pl.multiple_of(kind * tall, 8), tall), :]

    slots = lax.broadcasted_iota(jnp.int32, (512, subs), 0)
    line = lax.broadcasted_iota(jnp.int32, (8, subs), 0)
    codes = jnp.zeros((8, subs), F32)
    for g in range(4):
        h = g // 2
        for i in range(4):
            k8 = (g % 2) * 4 + i
            k = h * 8 + k8
            if k:
                near_copy(k).wait_recv()
            code = near[k, subs:subs + 1, :]
            fits = (code.astype(jnp.int32) // 256 == slots).astype(F32).astype(BF16)
            hi, lo = split(near[k, :subs, :])
            o = dot(jnp.concatenate([fits, fits], axis=1), jnp.concatenate([hi, lo], axis=0))
            for p in range(PAIRS):
                box[h, p, k8 * 32:k8 * 32 + 32, :] = o[p * 32:(p + 1) * 32]
            codes = jnp.where(line == k8, code, codes)
        if g % 2 == 1:
            for p in range(PAIRS):
                box[h, p, 256:264, :] = codes
        for k in range(15):
            far_copy(g, k).start()
        if g % 2 == 1:
            held[h, 15] = box[h, group]

    pos = lax.broadcasted_iota(jnp.int32, (256, 256), 0).astype(F32)
    for h in range(2):
        for g in (2 * h, 2 * h + 1):
            for k in range(15):
                far_copy(g, k).wait_recv()
        code = jnp.concatenate([held[h, k, 256:264, :] for k in range(16)], axis=0).T.astype(jnp.int32)
        at = code // 256 - group * 32
        value = (code % 256 + 1).astype(F32)

        def put(i):
            hot, data = [], []
            for rank in range(2):
                slot = i * 2 + rank
                label = jnp.sum(jnp.where(at == slot, value, 0.0), axis=0, keepdims=True) - 1.0
                hot.append(label)
                data += [held[h, k, pl.ds(slot, 8, stride=32), :] for k in range(16)]
            fits = (jnp.concatenate(hot, axis=1) == pos).astype(F32).astype(BF16)
            hi, lo = split(jnp.concatenate(data, axis=0))
            v = dot(fits, jnp.concatenate([hi, lo], axis=1))
            v = v[:, :128] + v[:, 128:]
            rows = pl.ds(pl.multiple_of(i % 8 * 32, 32), 32)
            for bc in range(8):
                where = i // 8 * 8 + bc
                add = v[bc * 32:(bc + 1) * 32]
                grid_ref[where, rows, :] = add if h == 0 else grid_ref[where, rows, :] + add

        def flip(i):
            x_ref[pl.ds(pl.multiple_of(i * 128, 128), 128), :] = grid_ref[i].T

        if h == 0:
            loop(0, 16, put)
        else:
            loop(8, 16, put)
            edge_src[...] = grid_ref[8].T[:64]
            tx, ty = (x + 1) % 4, (y + (x + 1) // 4) % 4
            edge = pltpu.make_async_remote_copy(
                src_ref=edge_src, dst_ref=edge_in, send_sem=edge_send, recv_sem=edge_recv,
                device_id=(ty, core, z, tx), device_id_type=MESH,
            )
            edge.start()
            loop(8, 16, flip)
            loop(0, 8, put)
            loop(0, 8, flip)

    edge.wait_recv()
    zero_class = kind == 0
    special = jnp.where((kind == 0) & (group == 0), 1, 0)
    near_x = lambda s, bc: x_ref[s * 1024 + bc * 128:s * 1024 + bc * 128 + 64, :]
    far_x = lambda s, bc: x_ref[s * 1024 + bc * 128 + 64:s * 1024 + bc * 128 + 128, :]
    for bc in range(8):
        for s in range(2):
            if s == 0:
                own = near_x(0, bc)
                first = edge_in[...] if bc == 0 else near_x(1, 8 - bc)
                mirror = jnp.where(zero_class, first, far_x(1, 7 - bc))
            else:
                own = jnp.where(zero_class, far_x(0, bc), near_x(1, bc))
                mirror = jnp.where(zero_class, far_x(1, 7 - bc), far_x(0, 7 - bc))
            for c2, v in enumerate((own, mirror)):
                hi, lo = split(v)
                row = (bc * 2 + s) * 64 + c2 * 32
                for ri in range(2):
                    lh[row:row + 32, ri * 256:(ri + 1) * 256] = hi[ri * 32:(ri + 1) * 32]
                    ll[row:row + 32, ri * 256:(ri + 1) * 256] = lo[ri * 32:(ri + 1) * 32]
    for c in tables:
        c.wait()
    e2 = jnp.concatenate([eh[...], eh[...]], axis=1)
    low = lax.broadcasted_iota(jnp.int32, (32, 128), 1) < 64

    def near2_copy(nt, t, dc):
        zh, tc = (z // 2 + t) % 4, (core + dc) % 2
        tz = zh * 2 + nt
        return (tz * 2 + tc) != kind, pltpu.make_async_remote_copy(
            src_ref=kbuf.at[pl.ds(pl.multiple_of((nt * 8 + tc * 4 + zh) * 128, 128), 128), :],
            dst_ref=near2.at[kind],
            send_sem=near2_send.at[nt, t, dc],
            recv_sem=near2_recv.at[kind],
            device_id=(y, tc, tz, x),
            device_id_type=MESH,
        )

    for nt in range(2):
        cols = slice(nt * 512, (nt + 1) * 512)

        def one(i):
            rows = pl.ds(pl.multiple_of(i * 256, 256), 256)
            v = dot3(lh[rows, :], ll[rows, :], wh[:, cols], wl[:, cols])
            for k in range(2):
                bc = i * 2 + k
                parts = []
                for s in range(2):
                    r = (k * 2 + s) * 64
                    ya, yb = v[r:r + 64, :256], v[r:r + 64, 256:]
                    which = 0
                    if s == 0 and k == 0:
                        which = jnp.where(i == 0, special, 0)
                    tab = lambda n: t_ref[which * 8 + n * 2 + nt]
                    parts.append(jnp.concatenate(
                        [ya * tab(0) + yb * tab(1), ya * tab(2) + yb * tab(3)], axis=0))
                th, tl = split(jnp.concatenate(parts, axis=1))
                o = dot(e2, jnp.concatenate([th, tl], axis=0)) + dot(el[...], th)
                for g in range(2):
                    o0 = o[:, g * 128:(g + 1) * 128]
                    o1 = o[:, 256 + g * 128:256 + (g + 1) * 128]
                    pair = (jnp.where(low, o0, pltpu.roll(o1, 64, 1)), jnp.where(low, pltpu.roll(o0, 64, 1), o1))
                    for e in range(2):
                        for ty in range(4):
                            first = nt * 1024 + ty * 32 + (g * 2 + e) * 8 + bc
                            kbuf[pl.ds(first, 8, stride=128), :] = pair[e][ty * 8:(ty + 1) * 8]

        loop(0, 4, one)
        for t in (0, 1, 3, 2):
            for dc in range(2):
                other, copy = near2_copy(nt, t, dc)

                @pl.when(other)
                def _():
                    copy.start()

    mine = (z % 2) * 8 + core * 4 + z // 2
    near2[kind] = kbuf[pl.ds(pl.multiple_of(mine * 128, 128), 128), :]

    def far2_copy(t, k):
        ty, tx = to_far(k)
        kinds = pl.ds(((z // 2 - t + 4) % 4) * 4, 4)
        return pltpu.make_async_remote_copy(
            src_ref=near2.at[kinds, pl.ds(pl.multiple_of((ty * 4 + tx) * 8, 8), 8), :],
            dst_ref=out_ref.at[kinds, pl.ds(pl.multiple_of(group * 8, 8), 8), :],
            send_sem=far2_send.at[t, k],
            recv_sem=far2_recv.at[t, k],
            device_id=(ty, core, z, tx),
            device_id_type=MESH,
        )

    for t in (0, 1, 3, 2):
        base = ((z // 2 - t + 4) % 4) * 4
        for i in range(4):
            sender = base + i

            @pl.when(sender != kind)
            def _():
                pltpu.make_async_remote_copy(
                    src_ref=kbuf.at[pl.ds(0, 128), :], dst_ref=near2.at[sender],
                    send_sem=near2_send.at[0, 0, 0], recv_sem=near2_recv.at[sender],
                    device_id=(y, 1 - core, z, x), device_id_type=MESH,
                ).wait_recv()

        for k in range(15):
            far2_copy(t, k).start()
        own = pl.ds(pl.multiple_of(group * 8, 8), 8)
        out_ref[pl.ds(base, 4), own, :] = near2[pl.ds(base, 4), own, :]

    for t in range(4):
        for k in range(15):
            far2_copy(t, k).wait_recv()
    edge.wait_send()
    for k in range(1, 16):
        near_copy(k).wait_send()
    for g in range(4):
        for k in range(15):
            far_copy(g, k).wait_send()
    for nt in range(2):
        for t in range(4):
            for dc in range(2):
                other, copy = near2_copy(nt, t, dc)

                @pl.when(other)
                def _():
                    copy.wait_send()
    for t in range(4):
        for k in range(15):
            far2_copy(t, k).wait_send()


def exchange(payload):
    tall = payload.shape[0] // CLASSES
    w, t, e = down_tables()
    wh, wl = halves(w)
    eh, el = halves(e)
    vmem = pl.BlockSpec(memory_space=pltpu.VMEM)
    hbm = pl.BlockSpec(memory_space=pl.ANY)
    dma = pltpu.SemaphoreType.DMA
    return pl.pallas_call(
        exchange_kernel,
        in_specs=[vmem, hbm, hbm, hbm, vmem, vmem],
        out_specs=vmem,
        out_shape=jax.ShapeDtypeStruct((16, 128, 128), F32),
        scratch_shapes=[
            pltpu.VMEM((16, tall, 128), F32),
            pltpu.VMEM((2, 16, 264, 128), F32),
            pltpu.VMEM((2, 16, 264, 128), F32),
            pltpu.VMEM((16, 256, 128), F32),
            pltpu.VMEM((2048, 256), F32),
            pltpu.VMEM((64, 256), F32),
            pltpu.VMEM((64, 256), F32),
            pltpu.VMEM((512, 1024), BF16),
            pltpu.VMEM((512, 1024), BF16),
            pltpu.VMEM((16, 64, 256), F32),
            pltpu.VMEM((1024, 512), BF16),
            pltpu.VMEM((1024, 512), BF16),
            pltpu.VMEM((2048, 128), F32),
            pltpu.VMEM((16, 128, 128), F32),
            dma((16,)), dma((16,)), dma((4, 16)), dma((4, 16)), dma(()), dma(()), dma((3,)),
            dma((2, 4, 2)), dma((16,)), dma((4, 16)), dma((4, 16)),
        ],
        compiler_params=pltpu.CompilerParams(
            collective_id=0, has_side_effects=True, vmem_limit_bytes=48 * MB
        ),
        name="exchange",
    )(payload, wh, wl, t, eh, el)


def across_kernel(k_ref, wh, wl, zh, zl, twist, out_ref, lh, ll, y_ref):
    for j in range(16):
        a = k_ref[j * 128:(j + 1) * 128, :].T
        h, l = split(a)
        for i in range(4):
            lh[j * 32:(j + 1) * 32, i * 128:(i + 1) * 128] = h[i * 32:(i + 1) * 32]
            ll[j * 32:(j + 1) * 32, i * 128:(i + 1) * 128] = l[i * 32:(i + 1) * 32]
    y_ref[0:32] = dot3(lh[0:32, :256], ll[0:32, :256], zh[...], zl[...])
    y_ref[512:544] = dot3(lh[0:32, 256:], ll[0:32, 256:], wh[:256, :], wl[:256, :])
    y_ref[32:512] = dot3(lh[32:512, :], ll[32:512, :], wh[...], wl[...])

    cos = [math.cos(2 * math.pi * i / 32) for i in range(32)]
    sin = [math.sin(2 * math.pi * i / 32) for i in range(32)]

    def combine(terms):
        total = None
        for f, x in terms:
            if abs(f) < 1e-12:
                continue
            v = x if f == 1.0 else -x if f == -1.0 else x * f
            total = v if total is None else total + v
        return total

    def rows(i, _):
        at = pl.multiple_of(i * 8, 8)
        for half in range(2):
            lane = slice(half * 128, (half + 1) * 128)
            tre, tim = [], []
            for v in range(17):
                yre = y_ref[pl.ds(v * 32 + at, 8), lane]
                yim = y_ref[pl.ds(v * 32 + at, 8), 256 + half * 128:256 + (half + 1) * 128]
                c = twist[v:v + 1, lane]
                s = twist[v:v + 1, 256 + half * 128:256 + (half + 1) * 128]
                tre.append(yre * c - yim * s)
                tim.append(yre * s + yim * c)
            for m2 in range(9):
                e0 = combine([(cos[v * m2 % 32], tre[v]) for v in range(0, 17, 2)])
                e1 = combine([(cos[v * m2 % 32], tre[v]) for v in range(1, 17, 2)])
                o0 = combine([(sin[v * m2 % 32], tim[v]) for v in range(0, 17, 2)])
                o1 = combine([(sin[v * m2 % 32], tim[v]) for v in range(1, 17, 2)])
                zero = jnp.zeros((8, 128), F32)
                e0, e1, o0, o1 = [zero if x is None else x for x in (e0, e1, o0, o1)]
                puts = {m2: (e0 + e1) - (o0 + o1), (32 - m2) % 32: (e0 + e1) + (o0 + o1)}
                puts[16 - m2] = (e0 - e1) + (o0 - o1)
                puts[16 + m2] = (e0 - e1) - (o0 - o1)
                for m, v in puts.items():
                    out_ref[pl.ds(at, 8), m * 256 + half * 128:m * 256 + (half + 1) * 128] = v
        return 0

    lax.fori_loop(0, 4, rows, 0)


def across(k):
    w, zero, twist = across_tables()
    wh, wl = halves(w)
    zh, zl = halves(zero)
    return pl.pallas_call(
        across_kernel,
        out_shape=jax.ShapeDtypeStruct((32, G), F32),
        scratch_shapes=[
            pltpu.VMEM((512, 512), BF16), pltpu.VMEM((512, 512), BF16), pltpu.VMEM((544, 512), F32),
        ],
        compiler_params=pltpu.CompilerParams(vmem_limit_bytes=32 * MB),
        name="across",
    )(k, wh, wl, zh, zl, twist)


def body(uv, vis, left, right, block_subgrid, subgrid_tile, block_row, block_col):
    visible = uv.shape[2]

    l, r = left.astype(F32), right.astype(F32)
    beam = jnp.stack([
        l[:, 0] * r[:, 0] + l[:, 1] * r[:, 1],
        l[:, 1] * r[:, 0] - l[:, 0] * r[:, 1],
    ])
    payload = make_payload(
        uv, vis, beam, block_subgrid, subgrid_tile, block_row[None], block_col[None], subgrid_tables(visible)
    )
    return across(exchange(payload).reshape(2048, 128))


def solution(mesh):
    names = ("y", "core", "z", "x")
    axes = Mesh(mesh.devices.reshape(4, 2, 8, 4), names)
    placed = (
        P(names, None, None),
        P(names, None, None),
        P(names, None, None),
        P(names, None, None),
        P(names, None),
        P(names, None),
        P(names),
        P(names),
    )
    return jax.shard_map(body, mesh=axes, in_specs=placed, out_specs=P(names, None), check_vma=False)
```

```python
import math
from functools import partial

import jax
import jax.numpy as jnp
import ml_dtypes
import numpy as np
from jax import lax
from jax.experimental import pallas as pl
from jax.experimental.pallas import tpu as pltpu
from jax.sharding import Mesh, PartitionSpec as P

G = 8192
SUB = 32
PAIRS = 16
CLASSES = 16
STEP = 32
F32 = jnp.float32
BF16 = jnp.bfloat16
MB = 1 << 20


def halves(table):
    high = np.asarray(table, np.float32).astype(ml_dtypes.bfloat16)
    low = (np.asarray(table, np.float64) - high.astype(np.float64)).astype(ml_dtypes.bfloat16)
    return high, low


def split(x):
    high = x.astype(BF16)
    return high, (x - high.astype(F32)).astype(BF16)


def dot(a, b):
    return lax.dot_general(a, b, (((1,), (0,)), ((), ())), preferred_element_type=F32)


def dot_nt(a, b):
    return lax.dot_general(a, b, (((1,), (1,)), ((), ())), preferred_element_type=F32)


def dot3(ah, al, bh, bl):
    return dot(ah, bh) + (dot(al, bh) + dot(ah, bl))


def taper(p):
    return np.sin(math.pi * (p + 0.5) / SUB)


def class_column(j, c2):
    return j if c2 == 0 else (16 if j == 0 else 32 - j)


def subgrid_tables(visible):
    m = np.arange(32)
    first = np.zeros((2, 4, 32, 2, 4, 2, 8, 2))
    second = np.zeros((8, 4, 2, 8, 2, 8, 2, 2, 32))
    for cg in range(2):
        for j8 in range(8):
            for c2 in range(2):
                phi = 2 * math.pi * ((class_column(cg * 8 + j8, c2) * m) % 32) / 32
                for l4 in range(4):
                    first[0, l4, :, cg, l4, 0, j8, c2] = np.cos(phi) * taper(m)
                    first[1, l4, :, cg, l4, 0, j8, c2] = np.sin(phi) * taper(m)
                    first[0, l4, :, cg, l4, 1, j8, c2] = -np.sin(phi) * taper(m)
                    first[1, l4, :, cg, l4, 1, j8, c2] = np.cos(phi) * taper(m)
    a = np.arange(32)
    scale = visible ** (-0.5) / SUB / G
    for l8 in range(8):
        for l4 in range(4):
            l = 4 * l8 + l4
            phi = 2 * math.pi * ((a * l) % 32) / 32
            weight = taper(l) * scale
            for j8 in range(8):
                for c2 in range(2):
                    second[l8, l4, 0, j8, c2, j8, c2, 0] = np.cos(phi) * weight
                    second[l8, l4, 1, j8, c2, j8, c2, 0] = np.sin(phi) * weight
                    second[l8, l4, 0, j8, c2, j8, c2, 1] = -np.sin(phi) * weight
                    second[l8, l4, 1, j8, c2, j8, c2, 1] = np.cos(phi) * weight
    return first.reshape(256, 256), second.reshape(1024, 1024)


def down_tables():
    r = np.arange(256)[:, None, None, None]
    nt, q4, lo = np.meshgrid(np.arange(2), np.arange(4), np.arange(32), indexing="ij")
    l1 = ((nt * 4 + q4) * 32 + lo)[None]
    phi = 2 * math.pi * ((r * l1) % 256) / 256
    c, s = np.cos(phi), np.sin(phi)
    w = np.zeros((2, 256, 2, 2, 4, 2, 32))
    w[0, :, :, 0, :, 0], w[1, :, :, 0, :, 0] = c, -s
    w[0, :, :, 0, :, 1], w[1, :, :, 0, :, 1] = s, c
    w[0, :, :, 1, :, 0], w[1, :, :, 1, :, 0] = -s, -c
    w[0, :, :, 1, :, 1], w[1, :, :, 1, :, 1] = c, -s
    a = np.arange(32)[None, :, None, None]
    l1 = ((nt * 4 + q4) * 32 + lo)[:, None]
    psi = 2 * math.pi * a * l1 / G
    c, s = np.cos(psi), np.sin(psi)
    t = np.zeros((2, 4, 2, 2, 32, 4, 2, 32))
    for which in range(2):
        t[which, 0, :, 0, :, :, 0], t[which, 1, :, 0, :, :, 0] = c, s
        t[which, 2, :, 0, :, :, 0], t[which, 3, :, 0, :, :, 0] = -s, c
    t[0, 0, :, 0, :, :, 1], t[0, 1, :, 0, :, :, 1] = c, s
    t[0, 2, :, 0, :, :, 1], t[0, 3, :, 0, :, :, 1] = -s, c
    t[0, 0, :, 1, :, :, 0], t[0, 1, :, 1, :, :, 0] = c, s
    t[0, 2, :, 1, :, :, 0], t[0, 3, :, 1, :, :, 0] = s, -c
    t[0, 0, :, 1, :, :, 1], t[0, 1, :, 1, :, :, 1] = -c, -s
    t[0, 2, :, 1, :, :, 1], t[0, 3, :, 1, :, :, 1] = -s, c
    t[1, 0, :, 1, :, :, 1], t[1, 1, :, 1, :, :, 1] = -s, c
    t[1, 2, :, 1, :, :, 1], t[1, 3, :, 1, :, :, 1] = c, s
    phi = 2 * math.pi * ((np.arange(32)[:, None] * np.arange(32)[None, :]) % 32) / 32
    e = np.zeros((32, 2, 2, 32))
    e[:, 0, 0], e[:, 0, 1] = np.cos(phi), np.cos(phi)
    e[:, 1, 0], e[:, 1, 1] = np.sin(phi), -np.sin(phi)
    return w.reshape(512, 1024), t.reshape(16, 64, 256).astype(np.float32), e.reshape(32, 128)


def across_tables():
    p, bc = np.meshgrid(np.arange(16), np.arange(8), indexing="ij")
    m1 = np.arange(256)[None, None, :]
    w = np.zeros((2, 2, 128, 2, 256))
    for s in range(2):
        v1 = (8 * p + bc if s == 0 else 8 * (31 - p) + bc).reshape(128, 1)
        phi = 2 * math.pi * ((v1 * np.arange(256)[None, :]) % 256) / 256
        w[s, 0, :, 0], w[s, 1, :, 0] = np.cos(phi), -np.sin(phi)
        w[s, 0, :, 1], w[s, 1, :, 1] = np.sin(phi), np.cos(phi)
    zero = w[0].copy()
    zero[1, 0, 0] = 1 - 2 * (np.arange(256) % 2)
    zero[1, 0, 1] = 0
    psi = 2 * math.pi * np.arange(17)[:, None] * np.arange(256)[None, :] / G
    twist = np.concatenate([np.cos(psi), np.sin(psi)], axis=1).astype(np.float32)
    return w.reshape(512, 512), zero.reshape(256, 512), twist


def turn(t):
    quarter = jnp.round(t * 4.0)
    x = (t - quarter * 0.25) * (2 * math.pi)
    y = x * x
    sine = x * (1 + y * (-1 / 6 + y * (1 / 120 + y * (-1 / 5040 + y * (1 / 362880)))))
    cosine = 1 + y * (-0.5 + y * (1 / 24 + y * (-1 / 720 + y * (1 / 40320))))
    q = quarter.astype(jnp.int32)
    odd = (q & 1) != 0
    c = jnp.where(odd, sine, cosine)
    s = jnp.where(odd, cosine, sine)
    c = jnp.where(((q + 1) & 2) != 0, -c, c)
    s = jnp.where((q & 2) != 0, -s, s)
    return c, s


def times(x, y):
    return x[0] * y[0] - x[1] * y[1], x[0] * y[1] + x[1] * y[0]


def conj(x):
    return x[0], -x[1]


def grid_kernel(
    uv_ref, vis_ref, beam_ref, seg_ref, tile_ref, row_ref, col_ref, d1h, d1l, d2h, d2l,
    out_ref,
    base_l, base_m, fact_l, fact_m, image, ch, cl, ah, al,
):
    step = pl.program_id(0)
    n = STEP
    zu = turn(uv_ref[:, 0, :] * (1 / 32))
    zv = turn(uv_ref[:, 1, :] * (1 / 32))
    vis = (vis_ref[:, 0, :], vis_ref[:, 1, :])
    u2 = times(zu, zu)
    u3 = times(u2, zu)
    u4 = times(u2, u2)
    u8 = times(u4, u4)
    u12 = times(u8, u4)
    u16 = times(u8, u8)
    for i, f in enumerate((conj(u16), conj(u12), conj(u8), conj(u4), None, u4, u8, u12)):
        b = vis if f is None else times(vis, f)
        base_l[0, pl.ds(i, n, stride=8), :] = b[0]
        base_l[1, pl.ds(i, n, stride=8), :] = b[1]
    for i, f in enumerate((zu, u2, u3)):
        fact_l[2 * i] = f[0]
        fact_l[2 * i + 1] = f[1]
    v2 = times(zv, zv)
    v3 = times(v2, zv)
    v4 = times(v2, v2)
    v5 = times(v4, zv)
    v6 = times(v4, v2)
    v7 = times(v4, v3)
    v8 = times(v4, v4)
    v16 = times(v8, v8)
    one = (jnp.ones_like(zv[0]), jnp.zeros_like(zv[0]))
    for i, f in enumerate((one, zv, v2, v3, v4, v5, v6, v7)):
        base_m[0, pl.ds(i, n, stride=8), :] = f[0]
        base_m[1, pl.ds(i, n, stride=8), :] = f[1]
    for i, f in enumerate((conj(v16), conj(v8), v8)):
        fact_m[2 * i] = f[0]
        fact_m[2 * i + 1] = f[1]

    def one_block(b, _):
        rows = pl.ds(pl.multiple_of(b * 8, 8), 8)
        line = pl.ds(b, 1)
        bl = (base_l[0, rows, :], base_l[1, rows, :])
        bm = (base_m[0, rows, :], base_m[1, rows, :])
        real, imag = [], []
        for t in range(4):
            w = bl if t == 0 else times(bl, (fact_l[2 * t - 2, line, :], fact_l[2 * t - 1, line, :]))
            real.append(w[0])
            imag.append(w[1])
        rh, rl = split(jnp.concatenate(real, axis=0))
        ih, il = split(jnp.concatenate(imag, axis=0))
        lh = jnp.concatenate([rh, ih], axis=1)
        ll = jnp.concatenate([rl, il], axis=1)
        cosine, sine = [], []
        for t in range(4):
            i = {0: 0, 1: 1, 3: 2}.get(t)
            w = bm if i is None else times(bm, (fact_m[2 * i, line, :], fact_m[2 * i + 1, line, :]))
            cosine.append(w[0])
            sine.append(w[1])
        cosh, cosl = split(jnp.concatenate(cosine, axis=0))
        sinh, sinl = split(jnp.concatenate(sine, axis=0))
        mh = jnp.concatenate(
            [jnp.concatenate([cosh, sinh], axis=0), jnp.concatenate([-sinh, cosh], axis=0)], axis=1)
        ml = jnp.concatenate(
            [jnp.concatenate([cosl, sinl], axis=0), jnp.concatenate([-sinl, cosl], axis=0)], axis=1)
        o = dot_nt(jnp.concatenate([lh, ll], axis=0), mh)
        o = o[:32] + (o[32:] + dot_nt(lh, ml))
        for ri in range(2):
            lanes = slice(ri * 32, ri * 32 + 32)
            image[ri, rows, :] = jnp.concatenate([o[8 * t:8 * t + 8, lanes] for t in range(4)], axis=1)
        return 0

    lax.fori_loop(0, n, one_block, 0, unroll=n)

    here = pl.ds(pl.multiple_of(step * n, n), n)
    for l8 in range(8):
        im = (image[0, pl.ds(l8, n, stride=8), :], image[1, pl.ds(l8, n, stride=8), :])
        bm = (beam_ref[0, :, l8 * 128:(l8 + 1) * 128], beam_ref[1, :, l8 * 128:(l8 + 1) * 128])
        c = times(bm, im)
        for ri in range(2):
            h, l = split(c[ri])
            ch[here, (2 * l8 + ri) * 128:(2 * l8 + ri + 1) * 128] = h
            cl[here, (2 * l8 + ri) * 128:(2 * l8 + ri + 1) * 128] = l

    @pl.when(step == pl.num_programs(0) - 1)
    def _():
        subs = tile_ref.shape[0]
        tall = subs + 8
        down_it = jnp.broadcast_to(tile_ref[...].astype(F32), (subs, subs))
        along = down_it.T
        ids = [lax.broadcasted_iota(jnp.int32, (subs, subs), d) for d in range(2)]
        earlier = (down_it == along) & (ids[0] < ids[1])
        rank = jnp.sum(earlier.astype(F32), axis=0, keepdims=True).astype(jnp.int32)
        tile = along[:1].astype(jnp.int32)
        band = tile % 32
        side = (band >= 16).astype(jnp.int32)
        pair = jnp.where(side == 1, 31 - band, band)
        slot = pair * 32 + side * 16 + (tile // 32) * 2 + rank
        code = (slot * 256 + col_ref[...] * 32 + row_ref[...]).astype(F32)
        for j in range(CLASSES):
            out_ref[j * tall + subs:(j + 1) * tall, :] = jnp.broadcast_to(code, (8, subs))
        blocks = seg_ref.shape[1]
        pick = (seg_ref[...] == lax.broadcasted_iota(jnp.int32, (subs, blocks), 0)).astype(F32).astype(BF16)
        for l8 in range(8):
            lanes = slice(l8 * 256, (l8 + 1) * 256)
            ih, il = split(dot(pick, ch[:, lanes]) + dot(pick, cl[:, lanes]))
            a = dot3(ih, il, d1h[...], d1l[...])
            for cg in range(2):
                h, l = split(a[:, cg * 128:(cg + 1) * 128])
                ah[cg * subs:(cg + 1) * subs, l8 * 128:(l8 + 1) * 128] = h
                al[cg * subs:(cg + 1) * subs, l8 * 128:(l8 + 1) * 128] = l
        for tile in range(4):
            lanes = slice(tile * 256, (tile + 1) * 256)
            spec = dot3(ah[...], al[...], d2h[:, lanes], d2l[:, lanes])
            for cg in range(2):
                for k in range(2):
                    j = cg * 8 + tile * 2 + k
                    out_ref[j * tall:j * tall + subs, :] = spec[cg * subs:(cg + 1) * subs, k * 128:(k + 1) * 128]


def make_payload(uv, vis, beam, seg, tile, row, col, tables):
    blocks, _, visible = uv.shape
    subs = tile.shape[0]
    tall = subs + 8
    (d1h, d1l), (d2h, d2l) = [halves(t) for t in tables]
    whole = lambda shape: pl.BlockSpec(shape, lambda i: (0,) * len(shape))
    return pl.pallas_call(
        grid_kernel,
        grid=(blocks // STEP,),
        in_specs=[
            pl.BlockSpec((STEP, 2, visible), lambda i: (i, 0, 0)),
            pl.BlockSpec((STEP, 2, visible), lambda i: (i, 0, 0)),
            pl.BlockSpec((2, STEP, SUB * SUB), lambda i: (0, i, 0)),
            whole((1, blocks)), whole((subs, 1)), whole((1, subs)), whole((1, subs)),
            whole((256, 256)), whole((256, 256)), whole((1024, 1024)), whole((1024, 1024)),
        ],
        out_specs=whole((CLASSES * tall, 128)),
        out_shape=jax.ShapeDtypeStruct((CLASSES * tall, 128), F32),
        scratch_shapes=[
            pltpu.VMEM((2, STEP * 8, 128), F32),
            pltpu.VMEM((2, STEP * 8, 128), F32),
            pltpu.VMEM((6, STEP, 128), F32),
            pltpu.VMEM((6, STEP, 128), F32),
            pltpu.VMEM((2, STEP * 8, 128), F32),
            pltpu.VMEM((blocks, 2048), BF16),
            pltpu.VMEM((blocks, 2048), BF16),
            pltpu.VMEM((2 * subs, 1024), BF16),
            pltpu.VMEM((2 * subs, 1024), BF16),
        ],
        compiler_params=pltpu.CompilerParams(vmem_limit_bytes=48 * MB),
        name="gridding",
    )(uv, vis, beam, seg, tile, row, col, d1h, d1l, d2h, d2l)


MESH = pl.DeviceIdType.MESH


NEAR = [(0, 0), (0, 1), (1, 0), (-1, 0), (1, 1), (-1, 1), (2, 0), (-2, 0),
        (2, 1), (-2, 1), (3, 0), (-3, 0), (3, 1), (-3, 1), (4, 0), (4, 1)]
FAR = [(0, 1), (1, 0), (0, -1), (-1, 0), (0, 2), (2, 0), (1, 1), (-1, -1),
       (-1, 1), (1, -1), (2, 2), (1, 2), (2, 1), (-1, 2), (2, -1)]


def exchange_kernel(
    src_ref, wh_hbm, wl_hbm, t_hbm, eh, el, out_ref,
    near, box, held, grid_ref, x_ref, edge_src, edge_in, wh, wl, t_ref, lh, ll, kbuf, near2,
    near_send, near_recv, far_send, far_recv, edge_send, edge_recv, table_sem,
    near2_send, near2_recv, far2_send, far2_recv,
):
    y, core, z, x = [lax.axis_index(a) for a in ("y", "core", "z", "x")]
    group, kind = y * 4 + x, z * 2 + core
    tall = src_ref.shape[0] // CLASSES
    subs = tall - 8

    tables = [
        pltpu.make_async_copy(a, b, table_sem.at[n])
        for n, (a, b) in enumerate(((wh_hbm, wh), (wl_hbm, wl), (t_hbm, t_ref)))
    ]
    for c in tables:
        c.start()

    def loop(lo, hi, f):
        def step(k, _):
            f(k)
            return 0

        lax.fori_loop(lo, hi, step, 0)

    def to_near(k):
        dz, dc = NEAR[k]
        return (z + dz + 8) % 8, (core + dc) % 2

    def to_far(k):
        dy, dx = FAR[k]
        return (y + dy + 4) % 4, (x + dx + 4) % 4

    barrier = pltpu.get_barrier_semaphore()
    for k in range(1, 16):
        tz, tc = to_near(k)
        pl.semaphore_signal(barrier, inc=1, device_id=(y, tc, tz, x), device_id_type=MESH)
    for k in range(15):
        ty, tx = to_far(k)
        pl.semaphore_signal(barrier, inc=1, device_id=(ty, core, z, tx), device_id_type=MESH)
    pl.semaphore_wait(barrier, 30)

    def near_copy(k):
        tz, tc = to_near(k)
        return pltpu.make_async_remote_copy(
            src_ref=src_ref.at[pl.ds(pl.multiple_of((tz * 2 + tc) * tall, 8), tall), :],
            dst_ref=near.at[k],
            send_sem=near_send.at[k],
            recv_sem=near_recv.at[k],
            device_id=(y, tc, tz, x),
            device_id_type=MESH,
        )

    def far_copy(g, k):
        ty, tx = to_far(k)
        h, rows = g // 2, pl.ds((g % 2) * 128, 128 + 8 * (g % 2))
        return pltpu.make_async_remote_copy(
            src_ref=box.at[h, ty * 4 + tx, rows, :],
            dst_ref=held.at[h, k, rows, :],
            send_sem=far_send.at[g, k],
            recv_sem=far_recv.at[g, k],
            device_id=(ty, core, z, tx),
            device_id_type=MESH,
        )

    for k in range(1, 16):
        near_copy(k).start()
    near[0] = src_ref[pl.ds(pl.multiple_of(kind * tall, 8), tall), :]

    slots = lax.broadcasted_iota(jnp.int32, (512, subs), 0)
    line = lax.broadcasted_iota(jnp.int32, (8, subs), 0)
    codes = jnp.zeros((8, subs), F32)
    for g in range(4):
        h = g // 2
        for i in range(4):
            k8 = (g % 2) * 4 + i
            k = h * 8 + k8
            if k:
                near_copy(k).wait_recv()
            code = near[k, subs:subs + 1, :]
            fits = (code.astype(jnp.int32) // 256 == slots).astype(F32).astype(BF16)
            hi, lo = split(near[k, :subs, :])
            o = dot(jnp.concatenate([fits, fits], axis=1), jnp.concatenate([hi, lo], axis=0))
            for p in range(PAIRS):
                box[h, p, k8 * 32:k8 * 32 + 32, :] = o[p * 32:(p + 1) * 32]
            codes = jnp.where(line == k8, code, codes)
        if g % 2 == 1:
            for p in range(PAIRS):
                box[h, p, 256:264, :] = codes
        for k in range(15):
            far_copy(g, k).start()
        if g % 2 == 1:
            held[h, 15] = box[h, group]

    pos = lax.broadcasted_iota(jnp.int32, (256, 256), 0).astype(F32)
    for h in range(2):
        for g in (2 * h, 2 * h + 1):
            for k in range(15):
                far_copy(g, k).wait_recv()
        code = jnp.concatenate([held[h, k, 256:264, :] for k in range(16)], axis=0).T.astype(jnp.int32)
        at = code // 256 - group * 32
        value = (code % 256 + 1).astype(F32)

        def put(i):
            hot, data = [], []
            for rank in range(2):
                slot = i * 2 + rank
                label = jnp.sum(jnp.where(at == slot, value, 0.0), axis=0, keepdims=True) - 1.0
                hot.append(label)
                data += [held[h, k, pl.ds(slot, 8, stride=32), :] for k in range(16)]
            fits = (jnp.concatenate(hot, axis=1) == pos).astype(F32).astype(BF16)
            hi, lo = split(jnp.concatenate(data, axis=0))
            v = dot(fits, jnp.concatenate([hi, lo], axis=1))
            v = v[:, :128] + v[:, 128:]
            rows = pl.ds(pl.multiple_of(i % 8 * 32, 32), 32)
            for bc in range(8):
                where = i // 8 * 8 + bc
                add = v[bc * 32:(bc + 1) * 32]
                grid_ref[where, rows, :] = add if h == 0 else grid_ref[where, rows, :] + add

        def flip(i):
            x_ref[pl.ds(pl.multiple_of(i * 128, 128), 128), :] = grid_ref[i].T

        if h == 0:
            loop(0, 16, put)
        else:
            loop(8, 16, put)
            edge_src[...] = grid_ref[8].T[:64]
            tx, ty = (x + 1) % 4, (y + (x + 1) // 4) % 4
            edge = pltpu.make_async_remote_copy(
                src_ref=edge_src, dst_ref=edge_in, send_sem=edge_send, recv_sem=edge_recv,
                device_id=(ty, core, z, tx), device_id_type=MESH,
            )
            edge.start()
            loop(8, 16, flip)
            loop(0, 8, put)
            loop(0, 8, flip)

    edge.wait_recv()
    zero_class = kind == 0
    special = jnp.where((kind == 0) & (group == 0), 1, 0)
    near_x = lambda s, bc: x_ref[s * 1024 + bc * 128:s * 1024 + bc * 128 + 64, :]
    far_x = lambda s, bc: x_ref[s * 1024 + bc * 128 + 64:s * 1024 + bc * 128 + 128, :]
    for bc in range(8):
        for s in range(2):
            if s == 0:
                own = near_x(0, bc)
                first = edge_in[...] if bc == 0 else near_x(1, 8 - bc)
                mirror = jnp.where(zero_class, first, far_x(1, 7 - bc))
            else:
                own = jnp.where(zero_class, far_x(0, bc), near_x(1, bc))
                mirror = jnp.where(zero_class, far_x(1, 7 - bc), far_x(0, 7 - bc))
            for c2, v in enumerate((own, mirror)):
                hi, lo = split(v)
                row = (bc * 2 + s) * 64 + c2 * 32
                for ri in range(2):
                    lh[row:row + 32, ri * 256:(ri + 1) * 256] = hi[ri * 32:(ri + 1) * 32]
                    ll[row:row + 32, ri * 256:(ri + 1) * 256] = lo[ri * 32:(ri + 1) * 32]
    for c in tables:
        c.wait()
    e2 = jnp.concatenate([eh[...], eh[...]], axis=1)
    low = lax.broadcasted_iota(jnp.int32, (32, 128), 1) < 64

    def near2_copy(nt, t, dc):
        zh, tc = (z // 2 + t) % 4, (core + dc) % 2
        tz = zh * 2 + nt
        return (tz * 2 + tc) != kind, pltpu.make_async_remote_copy(
            src_ref=kbuf.at[pl.ds(pl.multiple_of((nt * 8 + tc * 4 + zh) * 128, 128), 128), :],
            dst_ref=near2.at[kind],
            send_sem=near2_send.at[nt, t, dc],
            recv_sem=near2_recv.at[kind],
            device_id=(y, tc, tz, x),
            device_id_type=MESH,
        )

    for nt in range(2):
        cols = slice(nt * 512, (nt + 1) * 512)

        def one(i):
            rows = pl.ds(pl.multiple_of(i * 256, 256), 256)
            v = dot3(lh[rows, :], ll[rows, :], wh[:, cols], wl[:, cols])
            for k in range(2):
                bc = i * 2 + k
                parts = []
                for s in range(2):
                    r = (k * 2 + s) * 64
                    ya, yb = v[r:r + 64, :256], v[r:r + 64, 256:]
                    which = 0
                    if s == 0 and k == 0:
                        which = jnp.where(i == 0, special, 0)
                    tab = lambda n: t_ref[which * 8 + n * 2 + nt]
                    parts.append(jnp.concatenate(
                        [ya * tab(0) + yb * tab(1), ya * tab(2) + yb * tab(3)], axis=0))
                th, tl = split(jnp.concatenate(parts, axis=1))
                o = dot(e2, jnp.concatenate([th, tl], axis=0)) + dot(el[...], th)
                for g in range(2):
                    o0 = o[:, g * 128:(g + 1) * 128]
                    o1 = o[:, 256 + g * 128:256 + (g + 1) * 128]
                    pair = (jnp.where(low, o0, pltpu.roll(o1, 64, 1)), jnp.where(low, pltpu.roll(o0, 64, 1), o1))
                    for e in range(2):
                        for ty in range(4):
                            first = nt * 1024 + ty * 32 + (g * 2 + e) * 8 + bc
                            kbuf[pl.ds(first, 8, stride=128), :] = pair[e][ty * 8:(ty + 1) * 8]

        loop(0, 4, one)
        for t in (0, 1, 3, 2):
            for dc in range(2):
                other, copy = near2_copy(nt, t, dc)

                @pl.when(other)
                def _():
                    copy.start()

    mine = (z % 2) * 8 + core * 4 + z // 2
    near2[kind] = kbuf[pl.ds(pl.multiple_of(mine * 128, 128), 128), :]

    def far2_copy(t, k):
        ty, tx = to_far(k)
        kinds = pl.ds(((z // 2 - t + 4) % 4) * 4, 4)
        return pltpu.make_async_remote_copy(
            src_ref=near2.at[kinds, pl.ds(pl.multiple_of((ty * 4 + tx) * 8, 8), 8), :],
            dst_ref=out_ref.at[kinds, pl.ds(pl.multiple_of(group * 8, 8), 8), :],
            send_sem=far2_send.at[t, k],
            recv_sem=far2_recv.at[t, k],
            device_id=(ty, core, z, tx),
            device_id_type=MESH,
        )

    for t in (0, 1, 3, 2):
        base = ((z // 2 - t + 4) % 4) * 4
        for i in range(4):
            sender = base + i

            @pl.when(sender != kind)
            def _():
                pltpu.make_async_remote_copy(
                    src_ref=kbuf.at[pl.ds(0, 128), :], dst_ref=near2.at[sender],
                    send_sem=near2_send.at[0, 0, 0], recv_sem=near2_recv.at[sender],
                    device_id=(y, 1 - core, z, x), device_id_type=MESH,
                ).wait_recv()

        for k in range(15):
            far2_copy(t, k).start()
        own = pl.ds(pl.multiple_of(group * 8, 8), 8)
        out_ref[pl.ds(base, 4), own, :] = near2[pl.ds(base, 4), own, :]

    for t in range(4):
        for k in range(15):
            far2_copy(t, k).wait_recv()
    edge.wait_send()
    for k in range(1, 16):
        near_copy(k).wait_send()
    for g in range(4):
        for k in range(15):
            far_copy(g, k).wait_send()
    for nt in range(2):
        for t in range(4):
            for dc in range(2):
                other, copy = near2_copy(nt, t, dc)

                @pl.when(other)
                def _():
                    copy.wait_send()
    for t in range(4):
        for k in range(15):
            far2_copy(t, k).wait_send()


def exchange(payload):
    tall = payload.shape[0] // CLASSES
    w, t, e = down_tables()
    wh, wl = halves(w)
    eh, el = halves(e)
    vmem = pl.BlockSpec(memory_space=pltpu.VMEM)
    hbm = pl.BlockSpec(memory_space=pl.ANY)
    dma = pltpu.SemaphoreType.DMA
    return pl.pallas_call(
        exchange_kernel,
        in_specs=[vmem, hbm, hbm, hbm, vmem, vmem],
        out_specs=vmem,
        out_shape=jax.ShapeDtypeStruct((16, 128, 128), F32),
        scratch_shapes=[
            pltpu.VMEM((16, tall, 128), F32),
            pltpu.VMEM((2, 16, 264, 128), F32),
            pltpu.VMEM((2, 16, 264, 128), F32),
            pltpu.VMEM((16, 256, 128), F32),
            pltpu.VMEM((2048, 256), F32),
            pltpu.VMEM((64, 256), F32),
            pltpu.VMEM((64, 256), F32),
            pltpu.VMEM((512, 1024), BF16),
            pltpu.VMEM((512, 1024), BF16),
            pltpu.VMEM((16, 64, 256), F32),
            pltpu.VMEM((1024, 512), BF16),
            pltpu.VMEM((1024, 512), BF16),
            pltpu.VMEM((2048, 128), F32),
            pltpu.VMEM((16, 128, 128), F32),
            dma((16,)), dma((16,)), dma((4, 16)), dma((4, 16)), dma(()), dma(()), dma((3,)),
            dma((2, 4, 2)), dma((16,)), dma((4, 16)), dma((4, 16)),
        ],
        compiler_params=pltpu.CompilerParams(
            collective_id=0, has_side_effects=True, vmem_limit_bytes=48 * MB
        ),
        name="exchange",
    )(payload, wh, wl, t, eh, el)


def across_kernel(k_ref, wh, wl, zh, zl, twist, out_ref, lh, ll, y_ref):
    for j in range(16):
        a = k_ref[j * 128:(j + 1) * 128, :].T
        h, l = split(a)
        for i in range(4):
            lh[j * 32:(j + 1) * 32, i * 128:(i + 1) * 128] = h[i * 32:(i + 1) * 32]
            ll[j * 32:(j + 1) * 32, i * 128:(i + 1) * 128] = l[i * 32:(i + 1) * 32]
    y_ref[0:32] = dot3(lh[0:32, :256], ll[0:32, :256], zh[...], zl[...])
    y_ref[512:544] = dot3(lh[0:32, 256:], ll[0:32, 256:], wh[:256, :], wl[:256, :])
    y_ref[32:512] = dot3(lh[32:512, :], ll[32:512, :], wh[...], wl[...])

    cos = [math.cos(2 * math.pi * i / 32) for i in range(32)]
    sin = [math.sin(2 * math.pi * i / 32) for i in range(32)]

    def combine(terms):
        total = None
        for f, x in terms:
            if abs(f) < 1e-12:
                continue
            v = x if f == 1.0 else -x if f == -1.0 else x * f
            total = v if total is None else total + v
        return total

    def rows(i, _):
        at = pl.multiple_of(i * 8, 8)
        for half in range(2):
            lane = slice(half * 128, (half + 1) * 128)
            tre, tim = [], []
            for v in range(17):
                yre = y_ref[pl.ds(v * 32 + at, 8), lane]
                yim = y_ref[pl.ds(v * 32 + at, 8), 256 + half * 128:256 + (half + 1) * 128]
                c = twist[v:v + 1, lane]
                s = twist[v:v + 1, 256 + half * 128:256 + (half + 1) * 128]
                tre.append(yre * c - yim * s)
                tim.append(yre * s + yim * c)
            for m2 in range(9):
                e0 = combine([(cos[v * m2 % 32], tre[v]) for v in range(0, 17, 2)])
                e1 = combine([(cos[v * m2 % 32], tre[v]) for v in range(1, 17, 2)])
                o0 = combine([(sin[v * m2 % 32], tim[v]) for v in range(0, 17, 2)])
                o1 = combine([(sin[v * m2 % 32], tim[v]) for v in range(1, 17, 2)])
                zero = jnp.zeros((8, 128), F32)
                e0, e1, o0, o1 = [zero if x is None else x for x in (e0, e1, o0, o1)]
                puts = {m2: (e0 + e1) - (o0 + o1), (32 - m2) % 32: (e0 + e1) + (o0 + o1)}
                puts[16 - m2] = (e0 - e1) + (o0 - o1)
                puts[16 + m2] = (e0 - e1) - (o0 - o1)
                for m, v in puts.items():
                    out_ref[pl.ds(at, 8), m * 256 + half * 128:m * 256 + (half + 1) * 128] = v
        return 0

    lax.fori_loop(0, 4, rows, 0)


def across(k):
    w, zero, twist = across_tables()
    wh, wl = halves(w)
    zh, zl = halves(zero)
    return pl.pallas_call(
        across_kernel,
        out_shape=jax.ShapeDtypeStruct((32, G), F32),
        scratch_shapes=[
            pltpu.VMEM((512, 512), BF16), pltpu.VMEM((512, 512), BF16), pltpu.VMEM((544, 512), F32),
        ],
        compiler_params=pltpu.CompilerParams(vmem_limit_bytes=32 * MB),
        name="across",
    )(k, wh, wl, zh, zl, twist)


def body(uv, vis, left, right, block_subgrid, subgrid_tile, block_row, block_col):
    visible = uv.shape[2]

    l, r = left.astype(F32), right.astype(F32)
    beam = jnp.stack([
        l[:, 0] * r[:, 0] + l[:, 1] * r[:, 1],
        l[:, 1] * r[:, 0] - l[:, 0] * r[:, 1],
    ])
    payload = make_payload(
        uv, vis, beam, block_subgrid, subgrid_tile, block_row[None], block_col[None], subgrid_tables(visible)
    )
    return across(exchange(payload).reshape(2048, 128))


def solution(mesh):
    names = ("y", "core", "z", "x")
    axes = Mesh(mesh.devices.reshape(4, 2, 8, 4), names)
    placed = (
        P(names, None, None),
        P(names, None, None),
        P(names, None, None),
        P(names, None, None),
        P(names, None),
        P(names, None),
        P(names),
        P(names),
    )
    return jax.shard_map(body, mesh=axes, in_specs=placed, out_specs=P(names, None), check_vma=False)
```

```python
import math
from functools import partial

import jax
import jax.numpy as jnp
import ml_dtypes
import numpy as np
from jax import lax
from jax.experimental import pallas as pl
from jax.experimental.pallas import tpu as pltpu
from jax.sharding import Mesh, PartitionSpec as P

G = 8192
SUB = 32
PAIRS = 16
CLASSES = 16
STEP = 32
F32 = jnp.float32
BF16 = jnp.bfloat16
MB = 1 << 20


def halves(table):
    high = np.asarray(table, np.float32).astype(ml_dtypes.bfloat16)
    low = (np.asarray(table, np.float64) - high.astype(np.float64)).astype(ml_dtypes.bfloat16)
    return high, low


def split(x):
    high = x.astype(BF16)
    return high, (x - high.astype(F32)).astype(BF16)


def dot(a, b):
    return lax.dot_general(a, b, (((1,), (0,)), ((), ())), preferred_element_type=F32)


def dot_nt(a, b):
    return lax.dot_general(a, b, (((1,), (1,)), ((), ())), preferred_element_type=F32)


def dot3(ah, al, bh, bl):
    return dot(ah, bh) + (dot(al, bh) + dot(ah, bl))


def taper(p):
    return np.sin(math.pi * (p + 0.5) / SUB)


def class_column(j, c2):
    return j if c2 == 0 else (16 if j == 0 else 32 - j)


def subgrid_tables(visible):
    m = np.arange(32)
    first = np.zeros((2, 4, 32, 2, 4, 2, 8, 2))
    second = np.zeros((8, 4, 2, 8, 2, 8, 2, 2, 32))
    for cg in range(2):
        for j8 in range(8):
            for c2 in range(2):
                phi = 2 * math.pi * ((class_column(cg * 8 + j8, c2) * m) % 32) / 32
                for l4 in range(4):
                    first[0, l4, :, cg, l4, 0, j8, c2] = np.cos(phi) * taper(m)
                    first[1, l4, :, cg, l4, 0, j8, c2] = np.sin(phi) * taper(m)
                    first[0, l4, :, cg, l4, 1, j8, c2] = -np.sin(phi) * taper(m)
                    first[1, l4, :, cg, l4, 1, j8, c2] = np.cos(phi) * taper(m)
    a = np.arange(32)
    scale = visible ** (-0.5) / SUB / G
    for l8 in range(8):
        for l4 in range(4):
            l = 4 * l8 + l4
            phi = 2 * math.pi * ((a * l) % 32) / 32
            weight = taper(l) * scale
            for j8 in range(8):
                for c2 in range(2):
                    second[l8, l4, 0, j8, c2, j8, c2, 0] = np.cos(phi) * weight
                    second[l8, l4, 1, j8, c2, j8, c2, 0] = np.sin(phi) * weight
                    second[l8, l4, 0, j8, c2, j8, c2, 1] = -np.sin(phi) * weight
                    second[l8, l4, 1, j8, c2, j8, c2, 1] = np.cos(phi) * weight
    return first.reshape(256, 256), second.reshape(1024, 1024)


def down_tables():
    r = np.arange(256)[:, None, None, None]
    nt, q4, lo = np.meshgrid(np.arange(2), np.arange(4), np.arange(32), indexing="ij")
    l1 = ((nt * 4 + q4) * 32 + lo)[None]
    phi = 2 * math.pi * ((r * l1) % 256) / 256
    c, s = np.cos(phi), np.sin(phi)
    w = np.zeros((2, 256, 2, 2, 4, 2, 32))
    w[0, :, :, 0, :, 0], w[1, :, :, 0, :, 0] = c, -s
    w[0, :, :, 0, :, 1], w[1, :, :, 0, :, 1] = s, c
    w[0, :, :, 1, :, 0], w[1, :, :, 1, :, 0] = -s, -c
    w[0, :, :, 1, :, 1], w[1, :, :, 1, :, 1] = c, -s
    a = np.arange(32)[None, :, None, None]
    l1 = ((nt * 4 + q4) * 32 + lo)[:, None]
    psi = 2 * math.pi * a * l1 / G
    c, s = np.cos(psi), np.sin(psi)
    t = np.zeros((2, 4, 2, 2, 32, 4, 2, 32))
    for which in range(2):
        t[which, 0, :, 0, :, :, 0], t[which, 1, :, 0, :, :, 0] = c, s
        t[which, 2, :, 0, :, :, 0], t[which, 3, :, 0, :, :, 0] = -s, c
    t[0, 0, :, 0, :, :, 1], t[0, 1, :, 0, :, :, 1] = c, s
    t[0, 2, :, 0, :, :, 1], t[0, 3, :, 0, :, :, 1] = -s, c
    t[0, 0, :, 1, :, :, 0], t[0, 1, :, 1, :, :, 0] = c, s
    t[0, 2, :, 1, :, :, 0], t[0, 3, :, 1, :, :, 0] = s, -c
    t[0, 0, :, 1, :, :, 1], t[0, 1, :, 1, :, :, 1] = -c, -s
    t[0, 2, :, 1, :, :, 1], t[0, 3, :, 1, :, :, 1] = -s, c
    t[1, 0, :, 1, :, :, 1], t[1, 1, :, 1, :, :, 1] = -s, c
    t[1, 2, :, 1, :, :, 1], t[1, 3, :, 1, :, :, 1] = c, s
    phi = 2 * math.pi * ((np.arange(32)[:, None] * np.arange(32)[None, :]) % 32) / 32
    e = np.zeros((32, 2, 2, 32))
    e[:, 0, 0], e[:, 0, 1] = np.cos(phi), np.cos(phi)
    e[:, 1, 0], e[:, 1, 1] = np.sin(phi), -np.sin(phi)
    return w.reshape(512, 1024), t.reshape(16, 64, 256).astype(np.float32), e.reshape(32, 128)


def across_tables():
    w = np.zeros((3, 2, 2, 2, 4, 16, 2, 256))
    m1 = np.arange(256)
    bc2, p = np.meshgrid(np.arange(4), np.arange(16), indexing="ij")
    for bcl in range(2):
        bc = bc2 * 2 + bcl
        for kind, s, v1 in ((0, 0, 8 * p + bc), (0, 1, 8 * (31 - p) + bc), (1, 0, 8 * p + bc), (2, 1, 8 * p + bc)):
            phi = 2 * math.pi * ((v1[:, :, None] * m1) % 256) / 256
            w[kind, bcl, 0, s, :, :, 0], w[kind, bcl, 1, s, :, :, 0] = np.cos(phi), -np.sin(phi)
            w[kind, bcl, 0, s, :, :, 1], w[kind, bcl, 1, s, :, :, 1] = np.sin(phi), np.cos(phi)
    w[1, 0, 1, 0, 0, 0, 0] = 1 - 2 * (m1 % 2)
    w[1, 0, 1, 0, 0, 0, 1] = 0
    w = w.reshape(3, 512, 512)
    psi = 2 * math.pi * np.arange(17)[:, None] * np.arange(256)[None, :] / G
    twist = np.concatenate([np.cos(psi), np.sin(psi)], axis=1).astype(np.float32)
    return w[0], np.concatenate([w[1], w[2]], axis=1), twist


def turn(t):
    quarter = jnp.round(t * 4.0)
    x = (t - quarter * 0.25) * (2 * math.pi)
    y = x * x
    sine = x * (1 + y * (-1 / 6 + y * (1 / 120 + y * (-1 / 5040 + y * (1 / 362880)))))
    cosine = 1 + y * (-0.5 + y * (1 / 24 + y * (-1 / 720 + y * (1 / 40320))))
    q = quarter.astype(jnp.int32)
    odd = (q & 1) != 0
    c = jnp.where(odd, sine, cosine)
    s = jnp.where(odd, cosine, sine)
    c = jnp.where(((q + 1) & 2) != 0, -c, c)
    s = jnp.where((q & 2) != 0, -s, s)
    return c, s


def times(x, y):
    return x[0] * y[0] - x[1] * y[1], x[0] * y[1] + x[1] * y[0]


def conj(x):
    return x[0], -x[1]


def grid_kernel(
    uv_ref, vis_ref, beam_ref, seg_ref, tile_ref, row_ref, col_ref, d1h, d1l, d2h_hbm, d2l_hbm,
    out_ref,
    base_l, base_m, fact_l, fact_m, image, ch, cl, ah, al, d2h, d2l, table_sem,
):
    step = pl.program_id(0)
    n = STEP
    tables = [
        pltpu.make_async_copy(a, b, table_sem.at[i]) for i, (a, b) in enumerate(((d2h_hbm, d2h), (d2l_hbm, d2l)))
    ]

    @pl.when(step == 0)
    def _():
        for c in tables:
            c.start()

    zu = turn(uv_ref[:, 0, :] * (1 / 32))
    zv = turn(uv_ref[:, 1, :] * (1 / 32))
    vis = (vis_ref[:, 0, :], vis_ref[:, 1, :])
    u2 = times(zu, zu)
    u3 = times(u2, zu)
    u4 = times(u2, u2)
    u8 = times(u4, u4)
    u12 = times(u8, u4)
    u16 = times(u8, u8)
    for i, f in enumerate((conj(u16), conj(u12), conj(u8), conj(u4), None, u4, u8, u12)):
        b = vis if f is None else times(vis, f)
        base_l[0, pl.ds(i, n, stride=8), :] = b[0]
        base_l[1, pl.ds(i, n, stride=8), :] = b[1]
    for i, f in enumerate((zu, u2, u3)):
        fact_l[2 * i] = f[0]
        fact_l[2 * i + 1] = f[1]
    v2 = times(zv, zv)
    v3 = times(v2, zv)
    v4 = times(v2, v2)
    v5 = times(v4, zv)
    v6 = times(v4, v2)
    v7 = times(v4, v3)
    v8 = times(v4, v4)
    v16 = times(v8, v8)
    one = (jnp.ones_like(zv[0]), jnp.zeros_like(zv[0]))
    for i, f in enumerate((one, zv, v2, v3, v4, v5, v6, v7)):
        base_m[0, pl.ds(i, n, stride=8), :] = f[0]
        base_m[1, pl.ds(i, n, stride=8), :] = f[1]
    for i, f in enumerate((conj(v16), conj(v8), v8)):
        fact_m[2 * i] = f[0]
        fact_m[2 * i + 1] = f[1]

    def one_block(b, _):
        rows = pl.ds(pl.multiple_of(b * 8, 8), 8)
        line = pl.ds(b, 1)
        bl = (base_l[0, rows, :], base_l[1, rows, :])
        bm = (base_m[0, rows, :], base_m[1, rows, :])
        real, imag = [], []
        for t in range(4):
            w = bl if t == 0 else times(bl, (fact_l[2 * t - 2, line, :], fact_l[2 * t - 1, line, :]))
            real.append(w[0])
            imag.append(w[1])
        rh, rl = split(jnp.concatenate(real, axis=0))
        ih, il = split(jnp.concatenate(imag, axis=0))
        lh = jnp.concatenate([rh, ih], axis=1)
        ll = jnp.concatenate([rl, il], axis=1)
        cosine, sine = [], []
        for t in range(4):
            i = {0: 0, 1: 1, 3: 2}.get(t)
            w = bm if i is None else times(bm, (fact_m[2 * i, line, :], fact_m[2 * i + 1, line, :]))
            cosine.append(w[0])
            sine.append(w[1])
        cosh, cosl = split(jnp.concatenate(cosine, axis=0))
        sinh, sinl = split(jnp.concatenate(sine, axis=0))
        mh = jnp.concatenate(
            [jnp.concatenate([cosh, sinh], axis=0), jnp.concatenate([-sinh, cosh], axis=0)], axis=1)
        ml = jnp.concatenate(
            [jnp.concatenate([cosl, sinl], axis=0), jnp.concatenate([-sinl, cosl], axis=0)], axis=1)
        o = dot_nt(jnp.concatenate([lh, ll], axis=0), mh)
        o = o[:32] + (o[32:] + dot_nt(lh, ml))
        for ri in range(2):
            lanes = slice(ri * 32, ri * 32 + 32)
            image[ri, rows, :] = jnp.concatenate([o[8 * t:8 * t + 8, lanes] for t in range(4)], axis=1)
        return 0

    lax.fori_loop(0, n, one_block, 0, unroll=n)

    here = pl.ds(pl.multiple_of(step * n, n), n)
    for l8 in range(8):
        im = (image[0, pl.ds(l8, n, stride=8), :], image[1, pl.ds(l8, n, stride=8), :])
        bm = (beam_ref[0, :, l8 * 128:(l8 + 1) * 128], beam_ref[1, :, l8 * 128:(l8 + 1) * 128])
        c = times(bm, im)
        for ri in range(2):
            h, l = split(c[ri])
            ch[here, (2 * l8 + ri) * 128:(2 * l8 + ri + 1) * 128] = h
            cl[here, (2 * l8 + ri) * 128:(2 * l8 + ri + 1) * 128] = l

    @pl.when(step == pl.num_programs(0) - 1)
    def _():
        subs = tile_ref.shape[0]
        tall = subs + 8
        down_it = jnp.broadcast_to(tile_ref[...].astype(F32), (subs, subs))
        along = down_it.T
        ids = [lax.broadcasted_iota(jnp.int32, (subs, subs), d) for d in range(2)]
        earlier = (down_it == along) & (ids[0] < ids[1])
        rank = jnp.sum(earlier.astype(F32), axis=0, keepdims=True).astype(jnp.int32)
        tile = along[:1].astype(jnp.int32)
        band = tile % 32
        side = (band >= 16).astype(jnp.int32)
        pair = jnp.where(side == 1, 31 - band, band)
        slot = pair * 32 + side * 16 + (tile // 32) * 2 + rank
        code = (slot * 256 + col_ref[...] * 32 + row_ref[...]).astype(F32)
        for j in range(CLASSES):
            out_ref[j * tall + 64:j * tall + 72, :] = jnp.broadcast_to(code, (8, subs))
        swap = down_it.astype(jnp.int32) % 32 >= 16
        half = lax.broadcasted_iota(jnp.int32, (64, 128), 1) < 64
        blocks = seg_ref.shape[1]
        pick = (seg_ref[...] == lax.broadcasted_iota(jnp.int32, (subs, blocks), 0)).astype(F32).astype(BF16)
        for l8 in range(8):
            lanes = slice(l8 * 256, (l8 + 1) * 256)
            ih, il = split(dot(pick, ch[:, lanes]) + dot(pick, cl[:, lanes]))
            a = dot3(ih, il, d1h[...], d1l[...])
            for cg in range(2):
                h, l = split(a[:, cg * 128:(cg + 1) * 128])
                ah[cg * subs:(cg + 1) * subs, l8 * 128:(l8 + 1) * 128] = h
                al[cg * subs:(cg + 1) * subs, l8 * 128:(l8 + 1) * 128] = l
        for c in tables:
            c.wait()
        for tile in range(4):
            lanes = slice(tile * 256, (tile + 1) * 256)
            spec = dot3(ah[...], al[...], d2h[:, lanes], d2l[:, lanes])
            for cg in range(2):
                for k in range(2):
                    j = cg * 8 + tile * 2 + k
                    f = spec[cg * subs:(cg + 1) * subs, k * 128:(k + 1) * 128]
                    r = pltpu.roll(f, 64, 1)
                    if j:
                        f, r = jnp.where(swap, r, f), jnp.where(swap, f, r)
                    out_ref[j * tall:j * tall + 64, :] = jnp.where(half, f[:64], r[64:])
                    out_ref[j * tall + 72:j * tall + 136, :] = jnp.where(half, r[:64], f[64:])


def make_payload(uv, vis, beam, seg, tile, row, col, tables):
    blocks, _, visible = uv.shape
    subs = tile.shape[0]
    tall = subs + 8
    (d1h, d1l), (d2h, d2l) = [halves(t) for t in tables]
    whole = lambda shape: pl.BlockSpec(shape, lambda i: (0,) * len(shape))
    return pl.pallas_call(
        grid_kernel,
        grid=(blocks // STEP,),
        in_specs=[
            pl.BlockSpec((STEP, 2, visible), lambda i: (i, 0, 0)),
            pl.BlockSpec((STEP, 2, visible), lambda i: (i, 0, 0)),
            pl.BlockSpec((2, STEP, SUB * SUB), lambda i: (0, i, 0)),
            whole((1, blocks)), whole((subs, 1)), whole((1, subs)), whole((1, subs)),
            whole((256, 256)), whole((256, 256)),
            pl.BlockSpec(memory_space=pl.ANY), pl.BlockSpec(memory_space=pl.ANY),
        ],
        out_specs=whole((CLASSES * tall, 128)),
        out_shape=jax.ShapeDtypeStruct((CLASSES * tall, 128), F32),
        scratch_shapes=[
            pltpu.VMEM((2, STEP * 8, 128), F32),
            pltpu.VMEM((2, STEP * 8, 128), F32),
            pltpu.VMEM((6, STEP, 128), F32),
            pltpu.VMEM((6, STEP, 128), F32),
            pltpu.VMEM((2, STEP * 8, 128), F32),
            pltpu.VMEM((blocks, 2048), BF16),
            pltpu.VMEM((blocks, 2048), BF16),
            pltpu.VMEM((2 * subs, 1024), BF16),
            pltpu.VMEM((2 * subs, 1024), BF16),
            pltpu.VMEM((1024, 1024), BF16),
            pltpu.VMEM((1024, 1024), BF16),
            pltpu.SemaphoreType.DMA((2,)),
        ],
        compiler_params=pltpu.CompilerParams(vmem_limit_bytes=48 * MB),
        name="gridding",
    )(uv, vis, beam, seg, tile, row, col, d1h, d1l, d2h, d2l)


MESH = pl.DeviceIdType.MESH


NEAR = [(0, 0), (0, 1), (1, 0), (-1, 0), (1, 1), (-1, 1), (2, 0), (-2, 0),
        (2, 1), (-2, 1), (3, 0), (-3, 0), (3, 1), (-3, 1), (4, 0), (4, 1)]
FAR = [(0, 1), (1, 0), (0, -1), (-1, 0), (0, 2), (2, 0), (1, 1), (-1, -1),
       (-1, 1), (1, -1), (2, 2), (1, 2), (2, 1), (-1, 2), (2, -1)]


def exchange_kernel(
    src_ref, wh_hbm, wl_hbm, t_hbm, eh, el, out_ref,
    near, box, held, grid_ref, x_ref, edge_src, edge_in, wh, wl, t_ref, lh, ll, kbuf, near2, fwd,
    near_send, near_recv, far_send, far_recv, edge_send, edge_recv, table_sem,
    near2_send, near2_recv, far2_send, far2_recv,
):
    y, core, z, x = [lax.axis_index(a) for a in ("y", "core", "z", "x")]
    group, kind = y * 4 + x, z * 2 + core
    tall = src_ref.shape[0] // CLASSES
    subs = tall - 8

    tables = [
        pltpu.make_async_copy(a, b, table_sem.at[n])
        for n, (a, b) in enumerate(((wh_hbm, wh), (wl_hbm, wl), (t_hbm, t_ref)))
    ]
    for c in tables:
        c.start()

    def loop(lo, hi, f):
        def step(k, _):
            f(k)
            return 0

        lax.fori_loop(lo, hi, step, 0)

    def to_near(k):
        dz, dc = NEAR[k]
        return (z + dz + 8) % 8, (core + dc) % 2

    def to_far(k):
        dy, dx = FAR[k]
        return (y + dy + 4) % 4, (x + dx + 4) % 4

    barrier = pltpu.get_barrier_semaphore()
    for k in range(1, 16):
        tz, tc = to_near(k)
        pl.semaphore_signal(barrier, inc=1, device_id=(y, tc, tz, x), device_id_type=MESH)
    for k in range(15):
        ty, tx = to_far(k)
        pl.semaphore_signal(barrier, inc=1, device_id=(ty, core, z, tx), device_id_type=MESH)
    pl.semaphore_wait(barrier, 30)

    def near_copy(ab, k):
        tz, tc = to_near(k)
        first, rows = (72, 64) if ab else (0, 72)
        return pltpu.make_async_remote_copy(
            src_ref=src_ref.at[pl.ds(pl.multiple_of((tz * 2 + tc) * tall + first, 8), rows), :],
            dst_ref=near.at[k, pl.ds(first, rows), :],
            send_sem=near_send.at[ab, k],
            recv_sem=near_recv.at[ab, k],
            device_id=(y, tc, tz, x),
            device_id_type=MESH,
        )

    def far_copy(ab, g, k):
        ty, tx = to_far(k)
        h, rows = g // 2, pl.ds((g % 2) * 64, 64 + (8 if g % 2 and ab == 0 else 0))
        return pltpu.make_async_remote_copy(
            src_ref=box.at[ab, h, ty * 4 + tx, rows, :],
            dst_ref=held.at[ab, h, k, rows, :],
            send_sem=far_send.at[ab, g, k],
            recv_sem=far_recv.at[ab, g, k],
            device_id=(ty, core, z, tx),
            device_id_type=MESH,
        )

    window = 8
    queue = [(ab, k) for ab in range(2) for k in range(1, 16)]
    for item in queue[:window]:
        near_copy(*item).start()
    near[0] = src_ref[pl.ds(pl.multiple_of(kind * tall, 8), tall), :]

    zero_class = kind == 0
    special = jnp.where((kind == 0) & (group == 0), 1, 0)
    row = lax.broadcasted_iota(jnp.int32, (512, subs), 0)
    line = lax.broadcasted_iota(jnp.int32, (8, subs), 0)
    left = lax.broadcasted_iota(jnp.int32, (256, 128), 1) < 64
    for ab in range(2):
        side = jnp.where(zero_class, 0, ab)
        slots = row % 256 // 16 * 32 + (row // 256 + side) % 2 * 16 + row % 16
        first = 72 if ab else 0
        codes = jnp.zeros((8, subs), F32)
        for g in range(4):
            h = g // 2
            for i in range(4):
                k8 = (g % 2) * 4 + i
                k = h * 8 + k8
                if k:
                    near_copy(ab, k).wait()
                    after = queue.index((ab, k)) + window
                    if after < len(queue):
                        near_copy(*queue[after]).start()
                code = near[k, 64:65, :]
                fits = (code.astype(jnp.int32) // 256 == slots).astype(F32).astype(BF16)
                data = near[k, first:first + 64, :]
                turned = pltpu.roll(data, 64, 1)
                hi, lo = split(jnp.concatenate(
                    [jnp.where(left[:64], data, turned), jnp.where(left[:64], turned, data)], axis=0))
                o = dot(jnp.concatenate([fits, fits], axis=1), jnp.concatenate([hi, lo], axis=0))
                o = jnp.where(left, o[:256], o[256:])
                for p in range(PAIRS):
                    box[ab, h, p, k8 * 16:k8 * 16 + 16, :] = o[p * 16:(p + 1) * 16]
                codes = jnp.where(line == k8, code, codes)
            if g % 2 == 1 and ab == 0:
                for p in range(PAIRS):
                    box[0, h, p, 128:136, :] = codes
            for k in range(15):
                if ab:
                    far_copy(0, g, k).wait_send()
                far_copy(ab, g, k).start()
            if g % 2 == 1:
                rows = slice(0, 136 if ab == 0 else 128)
                held[ab, h, 15, rows, :] = box[ab, h, group, rows, :]

    pos = lax.broadcasted_iota(jnp.int32, (256, 256), 0).astype(F32)

    def place(ab):
        side = jnp.where(zero_class, 0, ab)
        if ab == 0:
            grid_ref[0, :, 64:128] = jnp.zeros((256, 64), F32)
            grid_ref[8] = jnp.zeros((256, 128), F32)
            last = jnp.where(zero_class, 8, 7)
        else:
            last = 7
        for h in range(2):
            for g in (2 * h, 2 * h + 1):
                for k in range(15):
                    far_copy(ab, g, k).wait_recv()
            code = jnp.concatenate([held[0, h, k, 128:136, :] for k in range(16)], axis=0).T.astype(jnp.int32)
            at = code // 256 - group * 32
            value = (code % 256 + 1).astype(F32)

            def put(r):
                hot = [[], []]
                data = []
                for rank in range(2):
                    slot = r * 2 + rank
                    for n, which in enumerate((side, 1 - side)):
                        hot[n].append(jnp.sum(
                            jnp.where(at == slot + which * 16, value, 0.0), axis=0, keepdims=True) - 1.0)
                    data += [held[ab, h, k, pl.ds(slot, 8, stride=16), :] for k in range(16)]
                fits = jnp.concatenate(
                    [(jnp.concatenate(x, axis=1) == pos).astype(F32).astype(BF16) for x in hot], axis=0)
                hi, lo = split(jnp.concatenate(data, axis=0))
                v = dot(fits, jnp.concatenate([hi, lo], axis=1))
                v = v[:, :128] + v[:, 128:]
                rows = pl.ds(pl.multiple_of(r * 32, 32), 32)
                for bc in range(8):
                    own = v[bc * 32:(bc + 1) * 32, 0:64]
                    mirror = v[256 + bc * 32:256 + (bc + 1) * 32, 64:128]
                    if h == 1:
                        own = grid_ref[bc, rows, 0:64] + own
                        mirror = grid_ref[last - bc, rows, 64:128] + mirror
                    grid_ref[bc, rows, 0:64] = own
                    grid_ref[last - bc, rows, 64:128] = mirror

            loop(0, 8, put)

        def flip(i):
            x_ref[pl.ds(pl.multiple_of(i * 128, 128), 128), :] = grid_ref[i].T

        loop(0, 8, flip)

    tx, ty = (x + 1) % 4, (y + (x + 1) // 4) % 4
    edge = pltpu.make_async_remote_copy(
        src_ref=edge_src, dst_ref=edge_in, send_sem=edge_send, recv_sem=edge_recv,
        device_id=(ty, core, z, tx), device_id_type=MESH,
    )

    e2 = jnp.concatenate([eh[...], eh[...]], axis=1)
    low = lax.broadcasted_iota(jnp.int32, (32, 128), 1) < 64

    def near2_copy(ab, nt, t, dc):
        zh, tc = (z // 2 + t) % 4, (core + dc) % 2
        tz = zh * 2 + nt
        return (tz * 2 + tc) != kind, pltpu.make_async_remote_copy(
            src_ref=kbuf.at[pl.ds(pl.multiple_of(((ab * 2 + nt) * 8 + tc * 4 + zh) * 64, 64), 64), :],
            dst_ref=near2.at[ab, kind],
            send_sem=near2_send.at[ab, nt, t, dc],
            recv_sem=near2_recv.at[ab, kind],
            device_id=(y, tc, tz, x),
            device_id_type=MESH,
        )

    def transform(ab):
        for bc in range(8):
            own = x_ref[bc * 128:bc * 128 + 64, :]
            mirror = x_ref[bc * 128 + 64:bc * 128 + 128, :]
            if ab == 0 and bc == 0:
                mirror = jnp.where(zero_class, edge_in[...], mirror)
            for c2, v in enumerate((own, mirror)):
                hi, lo = split(v)
                row = bc * 64 + c2 * 32
                for ri in range(2):
                    lh[row:row + 32, ri * 256:(ri + 1) * 256] = hi[ri * 32:(ri + 1) * 32]
                    ll[row:row + 32, ri * 256:(ri + 1) * 256] = lo[ri * 32:(ri + 1) * 32]
        for nt in range(2):
            cols = slice(nt * 512, (nt + 1) * 512)

            def one(i):
                rows = pl.ds(pl.multiple_of(i * 256, 256), 256)
                v = dot3(lh[rows, :], ll[rows, :], wh[:, cols], wl[:, cols])
                for k in range(2):
                    parts = []
                    for b in range(2):
                        r = (k * 2 + b) * 64
                        ya, yb = v[r:r + 64, :256], v[r:r + 64, 256:]
                        which = 0
                        if ab == 0 and k == 0 and b == 0:
                            which = jnp.where(i == 0, special, 0)
                        tab = lambda n: t_ref[which * 8 + n * 2 + nt]
                        parts.append(jnp.concatenate(
                            [ya * tab(0) + yb * tab(1), ya * tab(2) + yb * tab(3)], axis=0))
                    th, tl = split(jnp.concatenate(parts, axis=1))
                    o = dot(e2, jnp.concatenate([th, tl], axis=0)) + dot(el[...], th)
                    for g in range(2):
                        o0 = o[:, g * 128:(g + 1) * 128]
                        o1 = o[:, 256 + g * 128:256 + (g + 1) * 128]
                        pair = (jnp.where(low, o0, pltpu.roll(o1, 64, 1)), jnp.where(low, pltpu.roll(o0, 64, 1), o1))
                        for e in range(2):
                            for ty in range(4):
                                first = (ab * 2 + nt) * 512 + ty * 16 + (g * 2 + e) * 4 + i * 2 + k
                                kbuf[pl.ds(first, 8, stride=64), :] = pair[e][ty * 8:(ty + 1) * 8]

            loop(0, 2, one)
            for t in (0, 1, 3, 2):
                for dc in range(2):
                    other, copy = near2_copy(ab, nt, t, dc)

                    @pl.when(other)
                    def _():
                        copy.start()

        mine = ab * 1024 + ((z % 2) * 8 + core * 4 + z // 2) * 64
        near2[ab, kind] = kbuf[pl.ds(pl.multiple_of(mine, 64), 64), :]

    place(0)
    edge_src[...] = grid_ref[8].T[64:]
    edge.start()
    for c in tables:
        c.wait()
    edge.wait_recv()
    transform(0)
    place(1)
    transform(1)

    def far2_copy(ab, t, k):
        ty, tx = to_far(k)
        return pltpu.make_async_remote_copy(
            src_ref=fwd.at[ab, t, ty * 4 + tx],
            dst_ref=out_ref.at[ab, (z // 2 - t + 4) % 4, group],
            send_sem=far2_send.at[ab, t, k],
            recv_sem=far2_recv.at[ab, t, k],
            device_id=(ty, core, z, tx),
            device_id_type=MESH,
        )

    for ab in range(2):
        for t in (0, 1, 3, 2):
            zh = (z // 2 - t + 4) % 4
            for i in range(4):
                sender = zh * 4 + i

                @pl.when(sender != kind)
                def _():
                    pltpu.make_async_remote_copy(
                        src_ref=kbuf.at[pl.ds(0, 64), :], dst_ref=near2.at[ab, sender],
                        send_sem=near2_send.at[0, 0, 0, 0], recv_sem=near2_recv.at[ab, sender],
                        device_id=(y, 1 - core, z, x), device_id_type=MESH,
                    ).wait_recv()

                for m in range(8):
                    v = near2[ab, sender, m * 8:(m + 1) * 8, :]
                    for e in range(2):
                        fwd[ab, t, m * 2 + e, i * 4:i * 4 + 4, :] = v[e * 4:(e + 1) * 4]
            for k in range(15):
                far2_copy(ab, t, k).start()
            out_ref[ab, zh, group] = fwd[ab, t, group]

    for ab in range(2):
        for t in range(4):
            for k in range(15):
                far2_copy(ab, t, k).wait_recv()
    edge.wait_send()
    for g in range(4):
        for k in range(15):
            far_copy(1, g, k).wait_send()
    for ab in range(2):
        for nt in range(2):
            for t in range(4):
                for dc in range(2):
                    other, copy = near2_copy(ab, nt, t, dc)

                    @pl.when(other)
                    def _():
                        copy.wait_send()
    for ab in range(2):
        for t in range(4):
            for k in range(15):
                far2_copy(ab, t, k).wait_send()


def exchange(payload):
    tall = payload.shape[0] // CLASSES
    w, t, e = down_tables()
    wh, wl = halves(w)
    eh, el = halves(e)
    vmem = pl.BlockSpec(memory_space=pltpu.VMEM)
    hbm = pl.BlockSpec(memory_space=pl.ANY)
    dma = pltpu.SemaphoreType.DMA
    return pl.pallas_call(
        exchange_kernel,
        in_specs=[vmem, hbm, hbm, hbm, vmem, vmem],
        out_specs=vmem,
        out_shape=jax.ShapeDtypeStruct((2, 4, 16, 16, 128), F32),
        scratch_shapes=[
            pltpu.VMEM((16, tall, 128), F32),
            pltpu.VMEM((2, 2, 16, 136, 128), F32),
            pltpu.VMEM((2, 2, 16, 136, 128), F32),
            pltpu.VMEM((9, 256, 128), F32),
            pltpu.VMEM((1024, 256), F32),
            pltpu.VMEM((64, 256), F32),
            pltpu.VMEM((64, 256), F32),
            pltpu.VMEM((512, 1024), BF16),
            pltpu.VMEM((512, 1024), BF16),
            pltpu.VMEM((16, 64, 256), F32),
            pltpu.VMEM((512, 512), BF16),
            pltpu.VMEM((512, 512), BF16),
            pltpu.VMEM((2048, 128), F32),
            pltpu.VMEM((2, 16, 64, 128), F32),
            pltpu.VMEM((2, 4, 16, 16, 128), F32),
            dma((2, 16)), dma((2, 16)), dma((2, 4, 16)), dma((2, 4, 16)), dma(()), dma(()), dma((3,)),
            dma((2, 2, 4, 2)), dma((2, 16)), dma((2, 4, 16)), dma((2, 4, 16)),
        ],
        compiler_params=pltpu.CompilerParams(
            collective_id=0, has_side_effects=True, vmem_limit_bytes=48 * MB
        ),
        name="exchange",
    )(payload, wh, wl, t, eh, el)


def across_kernel(k_ref, wh, wl, zh, zl, twist, out_ref, lh, ll, y_ref):
    for j in range(16):
        first = [(ab * 4 + j // 4) * 256 + j % 4 * 4 + bc2 for ab in range(2) for bc2 in range(4)]
        a = jnp.concatenate([k_ref[pl.ds(i, PAIRS, stride=16), :] for i in first], axis=0).T
        h, l = split(a)
        for i in range(4):
            lh[j * 32:(j + 1) * 32, i * 128:(i + 1) * 128] = h[i * 32:(i + 1) * 32]
            ll[j * 32:(j + 1) * 32, i * 128:(i + 1) * 128] = l[i * 32:(i + 1) * 32]
    edge = dot3(lh[0:32, :], ll[0:32, :], zh[...], zl[...])
    y_ref[0:32] = edge[:, :512]
    y_ref[512:544] = edge[:, 512:]
    y_ref[32:512] = dot3(lh[32:512, :], ll[32:512, :], wh[...], wl[...])

    cos = [math.cos(2 * math.pi * i / 32) for i in range(32)]
    sin = [math.sin(2 * math.pi * i / 32) for i in range(32)]

    def combine(terms):
        total = None
        for f, x in terms:
            if abs(f) < 1e-12:
                continue
            v = x if f == 1.0 else -x if f == -1.0 else x * f
            total = v if total is None else total + v
        return total

    def rows(i, _):
        at = pl.multiple_of(i * 8, 8)
        for half in range(2):
            lane = slice(half * 128, (half + 1) * 128)
            tre, tim = [], []
            for v in range(17):
                yre = y_ref[pl.ds(v * 32 + at, 8), lane]
                yim = y_ref[pl.ds(v * 32 + at, 8), 256 + half * 128:256 + (half + 1) * 128]
                c = twist[v:v + 1, lane]
                s = twist[v:v + 1, 256 + half * 128:256 + (half + 1) * 128]
                tre.append(yre * c - yim * s)
                tim.append(yre * s + yim * c)
            for m2 in range(9):
                e0 = combine([(cos[v * m2 % 32], tre[v]) for v in range(0, 17, 2)])
                e1 = combine([(cos[v * m2 % 32], tre[v]) for v in range(1, 17, 2)])
                o0 = combine([(sin[v * m2 % 32], tim[v]) for v in range(0, 17, 2)])
                o1 = combine([(sin[v * m2 % 32], tim[v]) for v in range(1, 17, 2)])
                zero = jnp.zeros((8, 128), F32)
                e0, e1, o0, o1 = [zero if x is None else x for x in (e0, e1, o0, o1)]
                puts = {m2: (e0 + e1) - (o0 + o1), (32 - m2) % 32: (e0 + e1) + (o0 + o1)}
                puts[16 - m2] = (e0 - e1) + (o0 - o1)
                puts[16 + m2] = (e0 - e1) - (o0 - o1)
                for m, v in puts.items():
                    out_ref[pl.ds(at, 8), m * 256 + half * 128:m * 256 + (half + 1) * 128] = v
        return 0

    lax.fori_loop(0, 4, rows, 0)


def across(k):
    w, zero, twist = across_tables()
    wh, wl = halves(w)
    zh, zl = halves(zero)
    return pl.pallas_call(
        across_kernel,
        out_shape=jax.ShapeDtypeStruct((32, G), F32),
        scratch_shapes=[
            pltpu.VMEM((512, 512), BF16), pltpu.VMEM((512, 512), BF16), pltpu.VMEM((544, 512), F32),
        ],
        compiler_params=pltpu.CompilerParams(vmem_limit_bytes=32 * MB),
        name="across",
    )(k, wh, wl, zh, zl, twist)


def body(uv, vis, left, right, block_subgrid, subgrid_tile, block_row, block_col):
    visible = uv.shape[2]

    l, r = left.astype(F32), right.astype(F32)
    beam = jnp.stack([
        l[:, 0] * r[:, 0] + l[:, 1] * r[:, 1],
        l[:, 1] * r[:, 0] - l[:, 0] * r[:, 1],
    ])
    payload = make_payload(
        uv, vis, beam, block_subgrid, subgrid_tile, block_row[None], block_col[None], subgrid_tables(visible)
    )
    return across(exchange(payload).reshape(2048, 128))


def solution(mesh):
    names = ("y", "core", "z", "x")
    axes = Mesh(mesh.devices.reshape(4, 2, 8, 4), names)
    placed = (
        P(names, None, None),
        P(names, None, None),
        P(names, None, None),
        P(names, None, None),
        P(names, None),
        P(names, None),
        P(names),
        P(names),
    )
    return jax.shard_map(body, mesh=axes, in_specs=placed, out_specs=P(names, None), check_vma=False)
```

```python
import math
from functools import partial

import jax
import jax.numpy as jnp
import ml_dtypes
import numpy as np
from jax import lax
from jax.experimental import pallas as pl
from jax.experimental.pallas import tpu as pltpu
from jax.sharding import Mesh, PartitionSpec as P

G = 8192
SUB = 32
PAIRS = 16
CLASSES = 16
STEP = 64
F32 = jnp.float32
BF16 = jnp.bfloat16
MB = 1 << 20


def halves(table):
    high = np.asarray(table, np.float32).astype(ml_dtypes.bfloat16)
    low = (np.asarray(table, np.float64) - high.astype(np.float64)).astype(ml_dtypes.bfloat16)
    return high, low


def split(x):
    high = x.astype(BF16)
    return high, (x - high.astype(F32)).astype(BF16)


def dot(a, b):
    return lax.dot_general(a, b, (((1,), (0,)), ((), ())), preferred_element_type=F32)


def dot_nt(a, b):
    return lax.dot_general(a, b, (((1,), (1,)), ((), ())), preferred_element_type=F32)


def dot3(ah, al, bh, bl):
    return dot(ah, bh) + (dot(al, bh) + dot(ah, bl))


def taper(p):
    return np.sin(math.pi * (p + 0.5) / SUB)


def class_column(j, c2):
    return j if c2 == 0 else (16 if j == 0 else 32 - j)


def subgrid_tables(visible):
    m = np.arange(32)
    first = np.zeros((2, 4, 32, 2, 4, 2, 8, 2))
    second = np.zeros((8, 4, 2, 8, 2, 8, 2, 2, 32))
    for cg in range(2):
        for j8 in range(8):
            for c2 in range(2):
                phi = 2 * math.pi * ((class_column(cg * 8 + j8, c2) * m) % 32) / 32
                for l4 in range(4):
                    first[0, l4, :, cg, l4, 0, j8, c2] = np.cos(phi) * taper(m)
                    first[1, l4, :, cg, l4, 0, j8, c2] = np.sin(phi) * taper(m)
                    first[0, l4, :, cg, l4, 1, j8, c2] = -np.sin(phi) * taper(m)
                    first[1, l4, :, cg, l4, 1, j8, c2] = np.cos(phi) * taper(m)
    a = np.arange(32)
    scale = visible ** (-0.5) / SUB / G
    for l8 in range(8):
        for l4 in range(4):
            l = 4 * l8 + l4
            phi = 2 * math.pi * ((a * l) % 32) / 32
            weight = taper(l) * scale
            for j8 in range(8):
                for c2 in range(2):
                    second[l8, l4, 0, j8, c2, j8, c2, 0] = np.cos(phi) * weight
                    second[l8, l4, 1, j8, c2, j8, c2, 0] = np.sin(phi) * weight
                    second[l8, l4, 0, j8, c2, j8, c2, 1] = -np.sin(phi) * weight
                    second[l8, l4, 1, j8, c2, j8, c2, 1] = np.cos(phi) * weight
    return first.reshape(256, 256), second.reshape(1024, 1024)


def down_tables():
    r = np.arange(256)[:, None, None, None]
    nt, q4, lo = np.meshgrid(np.arange(2), np.arange(4), np.arange(32), indexing="ij")
    l1 = ((nt * 4 + q4) * 32 + lo)[None]
    phi = 2 * math.pi * ((r * l1) % 256) / 256
    c, s = np.cos(phi), np.sin(phi)
    w = np.zeros((2, 256, 2, 2, 4, 2, 32))
    w[0, :, :, 0, :, 0], w[1, :, :, 0, :, 0] = c, -s
    w[0, :, :, 0, :, 1], w[1, :, :, 0, :, 1] = s, c
    w[0, :, :, 1, :, 0], w[1, :, :, 1, :, 0] = -s, -c
    w[0, :, :, 1, :, 1], w[1, :, :, 1, :, 1] = c, -s
    a = np.arange(32)[None, :, None, None]
    l1 = ((nt * 4 + q4) * 32 + lo)[:, None]
    psi = 2 * math.pi * a * l1 / G
    c, s = np.cos(psi), np.sin(psi)
    t = np.zeros((2, 4, 2, 2, 32, 4, 2, 32))
    for which in range(2):
        t[which, 0, :, 0, :, :, 0], t[which, 1, :, 0, :, :, 0] = c, s
        t[which, 2, :, 0, :, :, 0], t[which, 3, :, 0, :, :, 0] = -s, c
    t[0, 0, :, 0, :, :, 1], t[0, 1, :, 0, :, :, 1] = c, s
    t[0, 2, :, 0, :, :, 1], t[0, 3, :, 0, :, :, 1] = -s, c
    t[0, 0, :, 1, :, :, 0], t[0, 1, :, 1, :, :, 0] = c, s
    t[0, 2, :, 1, :, :, 0], t[0, 3, :, 1, :, :, 0] = s, -c
    t[0, 0, :, 1, :, :, 1], t[0, 1, :, 1, :, :, 1] = -c, -s
    t[0, 2, :, 1, :, :, 1], t[0, 3, :, 1, :, :, 1] = -s, c
    t[1, 0, :, 1, :, :, 1], t[1, 1, :, 1, :, :, 1] = -s, c
    t[1, 2, :, 1, :, :, 1], t[1, 3, :, 1, :, :, 1] = c, s
    phi = 2 * math.pi * ((np.arange(32)[:, None] * np.arange(32)[None, :]) % 32) / 32
    e = np.zeros((32, 2, 2, 32))
    e[:, 0, 0], e[:, 0, 1] = np.cos(phi), np.cos(phi)
    e[:, 1, 0], e[:, 1, 1] = np.sin(phi), -np.sin(phi)
    return w.reshape(512, 1024), t.reshape(16, 64, 256).astype(np.float32), e.reshape(32, 128)


def across_tables():
    w = np.zeros((3, 2, 2, 2, 4, 16, 2, 256))
    m1 = np.arange(256)
    bc2, p = np.meshgrid(np.arange(4), np.arange(16), indexing="ij")
    for bcl in range(2):
        bc = bc2 * 2 + bcl
        for kind, s, v1 in ((0, 0, 8 * p + bc), (0, 1, 8 * (31 - p) + bc), (1, 0, 8 * p + bc), (2, 1, 8 * p + bc)):
            phi = 2 * math.pi * ((v1[:, :, None] * m1) % 256) / 256
            w[kind, bcl, 0, s, :, :, 0], w[kind, bcl, 1, s, :, :, 0] = np.cos(phi), -np.sin(phi)
            w[kind, bcl, 0, s, :, :, 1], w[kind, bcl, 1, s, :, :, 1] = np.sin(phi), np.cos(phi)
    w[1, 0, 1, 0, 0, 0, 0] = 1 - 2 * (m1 % 2)
    w[1, 0, 1, 0, 0, 0, 1] = 0
    w = w.reshape(3, 512, 512)
    psi = 2 * math.pi * np.arange(17)[:, None] * np.arange(256)[None, :] / G
    twist = np.concatenate([np.cos(psi), np.sin(psi)], axis=1).astype(np.float32)
    return w[0], np.concatenate([w[1], w[2]], axis=1), twist


def turn(t):
    quarter = jnp.round(t * 4.0)
    x = (t - quarter * 0.25) * (2 * math.pi)
    y = x * x
    sine = x * (1 + y * (-1 / 6 + y * (1 / 120 + y * (-1 / 5040 + y * (1 / 362880)))))
    cosine = 1 + y * (-0.5 + y * (1 / 24 + y * (-1 / 720 + y * (1 / 40320))))
    q = quarter.astype(jnp.int32)
    odd = (q & 1) != 0
    c = jnp.where(odd, sine, cosine)
    s = jnp.where(odd, cosine, sine)
    c = jnp.where(((q + 1) & 2) != 0, -c, c)
    s = jnp.where((q & 2) != 0, -s, s)
    return c, s


def times(x, y):
    return x[0] * y[0] - x[1] * y[1], x[0] * y[1] + x[1] * y[0]


def conj(x):
    return x[0], -x[1]


def grid_kernel(
    uv_ref, vis_ref, beam_ref, seg_ref, tile_ref, row_ref, col_ref, d1h, d1l, d2h_hbm, d2l_hbm,
    out_ref,
    base_l, base_m, fact_l, fact_m, image, ch, cl, ah, al, d2h, d2l, table_sem,
):
    step = pl.program_id(0)
    n = STEP
    tables = [
        pltpu.make_async_copy(a, b, table_sem.at[i]) for i, (a, b) in enumerate(((d2h_hbm, d2h), (d2l_hbm, d2l)))
    ]

    @pl.when(step == 0)
    def _():
        for c in tables:
            c.start()

    zu = turn(uv_ref[:, 0, :] * (1 / 32))
    zv = turn(uv_ref[:, 1, :] * (1 / 32))
    vis = (vis_ref[:, 0, :], vis_ref[:, 1, :])
    u2 = times(zu, zu)
    u3 = times(u2, zu)
    u4 = times(u2, u2)
    u8 = times(u4, u4)
    u12 = times(u8, u4)
    u16 = times(u8, u8)
    for i, f in enumerate((conj(u16), conj(u12), conj(u8), conj(u4), None, u4, u8, u12)):
        b = vis if f is None else times(vis, f)
        base_l[0, pl.ds(i, n, stride=8), :] = b[0]
        base_l[1, pl.ds(i, n, stride=8), :] = b[1]
    for i, f in enumerate((zu, u2, u3)):
        fact_l[2 * i] = f[0]
        fact_l[2 * i + 1] = f[1]
    v2 = times(zv, zv)
    v3 = times(v2, zv)
    v4 = times(v2, v2)
    v5 = times(v4, zv)
    v6 = times(v4, v2)
    v7 = times(v4, v3)
    v8 = times(v4, v4)
    v16 = times(v8, v8)
    one = (jnp.ones_like(zv[0]), jnp.zeros_like(zv[0]))
    for i, f in enumerate((one, zv, v2, v3, v4, v5, v6, v7)):
        base_m[0, pl.ds(i, n, stride=8), :] = f[0]
        base_m[1, pl.ds(i, n, stride=8), :] = f[1]
    for i, f in enumerate((conj(v16), conj(v8), v8)):
        fact_m[2 * i] = f[0]
        fact_m[2 * i + 1] = f[1]

    def one_block(b, _):
        rows = pl.ds(pl.multiple_of(b * 8, 8), 8)
        line = pl.ds(b, 1)
        bl = (base_l[0, rows, :], base_l[1, rows, :])
        bm = (base_m[0, rows, :], base_m[1, rows, :])
        real, imag = [], []
        for t in range(4):
            w = bl if t == 0 else times(bl, (fact_l[2 * t - 2, line, :], fact_l[2 * t - 1, line, :]))
            real.append(w[0])
            imag.append(w[1])
        rh, rl = split(jnp.concatenate(real, axis=0))
        ih, il = split(jnp.concatenate(imag, axis=0))
        lh = jnp.concatenate([rh, ih], axis=1)
        ll = jnp.concatenate([rl, il], axis=1)
        cosine, sine = [], []
        for t in range(4):
            i = {0: 0, 1: 1, 3: 2}.get(t)
            w = bm if i is None else times(bm, (fact_m[2 * i, line, :], fact_m[2 * i + 1, line, :]))
            cosine.append(w[0])
            sine.append(w[1])
        cosh, cosl = split(jnp.concatenate(cosine, axis=0))
        sinh, sinl = split(jnp.concatenate(sine, axis=0))
        mh = jnp.concatenate(
            [jnp.concatenate([cosh, sinh], axis=0), jnp.concatenate([-sinh, cosh], axis=0)], axis=1)
        ml = jnp.concatenate(
            [jnp.concatenate([cosl, sinl], axis=0), jnp.concatenate([-sinl, cosl], axis=0)], axis=1)
        o = dot_nt(jnp.concatenate([lh, ll], axis=0), mh)
        o = o[:32] + (o[32:] + dot_nt(lh, ml))
        for ri in range(2):
            lanes = slice(ri * 32, ri * 32 + 32)
            image[ri, rows, :] = jnp.concatenate([o[8 * t:8 * t + 8, lanes] for t in range(4)], axis=1)
        return 0

    lax.fori_loop(0, n, one_block, 0, unroll=n)

    here = pl.ds(pl.multiple_of(step * n, n), n)
    for l8 in range(8):
        im = (image[0, pl.ds(l8, n, stride=8), :], image[1, pl.ds(l8, n, stride=8), :])
        bm = (beam_ref[0, :, l8 * 128:(l8 + 1) * 128], beam_ref[1, :, l8 * 128:(l8 + 1) * 128])
        c = times(bm, im)
        for ri in range(2):
            h, l = split(c[ri])
            ch[here, (2 * l8 + ri) * 128:(2 * l8 + ri + 1) * 128] = h
            cl[here, (2 * l8 + ri) * 128:(2 * l8 + ri + 1) * 128] = l

    @pl.when(step == pl.num_programs(0) - 1)
    def _():
        subs = tile_ref.shape[0]
        tall = subs + 8
        down_it = jnp.broadcast_to(tile_ref[...].astype(F32), (subs, subs))
        along = down_it.T
        ids = [lax.broadcasted_iota(jnp.int32, (subs, subs), d) for d in range(2)]
        earlier = (down_it == along) & (ids[0] < ids[1])
        rank = jnp.sum(earlier.astype(F32), axis=0, keepdims=True).astype(jnp.int32)
        tile = along[:1].astype(jnp.int32)
        band = tile % 32
        side = (band >= 16).astype(jnp.int32)
        pair = jnp.where(side == 1, 31 - band, band)
        slot = pair * 32 + side * 16 + (tile // 32) * 2 + rank
        code = (slot * 256 + col_ref[...] * 32 + row_ref[...]).astype(F32)
        for j in range(CLASSES):
            out_ref[j * tall + 64:j * tall + 72, :] = jnp.broadcast_to(code, (8, subs))
        swap = down_it.astype(jnp.int32) % 32 >= 16
        half = lax.broadcasted_iota(jnp.int32, (64, 128), 1) < 64
        blocks = seg_ref.shape[1]
        pick = (seg_ref[...] == lax.broadcasted_iota(jnp.int32, (subs, blocks), 0)).astype(F32).astype(BF16)
        for l8 in range(8):
            lanes = slice(l8 * 256, (l8 + 1) * 256)
            ih, il = split(dot(pick, ch[:, lanes]) + dot(pick, cl[:, lanes]))
            a = dot3(ih, il, d1h[...], d1l[...])
            for cg in range(2):
                h, l = split(a[:, cg * 128:(cg + 1) * 128])
                ah[cg * subs:(cg + 1) * subs, l8 * 128:(l8 + 1) * 128] = h
                al[cg * subs:(cg + 1) * subs, l8 * 128:(l8 + 1) * 128] = l
        for c in tables:
            c.wait()
        for tile in range(4):
            lanes = slice(tile * 256, (tile + 1) * 256)
            spec = dot3(ah[...], al[...], d2h[:, lanes], d2l[:, lanes])
            for cg in range(2):
                for k in range(2):
                    j = cg * 8 + tile * 2 + k
                    f = spec[cg * subs:(cg + 1) * subs, k * 128:(k + 1) * 128]
                    r = pltpu.roll(f, 64, 1)
                    if j:
                        f, r = jnp.where(swap, r, f), jnp.where(swap, f, r)
                    out_ref[j * tall:j * tall + 64, :] = jnp.where(half, f[:64], r[64:])
                    out_ref[j * tall + 72:j * tall + 136, :] = jnp.where(half, r[:64], f[64:])


def make_payload(uv, vis, beam, seg, tile, row, col, tables):
    blocks, _, visible = uv.shape
    subs = tile.shape[0]
    tall = subs + 8
    (d1h, d1l), (d2h, d2l) = [halves(t) for t in tables]
    whole = lambda shape: pl.BlockSpec(shape, lambda i: (0,) * len(shape))
    return pl.pallas_call(
        grid_kernel,
        grid=(blocks // STEP,),
        in_specs=[
            pl.BlockSpec((STEP, 2, visible), lambda i: (i, 0, 0)),
            pl.BlockSpec((STEP, 2, visible), lambda i: (i, 0, 0)),
            pl.BlockSpec((2, STEP, SUB * SUB), lambda i: (0, i, 0)),
            whole((1, blocks)), whole((subs, 1)), whole((1, subs)), whole((1, subs)),
            whole((256, 256)), whole((256, 256)),
            pl.BlockSpec(memory_space=pltpu.HBM), pl.BlockSpec(memory_space=pltpu.HBM),
        ],
        out_specs=whole((CLASSES * tall, 128)),
        out_shape=jax.ShapeDtypeStruct((CLASSES * tall, 128), F32),
        scratch_shapes=[
            pltpu.VMEM((2, STEP * 8, 128), F32),
            pltpu.VMEM((2, STEP * 8, 128), F32),
            pltpu.VMEM((6, STEP, 128), F32),
            pltpu.VMEM((6, STEP, 128), F32),
            pltpu.VMEM((2, STEP * 8, 128), F32),
            pltpu.VMEM((blocks, 2048), BF16),
            pltpu.VMEM((blocks, 2048), BF16),
            pltpu.VMEM((2 * subs, 1024), BF16),
            pltpu.VMEM((2 * subs, 1024), BF16),
            pltpu.VMEM((1024, 1024), BF16),
            pltpu.VMEM((1024, 1024), BF16),
            pltpu.SemaphoreType.DMA((2,)),
        ],
        compiler_params=pltpu.CompilerParams(vmem_limit_bytes=48 * MB),
        name="gridding",
    )(uv, vis, beam, seg, tile, row, col, d1h, d1l, d2h, d2l)


MESH = pl.DeviceIdType.MESH


NEAR = [(0, 0), (0, 1), (1, 0), (-1, 0), (1, 1), (-1, 1), (2, 0), (-2, 0),
        (2, 1), (-2, 1), (3, 0), (-3, 0), (3, 1), (-3, 1), (4, 0), (4, 1)]
FAR = [(0, 1), (1, 0), (0, -1), (-1, 0), (0, 2), (2, 0), (1, 1), (-1, -1),
       (-1, 1), (1, -1), (2, 2), (1, 2), (2, 1), (-1, 2), (2, -1)]


def exchange_kernel(
    src_ref, wh_hbm, wl_hbm, t_hbm, eh, el, out_ref,
    near, box, held, grid_ref, x_ref, edge_src, edge_in, wh, wl, t_ref, lh, ll, kbuf, near2, fwd,
    near_send, near_recv, far_send, far_recv, edge_send, edge_recv, table_sem,
    near2_send, near2_recv, far2_send, far2_recv,
):
    y, core, z, x = [lax.axis_index(a) for a in ("y", "core", "z", "x")]
    group, kind = y * 4 + x, z * 2 + core
    tall = src_ref.shape[0] // CLASSES
    subs = tall - 8

    tables = [
        pltpu.make_async_copy(a, b, table_sem.at[n])
        for n, (a, b) in enumerate(((wh_hbm, wh), (wl_hbm, wl), (t_hbm, t_ref)))
    ]
    for c in tables:
        c.start()

    def loop(lo, hi, f):
        def step(k, _):
            f(k)
            return 0

        lax.fori_loop(lo, hi, step, 0)

    def to_near(k):
        dz, dc = NEAR[k]
        return (z + dz + 8) % 8, (core + dc) % 2

    def to_far(k):
        dy, dx = FAR[k]
        return (y + dy + 4) % 4, (x + dx + 4) % 4

    barrier = pltpu.get_barrier_semaphore()
    for k in range(1, 16):
        tz, tc = to_near(k)
        pl.semaphore_signal(barrier, inc=1, device_id=(y, tc, tz, x), device_id_type=MESH)
    for k in range(15):
        ty, tx = to_far(k)
        pl.semaphore_signal(barrier, inc=1, device_id=(ty, core, z, tx), device_id_type=MESH)
    pl.semaphore_wait(barrier, 30)

    def near_copy(ab, k):
        tz, tc = to_near(k)
        first, rows = (72, 64) if ab else (0, 72)
        return pltpu.make_async_remote_copy(
            src_ref=src_ref.at[pl.ds(pl.multiple_of((tz * 2 + tc) * tall + first, 8), rows), :],
            dst_ref=near.at[k, pl.ds(first, rows), :],
            send_sem=near_send.at[ab, k],
            recv_sem=near_recv.at[ab, k],
            device_id=(y, tc, tz, x),
            device_id_type=MESH,
        )

    def far_copy(ab, g, k):
        ty, tx = to_far(k)
        h, rows = g // 2, pl.ds((g % 2) * 64, 64 + (8 if g % 2 and ab == 0 else 0))
        return pltpu.make_async_remote_copy(
            src_ref=box.at[ab, h, ty * 4 + tx, rows, :],
            dst_ref=held.at[ab, h, k, rows, :],
            send_sem=far_send.at[ab, g, k],
            recv_sem=far_recv.at[ab, g, k],
            device_id=(ty, core, z, tx),
            device_id_type=MESH,
        )

    window = 8
    queue = [(ab, k) for ab in range(2) for k in range(1, 16)]
    for item in queue[:window]:
        near_copy(*item).start()
    near[0] = src_ref[pl.ds(pl.multiple_of(kind * tall, 8), tall), :]

    zero_class = kind == 0
    special = jnp.where((kind == 0) & (group == 0), 1, 0)
    row = lax.broadcasted_iota(jnp.int32, (512, subs), 0)
    line = lax.broadcasted_iota(jnp.int32, (8, subs), 0)
    left = lax.broadcasted_iota(jnp.int32, (256, 128), 1) < 64
    for ab in range(2):
        side = jnp.where(zero_class, 0, ab)
        slots = row % 256 // 16 * 32 + (row // 256 + side) % 2 * 16 + row % 16
        first = 72 if ab else 0
        codes = jnp.zeros((8, subs), F32)
        for g in range(4):
            h = g // 2
            for i in range(4):
                k8 = (g % 2) * 4 + i
                k = h * 8 + k8
                if k:
                    near_copy(ab, k).wait()
                    after = queue.index((ab, k)) + window
                    if after < len(queue):
                        near_copy(*queue[after]).start()
                code = near[k, 64:65, :]
                fits = (code.astype(jnp.int32) // 256 == slots).astype(F32).astype(BF16)
                data = near[k, first:first + 64, :]
                turned = pltpu.roll(data, 64, 1)
                hi, lo = split(jnp.concatenate(
                    [jnp.where(left[:64], data, turned), jnp.where(left[:64], turned, data)], axis=0))
                o = dot(jnp.concatenate([fits, fits], axis=1), jnp.concatenate([hi, lo], axis=0))
                o = jnp.where(left, o[:256], o[256:])
                for p in range(PAIRS):
                    box[ab, h, p, k8 * 16:k8 * 16 + 16, :] = o[p * 16:(p + 1) * 16]
                codes = jnp.where(line == k8, code, codes)
            if g % 2 == 1 and ab == 0:
                for p in range(PAIRS):
                    box[0, h, p, 128:136, :] = codes
            for k in range(15):
                if ab:
                    far_copy(0, g, k).wait_send()
                far_copy(ab, g, (k + 4 * g) % 15).start()
            if g % 2 == 1:
                rows = slice(0, 136 if ab == 0 else 128)
                held[ab, h, 15, rows, :] = box[ab, h, group, rows, :]

    pos = lax.broadcasted_iota(jnp.int32, (256, 256), 0).astype(F32)

    def place(ab):
        side = jnp.where(zero_class, 0, ab)
        if ab == 0:
            grid_ref[0, :, 64:128] = jnp.zeros((256, 64), F32)
            grid_ref[8] = jnp.zeros((256, 128), F32)
            last = jnp.where(zero_class, 8, 7)
        else:
            last = 7
        for h in range(2):
            for g in (2 * h, 2 * h + 1):
                for k in range(15):
                    far_copy(ab, g, k).wait_recv()
            code = jnp.concatenate([held[0, h, k, 128:136, :] for k in range(16)], axis=0).T.astype(jnp.int32)
            at = code // 256 - group * 32
            value = (code % 256 + 1).astype(F32)

            def put(r):
                hot = [[], []]
                data = []
                for rank in range(2):
                    slot = r * 2 + rank
                    for n, which in enumerate((side, 1 - side)):
                        hot[n].append(jnp.sum(
                            jnp.where(at == slot + which * 16, value, 0.0), axis=0, keepdims=True) - 1.0)
                    data += [held[ab, h, k, pl.ds(slot, 8, stride=16), :] for k in range(16)]
                fits = jnp.concatenate(
                    [(jnp.concatenate(x, axis=1) == pos).astype(F32).astype(BF16) for x in hot], axis=0)
                hi, lo = split(jnp.concatenate(data, axis=0))
                v = dot(fits, jnp.concatenate([hi, lo], axis=1))
                v = v[:, :128] + v[:, 128:]
                rows = pl.ds(pl.multiple_of(r * 32, 32), 32)
                for bc in range(8):
                    own = v[bc * 32:(bc + 1) * 32, 0:64]
                    mirror = v[256 + bc * 32:256 + (bc + 1) * 32, 64:128]
                    if h == 1:
                        own = grid_ref[bc, rows, 0:64] + own
                        mirror = grid_ref[last - bc, rows, 64:128] + mirror
                    grid_ref[bc, rows, 0:64] = own
                    grid_ref[last - bc, rows, 64:128] = mirror

            loop(0, 8, put)

        def flip(i):
            x_ref[pl.ds(pl.multiple_of(i * 128, 128), 128), :] = grid_ref[i].T

        loop(0, 8, flip)

    tx, ty = (x + 1) % 4, (y + (x + 1) // 4) % 4
    edge = pltpu.make_async_remote_copy(
        src_ref=edge_src, dst_ref=edge_in, send_sem=edge_send, recv_sem=edge_recv,
        device_id=(ty, core, z, tx), device_id_type=MESH,
    )

    e2 = jnp.concatenate([eh[...], eh[...]], axis=1)
    low = lax.broadcasted_iota(jnp.int32, (32, 128), 1) < 64

    def near2_copy(ab, nt, t, dc):
        zh, tc = (z // 2 + t) % 4, (core + dc) % 2
        tz = zh * 2 + nt
        return (tz * 2 + tc) != kind, pltpu.make_async_remote_copy(
            src_ref=kbuf.at[pl.ds(pl.multiple_of(((ab * 2 + nt) * 8 + tc * 4 + zh) * 64, 64), 64), :],
            dst_ref=near2.at[ab, kind],
            send_sem=near2_send.at[ab, nt, t, dc],
            recv_sem=near2_recv.at[ab, kind],
            device_id=(y, tc, tz, x),
            device_id_type=MESH,
        )

    def transform(ab):
        for bc in range(8):
            own = x_ref[bc * 128:bc * 128 + 64, :]
            mirror = x_ref[bc * 128 + 64:bc * 128 + 128, :]
            if ab == 0 and bc == 0:
                mirror = jnp.where(zero_class, edge_in[...], mirror)
            for c2, v in enumerate((own, mirror)):
                hi, lo = split(v)
                row = bc * 64 + c2 * 32
                for ri in range(2):
                    lh[row:row + 32, ri * 256:(ri + 1) * 256] = hi[ri * 32:(ri + 1) * 32]
                    ll[row:row + 32, ri * 256:(ri + 1) * 256] = lo[ri * 32:(ri + 1) * 32]
        for nt in range(2):
            cols = slice(nt * 512, (nt + 1) * 512)

            def one(i):
                rows = pl.ds(pl.multiple_of(i * 256, 256), 256)
                v = dot3(lh[rows, :], ll[rows, :], wh[:, cols], wl[:, cols])
                for k in range(2):
                    parts = []
                    for b in range(2):
                        r = (k * 2 + b) * 64
                        ya, yb = v[r:r + 64, :256], v[r:r + 64, 256:]
                        which = 0
                        if ab == 0 and k == 0 and b == 0:
                            which = jnp.where(i == 0, special, 0)
                        tab = lambda n: t_ref[which * 8 + n * 2 + nt]
                        parts.append(jnp.concatenate(
                            [ya * tab(0) + yb * tab(1), ya * tab(2) + yb * tab(3)], axis=0))
                    th, tl = split(jnp.concatenate(parts, axis=1))
                    o = dot(e2, jnp.concatenate([th, tl], axis=0)) + dot(el[...], th)
                    for g in range(2):
                        o0 = o[:, g * 128:(g + 1) * 128]
                        o1 = o[:, 256 + g * 128:256 + (g + 1) * 128]
                        pair = (jnp.where(low, o0, pltpu.roll(o1, 64, 1)), jnp.where(low, pltpu.roll(o0, 64, 1), o1))
                        for e in range(2):
                            for ty in range(4):
                                first = (ab * 2 + nt) * 512 + ty * 16 + (g * 2 + e) * 4 + i * 2 + k
                                kbuf[pl.ds(first, 8, stride=64), :] = pair[e][ty * 8:(ty + 1) * 8]

            loop(0, 2, one)
            for t in (0, 1, 3, 2):
                for dc in range(2):
                    other, copy = near2_copy(ab, nt, t, dc)

                    @pl.when(other)
                    def _():
                        copy.start()

        mine = ab * 1024 + ((z % 2) * 8 + core * 4 + z // 2) * 64
        near2[ab, kind] = kbuf[pl.ds(pl.multiple_of(mine, 64), 64), :]

    place(0)
    edge_src[...] = grid_ref[8].T[64:]
    edge.start()
    for c in tables:
        c.wait()
    edge.wait_recv()
    transform(0)
    place(1)
    transform(1)

    def far2_copy(ab, t, k):
        ty, tx = to_far(k)
        return pltpu.make_async_remote_copy(
            src_ref=fwd.at[ab, t, ty * 4 + tx],
            dst_ref=out_ref.at[ab, (z // 2 - t + 4) % 4, group],
            send_sem=far2_send.at[ab, t, k],
            recv_sem=far2_recv.at[ab, t, k],
            device_id=(ty, core, z, tx),
            device_id_type=MESH,
        )

    for ab in range(2):
        for t in (0, 1, 3, 2):
            zh = (z // 2 - t + 4) % 4
            for i in range(4):
                sender = zh * 4 + i

                @pl.when(sender != kind)
                def _():
                    pltpu.make_async_remote_copy(
                        src_ref=kbuf.at[pl.ds(0, 64), :], dst_ref=near2.at[ab, sender],
                        send_sem=near2_send.at[0, 0, 0, 0], recv_sem=near2_recv.at[ab, sender],
                        device_id=(y, 1 - core, z, x), device_id_type=MESH,
                    ).wait_recv()

                for m in range(8):
                    v = near2[ab, sender, m * 8:(m + 1) * 8, :]
                    for e in range(2):
                        fwd[ab, t, m * 2 + e, i * 4:i * 4 + 4, :] = v[e * 4:(e + 1) * 4]
            for k in range(15):
                far2_copy(ab, t, k).start()
            out_ref[ab, zh, group] = fwd[ab, t, group]

    for ab in range(2):
        for t in range(4):
            for k in range(15):
                far2_copy(ab, t, k).wait_recv()
    edge.wait_send()
    for g in range(4):
        for k in range(15):
            far_copy(1, g, k).wait_send()
    for ab in range(2):
        for nt in range(2):
            for t in range(4):
                for dc in range(2):
                    other, copy = near2_copy(ab, nt, t, dc)

                    @pl.when(other)
                    def _():
                        copy.wait_send()
    for ab in range(2):
        for t in range(4):
            for k in range(15):
                far2_copy(ab, t, k).wait_send()


def exchange(payload):
    tall = payload.shape[0] // CLASSES
    w, t, e = down_tables()
    wh, wl = halves(w)
    eh, el = halves(e)
    vmem = pl.BlockSpec(memory_space=pltpu.VMEM)
    hbm = pl.BlockSpec(memory_space=pltpu.HBM)
    dma = pltpu.SemaphoreType.DMA
    return pl.pallas_call(
        exchange_kernel,
        in_specs=[vmem, hbm, hbm, hbm, vmem, vmem],
        out_specs=vmem,
        out_shape=jax.ShapeDtypeStruct((2, 4, 16, 16, 128), F32),
        scratch_shapes=[
            pltpu.VMEM((16, tall, 128), F32),
            pltpu.VMEM((2, 2, 16, 136, 128), F32),
            pltpu.VMEM((2, 2, 16, 136, 128), F32),
            pltpu.VMEM((9, 256, 128), F32),
            pltpu.VMEM((1024, 256), F32),
            pltpu.VMEM((64, 256), F32),
            pltpu.VMEM((64, 256), F32),
            pltpu.VMEM((512, 1024), BF16),
            pltpu.VMEM((512, 1024), BF16),
            pltpu.VMEM((16, 64, 256), F32),
            pltpu.VMEM((512, 512), BF16),
            pltpu.VMEM((512, 512), BF16),
            pltpu.VMEM((2048, 128), F32),
            pltpu.VMEM((2, 16, 64, 128), F32),
            pltpu.VMEM((2, 4, 16, 16, 128), F32),
            dma((2, 16)), dma((2, 16)), dma((2, 4, 16)), dma((2, 4, 16)), dma(()), dma(()), dma((3,)),
            dma((2, 2, 4, 2)), dma((2, 16)), dma((2, 4, 16)), dma((2, 4, 16)),
        ],
        compiler_params=pltpu.CompilerParams(
            collective_id=0, has_side_effects=True, vmem_limit_bytes=48 * MB
        ),
        name="exchange",
    )(payload, wh, wl, t, eh, el)


def across_kernel(k_ref, wh, wl, zh, zl, twist, out_ref, lh, ll, y_ref):
    for j in range(16):
        first = [(ab * 4 + j // 4) * 256 + j % 4 * 4 + bc2 for ab in range(2) for bc2 in range(4)]
        a = jnp.concatenate([k_ref[pl.ds(i, PAIRS, stride=16), :] for i in first], axis=0).T
        h, l = split(a)
        for i in range(4):
            lh[j * 32:(j + 1) * 32, i * 128:(i + 1) * 128] = h[i * 32:(i + 1) * 32]
            ll[j * 32:(j + 1) * 32, i * 128:(i + 1) * 128] = l[i * 32:(i + 1) * 32]
    edge = dot3(lh[0:32, :], ll[0:32, :], zh[...], zl[...])
    y_ref[0:32] = edge[:, :512]
    y_ref[512:544] = edge[:, 512:]
    y_ref[32:512] = dot3(lh[32:512, :], ll[32:512, :], wh[...], wl[...])

    cos = [math.cos(2 * math.pi * i / 32) for i in range(32)]
    sin = [math.sin(2 * math.pi * i / 32) for i in range(32)]

    def combine(terms):
        total = None
        for f, x in terms:
            if abs(f) < 1e-12:
                continue
            v = x if f == 1.0 else -x if f == -1.0 else x * f
            total = v if total is None else total + v
        return total

    def rows(i, _):
        at = pl.multiple_of(i * 8, 8)
        for half in range(2):
            lane = slice(half * 128, (half + 1) * 128)
            tre, tim = [], []
            for v in range(17):
                yre = y_ref[pl.ds(v * 32 + at, 8), lane]
                yim = y_ref[pl.ds(v * 32 + at, 8), 256 + half * 128:256 + (half + 1) * 128]
                c = twist[v:v + 1, lane]
                s = twist[v:v + 1, 256 + half * 128:256 + (half + 1) * 128]
                tre.append(yre * c - yim * s)
                tim.append(yre * s + yim * c)
            for m2 in range(9):
                e0 = combine([(cos[v * m2 % 32], tre[v]) for v in range(0, 17, 2)])
                e1 = combine([(cos[v * m2 % 32], tre[v]) for v in range(1, 17, 2)])
                o0 = combine([(sin[v * m2 % 32], tim[v]) for v in range(0, 17, 2)])
                o1 = combine([(sin[v * m2 % 32], tim[v]) for v in range(1, 17, 2)])
                zero = jnp.zeros((8, 128), F32)
                e0, e1, o0, o1 = [zero if x is None else x for x in (e0, e1, o0, o1)]
                puts = {m2: (e0 + e1) - (o0 + o1), (32 - m2) % 32: (e0 + e1) + (o0 + o1)}
                puts[16 - m2] = (e0 - e1) + (o0 - o1)
                puts[16 + m2] = (e0 - e1) - (o0 - o1)
                for m, v in puts.items():
                    out_ref[pl.ds(at, 8), m * 256 + half * 128:m * 256 + (half + 1) * 128] = v
        return 0

    lax.fori_loop(0, 4, rows, 0)


def across(k):
    w, zero, twist = across_tables()
    wh, wl = halves(w)
    zh, zl = halves(zero)
    return pl.pallas_call(
        across_kernel,
        out_shape=jax.ShapeDtypeStruct((32, G), F32),
        scratch_shapes=[
            pltpu.VMEM((512, 512), BF16), pltpu.VMEM((512, 512), BF16), pltpu.VMEM((544, 512), F32),
        ],
        compiler_params=pltpu.CompilerParams(vmem_limit_bytes=32 * MB),
        name="across",
    )(k, wh, wl, zh, zl, twist)


def body(uv, vis, left, right, block_subgrid, subgrid_tile, block_row, block_col):
    visible = uv.shape[2]

    l, r = left.astype(F32), right.astype(F32)
    beam = jnp.stack([
        l[:, 0] * r[:, 0] + l[:, 1] * r[:, 1],
        l[:, 1] * r[:, 0] - l[:, 0] * r[:, 1],
    ])
    payload = make_payload(
        uv, vis, beam, block_subgrid, subgrid_tile, block_row[None], block_col[None], subgrid_tables(visible)
    )
    return across(exchange(payload).reshape(2048, 128))


def solution(mesh):
    names = ("y", "core", "z", "x")
    axes = Mesh(mesh.devices.reshape(4, 2, 8, 4), names)
    placed = (
        P(names, None, None),
        P(names, None, None),
        P(names, None, None),
        P(names, None, None),
        P(names, None),
        P(names, None),
        P(names),
        P(names),
    )
    return jax.shard_map(body, mesh=axes, in_specs=placed, out_specs=P(names, None), check_vma=False)
```
